32 devices in a mesh: seq: 8 (over y, x, core), chan: 4 (over z).
Axes of the slice: x: 2, y: 2, z: 4, core: 2. Of those that a mesh axis runs over, the one named last changes fastest.
Arguments:
- inner_input: bfloat16 [8192, 8192], P('seq', 'chan'), may hold values from -6 to 6
- state_maps: bfloat16 [8192, 2, 8, 128], P('seq', None, 'chan'), may hold values from -6 to 6
- gate_input: bfloat16 [8192, 8192], P('seq', 'chan'), may hold values from -6 to 6
- step_input: float32 [8192, 128], P('seq', 'chan'), may hold values from -3 to 12
- log_decay_rate: float32 [128], P('chan'), may hold values from 0 to 2.78
- step_bias: float32 [128], P('chan'), may hold values from -17 to 0
- skip_gain: float32 [128], P('chan'), may hold values from 0.5 to 1.5
- conv_kernel: float32 [4, 8192], P(None, 'chan'), may hold values from -3 to 3
- map_kernel: float32 [4, 2, 8, 128], P(None, None, 'chan'), may hold values from -3 to 3
- norm_gain: float32 [8192], P('chan'), may hold values from 0.1 to 1.9
- out_weight: bfloat16 [8192, 2048], P('chan'), may hold values from -0.09375 to 0.09375
Outputs:
- mixed_out: bfloat16 [8192, 2048], P('seq', 'chan')
The draws below stay inside these ranges and needn't reach their ends.
All inputs are finite; a program needn't handle non-finite values.
Results may differ from the reference program's by a relative error of at most 0.011.
Values may be sent and summed in bfloat16 or wider, within the bound.
No kernel may reach another device: no remote copies, remote signals or barrier semaphores. Data moves between devices by JAX's collectives and lax.ppermute only.
A program may use at most 128 MiB of HBM per device.

```python
import math
import jax
import jax.numpy as jnp
from jax import lax

HEADS = 128
HEAD_DIM = 64
STATE = 128
NGROUPS = 8
KCONV = 4
BLOCK = 256
DOUT = 2048
TOK_DEV = 1024
INNER = 8192
TOKEN_COUNT = 8192


def head_law(key):
    head_key = jax.random.fold_in(key, 11)
    first_key, second_key, tertiary_key = jax.random.split(head_key, 3)
    fast_share = 8
    fast_heads = jax.random.randint(first_key, (HEADS,), 0, 16) < fast_share
    log_decay_rate = jax.random.uniform(second_key, (HEADS,), jnp.float32, 0.0, math.log(16.0))
    spread = jnp.exp(jax.random.uniform(tertiary_key, (HEADS,), jnp.float32, -0.5, 0.5))
    fast_rate = 1.0 / min(40, TOK_DEV // 4)
    slow_rate = 0.7 / TOKEN_COUNT
    target = jnp.where(fast_heads, fast_rate, slow_rate) * spread / jnp.exp(log_decay_rate)
    return (log_decay_rate, jnp.log(jnp.expm1(target)))


def draw_log_decay_rate(key, part):
    return head_law(key)[0]


def draw_step_bias(key, part):
    return head_law(key)[1]


def draw_step_input(key, part):
    step_key = jax.random.fold_in(key, 23)
    first_key, second_key, tertiary_key = jax.random.split(step_key, 3)
    jitter = 0.5 * jnp.clip(jax.random.normal(first_key, (TOKEN_COUNT, HEADS), jnp.float32), -4.0, 4.0)
    slab_shift = jax.random.uniform(second_key, (TOKEN_COUNT // TOK_DEV, 1, HEADS), jnp.float32, -0.4, 0.4)
    baseline = (jitter.reshape(TOKEN_COUNT // TOK_DEV, TOK_DEV, HEADS) + slab_shift).reshape(TOKEN_COUNT, HEADS)
    surge_rows = jax.random.randint(tertiary_key, (3,), 0, TOKEN_COUNT)
    surge_mask = jnp.any(jnp.arange(TOKEN_COUNT)[:, None] == surge_rows[None, :], axis=1)
    boost_factor = jnp.where(surge_mask, math.log(0.43 * TOKEN_COUNT), 0.0).astype(jnp.float32)
    return baseline + boost_factor[:, None]


def raised(result, key, source, target, blocks, factor):
    owner, partner = [(jnp.arange(result.shape[dim]) // (result.shape[dim] // blocks)).reshape([-1 if axis == dim else 1 for axis in range(result.ndim)]) for dim in (source, target)]
    chosen = jax.random.permutation(key, blocks)[partner]
    strong = (owner == chosen) | (owner == (partner + blocks // 2) % blocks)
    return jnp.where(strong, factor * result, result)


def level_of(own_key, dims, shards, low, high):
    def one(axis_at, shards_of):
        draws = jax.random.uniform(jax.random.fold_in(jax.random.fold_in(own_key, 6), axis_at), (shards_of,), jnp.float32, low / len(shards), high / len(shards))
        return jnp.repeat(jnp.exp(draws), dims[axis_at] // shards_of).reshape((-1,) + (1,) * (len(dims) - axis_at - 1))

    loudness = one(*shards[0])
    for cut in shards[1:]:
        loudness = loudness * one(*cut)
    return loudness


def scatter_about(own_key, shape, deviation, most, cuts=(), dtype=jnp.bfloat16):
    entries = deviation * jax.random.normal(own_key, shape, jnp.float32)
    if cuts:
        entries = entries * level_of(own_key, shape, cuts, -0.22, 0.18)
    return jnp.clip(entries, -most, most).astype(dtype)


def bell_draw_with(own_key, dims, deviation, bound, cuts, heavy, held_as=jnp.bfloat16):
    result = deviation * jax.random.normal(own_key, dims, jnp.float32)
    if cuts:
        result = result * level_of(own_key, dims, cuts, -0.22, 0.18)
    return jnp.clip(raised(result, jax.random.fold_in(own_key, 3), *heavy), -bound, bound).astype(held_as)


def setup_inputs(seed: int = 0) -> dict:
    arg_keys = jax.random.split(jax.random.key(seed), 12)
    return {
        "inner_input": scatter_about(arg_keys[0], (TOKEN_COUNT, INNER), 1.0, 6.0, ((0, 8), (1, 4))),
        "state_maps": scatter_about(arg_keys[1], (TOKEN_COUNT, 2, NGROUPS, STATE), 1.0, 6.0, ((0, 8), (2, 4))),
        "gate_input": scatter_about(arg_keys[2], (TOKEN_COUNT, INNER), 1.0, 6.0, ((0, 8), (1, 4))),
        "step_input": draw_step_input(jax.random.fold_in(arg_keys[11], 71), 0),
        "log_decay_rate": draw_log_decay_rate(jax.random.fold_in(arg_keys[11], 71), 0),
        "step_bias": draw_step_bias(jax.random.fold_in(arg_keys[11], 71), 0),
        "skip_gain": jnp.clip(0.5 + 1.0 * jax.random.uniform(arg_keys[6], (HEADS,), jnp.float32) ** level_of(arg_keys[6], (HEADS,), ((0, 4),), -0.2, 0.2), 0.5, 1.5),
        "conv_kernel": scatter_about(arg_keys[7], (KCONV, INNER), 0.5, 3.0, ((1, 4),), jnp.float32),
        "map_kernel": scatter_about(arg_keys[8], (KCONV, 2, NGROUPS, STATE), 0.5, 3.0, ((2, 4),), jnp.float32),
        "norm_gain": jnp.clip(1.0 + 0.18 * jax.random.normal(arg_keys[9], (INNER,), jnp.float32), 0.1, 1.9),
        "out_weight": bell_draw_with(arg_keys[10], (INNER, DOUT), INNER ** -0.5, 0.09375, ((0, 4),), (0, 1, 4, 2.0)),
    }


step_limit = 0.5
epsilon = 1e-05

def conv_silu(padded, kernel, length):
    acc = jnp.zeros((length,) + padded.shape[1:], jnp.float32)
    for offset in range(kernel.shape[0]):
        acc = acc + kernel[offset] * padded[offset:offset + length].astype(jnp.float32)
    return jax.nn.silu(acc).astype(jnp.bfloat16)

def reference(inner_input, state_maps, gate_input, step_input, log_decay_rate, step_bias, skip_gain, conv_kernel, map_kernel, norm_gain, out_weight):
    per_group = HEADS // NGROUPS
    block_count = TOKEN_COUNT // BLOCK
    kernel_remainder = KCONV - 1
    rate = -jnp.exp(log_decay_rate)
    row_ids = lax.broadcasted_iota(jnp.int32, (BLOCK, BLOCK), 0)
    col_ids = lax.broadcasted_iota(jnp.int32, (BLOCK, BLOCK), 1)
    causal = row_ids >= col_ids

    def advance(carry, inputs):
        state, tail_inner, tail_maps = carry
        inner_rows, map_rows, gate_rows, step_rows = inputs
        inner_conv = conv_silu(jnp.concatenate([tail_inner, inner_rows], 0), conv_kernel, BLOCK)
        maps_conv = conv_silu(jnp.concatenate([tail_maps, map_rows], 0), map_kernel, BLOCK)
        step = jnp.minimum(jax.nn.softplus(step_rows + step_bias), step_limit)
        log_step = step * rate
        cumul = jnp.cumsum(log_step, axis=0).reshape(BLOCK, NGROUPS, per_group)
        step_group = step.reshape(BLOCK, NGROUPS, per_group)
        x_heads = inner_conv.reshape(BLOCK, NGROUPS, per_group, HEAD_DIM).astype(jnp.float32)
        b_rows = maps_conv[:, 0].astype(jnp.float32)
        c_rows = maps_conv[:, 1].astype(jnp.float32)
        scores = jnp.einsum('tgn,sgn->gts', c_rows, b_rows)
        cumul_t = cumul.transpose(1, 2, 0)
        gap = cumul_t[..., :, None] - cumul_t[..., None, :]
        decay = jnp.exp(jnp.where(causal, gap, -jnp.inf))
        mixing = (scores[:, None] * decay * step_group.transpose(1, 2, 0)[..., None, :]).astype(jnp.bfloat16)
        mixing = lax.optimization_barrier(mixing).astype(jnp.float32)
        y_local = jnp.einsum('gjts,sgjp->tgjp', mixing, x_heads)
        state_in = lax.optimization_barrier(state.astype(jnp.bfloat16)).astype(jnp.float32)
        y_carry = jnp.exp(cumul)[..., None] * jnp.einsum('tgn,gjpn->tgjp', c_rows, state_in)
        weighted = ((jnp.exp(cumul[-1:] - cumul) * step_group)[..., None] * b_rows[:, :, None, :]).astype(jnp.bfloat16)
        weighted = lax.optimization_barrier(weighted).astype(jnp.float32)
        updated_state = jnp.exp(cumul[-1])[..., None, None] * state + jnp.einsum('sgjp,sgjn->gjpn', x_heads, weighted)
        y_all = y_local + y_carry + skip_gain.reshape(NGROUPS, per_group)[:, :, None] * x_heads
        gated = y_all.reshape(BLOCK, NGROUPS, per_group * HEAD_DIM) * jax.nn.silu(gate_rows.reshape(BLOCK, NGROUPS, per_group * HEAD_DIM).astype(jnp.float32))
        square_mean = lax.optimization_barrier(jnp.mean(gated * gated, axis=-1, keepdims=True))
        normed = (gated * lax.rsqrt(square_mean + epsilon) * norm_gain.reshape(NGROUPS, -1)).astype(jnp.bfloat16).reshape(BLOCK, INNER)
        out_rows = jnp.dot(normed, out_weight, preferred_element_type=jnp.float32).astype(jnp.bfloat16)
        return ((updated_state, inner_rows[BLOCK - kernel_remainder:], map_rows[BLOCK - kernel_remainder:]), out_rows)
    start_state = jnp.zeros((NGROUPS, per_group, HEAD_DIM, STATE), jnp.float32)
    start_inner = jnp.zeros((kernel_remainder, INNER), jnp.bfloat16)
    start_maps = jnp.zeros((kernel_remainder, 2, NGROUPS, STATE), jnp.bfloat16)
    inputs = (inner_input.reshape(block_count, BLOCK, INNER), state_maps.reshape(block_count, BLOCK, 2, NGROUPS, STATE), gate_input.reshape(block_count, BLOCK, INNER), step_input.reshape(block_count, BLOCK, HEADS))
    final_carry, outputs = lax.scan(advance, (start_state, start_inner, start_maps), inputs)
    return outputs.reshape(TOKEN_COUNT, DOUT)
```

```python
import functools

import jax
import jax.numpy as jnp
from jax import lax
from jax.experimental import pallas as pl
from jax.experimental.pallas import tpu as pltpu
from jax.sharding import PartitionSpec as P

HEAD_DIM = 64
STATE = 128
BLK = 128
LANES = 128
HALO = 8
CHUNKS = 4

step_limit = 0.5
epsilon = 1e-05
LOG2E = 1.4426950408889634
F32 = jnp.float32
BF16 = jnp.bfloat16
VMEM_LIMIT = 56 * 1024 * 1024


def silu(v):
    half = 0.5 * v
    return half + half * jnp.tanh(half)


def high_low(v):
    high = v.astype(BF16).astype(F32)
    return high, v - high


def spread(first_row, heads, width):
    row = lax.broadcasted_iota(jnp.int32, (LANES, width), 0) - first_row
    col = lax.broadcasted_iota(jnp.int32, (LANES, width), 1)
    low = jnp.logical_and(col >= row * HEAD_DIM, col < (row + 1) * HEAD_DIM)
    again = row - heads
    high = jnp.logical_and(col >= again * HEAD_DIM, col < (again + 1) * HEAD_DIM)
    return jnp.where(jnp.logical_or(low, high), 1.0, 0.0).astype(BF16)


def dot(a, b):
    return jnp.dot(a, b, preferred_element_type=F32)


def dot_t(a, b):
    return lax.dot_general(a, b, (((1,), (1,)), ((), ())), preferred_element_type=F32)


def padded(rows):
    return jnp.concatenate([rows, jnp.zeros((LANES - rows.shape[0], rows.shape[1]), rows.dtype)], 0)


def states_kernel(
    x_ref, maps_ref, step_ref, tail_ref, par_ref, ck_ref, mk_ref,
    xc_ref, bc_ref, crow_ref, ec_ref, cols_ref, sloc_ref, pay_ref,
    lead, state, prev_x, prev_m, e_w, pick, tri,
):
    b = pl.program_id(0)
    heads = step_ref.shape[0]
    width = x_ref.shape[1]
    parts = mk_ref.shape[0] // 4
    groups = parts // 2
    gw = width // groups

    @pl.when(b == 0)
    def _():
        lead[...] = jnp.zeros_like(lead)
        state[...] = jnp.zeros_like(state)
        prev_x[...] = tail_ref[:, :width].astype(F32)
        for q in range(parts):
            prev_m[q] = tail_ref[:, width + q * STATE : width + (q + 1) * STATE].astype(F32)
        e_w[...] = spread(0, heads, width)
        row = lax.broadcasted_iota(jnp.int32, pick.shape, 0)
        col = lax.broadcasted_iota(jnp.int32, pick.shape, 1)
        source = (row & (BLK - 1)) * parts + row // BLK
        pick[...] = jnp.where(col == source, 1.0, 0.0).astype(BF16)
        row = lax.broadcasted_iota(jnp.int32, tri.shape, 0)
        col = lax.broadcasted_iota(jnp.int32, tri.shape, 1)
        tri[...] = jnp.where(row <= col, 1.0, 0.0).astype(BF16)

    bias, rate, = par_ref[:, 0:1], -jnp.exp(par_ref[:, 1:2])
    v = step_ref[...] + bias
    step = jnp.minimum(jnp.maximum(v, 0.0) + jnp.log1p(jnp.exp(-jnp.abs(v))), step_limit)
    log_step = rate * step
    first, rest = high_low(log_step)
    second, third = high_low(rest)
    sums = dot(jnp.concatenate([first, second, third], 0).astype(BF16), tri[...])
    cum = sums[:heads] + sums[heads : 2 * heads] + sums[2 * heads :]
    total = cum[:, BLK - 1 : BLK]
    weight = jnp.exp(total - cum) * step
    leading = lead[:, 0:1]
    lead[...] = jnp.broadcast_to(leading + total, lead.shape)
    grown = jnp.exp(cum)
    entered = jnp.exp(cum + leading)
    crow_ref[...] = (cum - jnp.log(step)) * LOG2E
    one = padded(jnp.concatenate(high_low(weight), 0)).T
    two = padded(jnp.concatenate(high_low(grown), 0)).T
    three = padded(jnp.concatenate((cum * LOG2E,) + high_low(entered), 0)).T
    ec_ref[...] = two.astype(BF16)
    cols_ref[...] = three
    expanded = dot(
        jnp.concatenate([one, two[BLK - HALO :]], 0).astype(BF16), e_w[...]
    )

    sorted_maps = dot(pick[...], maps_ref[...])
    b_t = []
    for q in range(parts):
        cur = sorted_maps[q * BLK : (q + 1) * BLK]
        full = jnp.concatenate([prev_m[q], cur], 0)
        acc = cur * mk_ref[3 * parts + q : 3 * parts + q + 1]
        for back in range(1, 4):
            k = (3 - back) * parts + q
            acc = acc + pltpu.roll(full, back, 0)[HALO:] * mk_ref[k : k + 1]
        prev_m[q] = cur[BLK - HALO :]
        conv = silu(acc)
        bc_ref[:, q * STATE : (q + 1) * STATE] = conv.astype(BF16)
        if q < groups:
            b_t.append(conv.astype(BF16).astype(F32).T.astype(BF16))

    cw = 256
    for c in range(0, width, cw):
        at = slice(c, c + cw)
        cur = x_ref[:, at].astype(F32)
        full = jnp.concatenate([prev_x[:, at], cur], 0)
        acc = cur * ck_ref[3:4, at]
        for back in range(1, 4):
            acc = acc + pltpu.roll(full, back, 0)[HALO:] * ck_ref[3 - back : 4 - back, at]
        prev_x[:, at] = cur[BLK - HALO :]
        conv = silu(acc).astype(BF16)
        xc_ref[:, at] = conv
        weighted = (conv.astype(F32) * expanded[:BLK, at]).astype(BF16)
        before = state[:, at]
        sloc_ref[0, :, at] = before.astype(BF16)
        after = expanded[BLK + HALO - 1 : BLK + HALO, at] * before + dot(b_t[c // gw], weighted)
        state[:, at] = after
        pay_ref[:, at] = after.astype(BF16)
    pay_ref[:, width:] = jnp.broadcast_to(three[BLK - 1 :], (STATE, LANES)).astype(BF16)


def local_kernel(xc_ref, bc_ref, crow_ref, ec_ref, cols_ref, sloc_ref, gain_ref, y_ref, e_c):
    heads = crow_ref.shape[0]
    width = xc_ref.shape[1]
    groups = bc_ref.shape[1] // (2 * STATE)
    gw = width // groups

    @pl.when(pl.program_id(0) == 0)
    def _():
        e_c[...] = spread(0, heads, width)

    lane = lax.broadcasted_iota(jnp.int32, (BLK, LANES), 1)
    row = lax.broadcasted_iota(jnp.int32, (BLK, BLK), 0)
    left = lane < HEAD_DIM
    causal = row >= lax.broadcasted_iota(jnp.int32, (BLK, BLK), 1)
    for g in range(groups):
        b_g = bc_ref[:, g * STATE : (g + 1) * STATE]
        c_g = bc_ref[:, (groups + g) * STATE : (groups + g + 1) * STATE]
        scores = jnp.where(causal, dot_t(c_g, b_g), 0.0)
        for c in range(g * gw, (g + 1) * gw, LANES):
            at = slice(c, c + LANES)
            mixing = []
            for h in (c // HEAD_DIM, c // HEAD_DIM + 1):
                gap = jnp.minimum(cols_ref[:, h : h + 1] - crow_ref[h : h + 1], 0.0)
                mixing.append((jnp.exp2(gap) * scores).astype(BF16))
            x = xc_ref[:, at]
            nil = jnp.zeros_like(x)
            stacked = jnp.concatenate([jnp.where(left, x, nil), jnp.where(left, nil, x)], 0)
            y = dot(jnp.concatenate(mixing, 1), stacked)
            carry = dot(c_g, sloc_ref[0, :, at])
            y = y + dot(ec_ref[...], e_c[:, at]) * carry + gain_ref[:, at] * x.astype(F32)
            y_ref[:, at] = y.astype(BF16)


def prefix_kernel(pay_ref, out_ref, *, heads):
    width = out_ref.shape[2]
    decays = dot(pay_ref[:, 0, width:], spread(heads, heads, width))
    running = jnp.zeros(out_ref.shape[1:], F32)
    for slab in range(out_ref.shape[0]):
        out_ref[slab] = running.astype(BF16)
        running = decays[slab : slab + 1] * running + pay_ref[slab, :, :width].astype(F32)


def project_kernel(y_ref, bc_ref, cols_ref, enter_ref, gate_ref, gain_ref, w_ref, out_ref, e_c, *, heads):
    width = y_ref.shape[1]
    groups = bc_ref.shape[1] // (2 * STATE)
    gw = width // groups
    count, _, part = out_ref.shape

    @pl.when(pl.program_id(0) == 0)
    def _():
        e_c[...] = spread(heads, heads, width)

    grown = cols_ref[...].astype(BF16)
    normed = []
    for g in range(groups):
        at = slice(g * gw, (g + 1) * gw)
        c_g = bc_ref[:, (groups + g) * STATE : (groups + g + 1) * STATE]
        carry = dot(c_g, enter_ref[:, at])
        y = y_ref[:, at].astype(F32) + dot(grown, e_c[:, at]) * carry
        gated = y * silu(gate_ref[:, at].astype(F32))
        square_mean = jnp.mean(gated * gated, axis=-1, keepdims=True)
        normed.append((gated * lax.rsqrt(square_mean + epsilon) * gain_ref[:, at]).astype(BF16))
    normed = jnp.concatenate(normed, 1)
    for k in range(count):
        out_ref[k] = dot(normed, w_ref[:, k * part : (k + 1) * part]).astype(BF16)


def params():
    return pltpu.CompilerParams(
        dimension_semantics=("arbitrary",), vmem_limit_bytes=VMEM_LIMIT
    )


def whole(shape):
    return pl.BlockSpec(shape, lambda b: (0,) * len(shape))


def rows(count, width, start=0):
    return pl.BlockSpec((count, width), lambda b: (start + b, 0))


def local(
    inner_input, state_maps, gate_input, step_input, log_decay_rate, step_bias,
    skip_gain, conv_kernel, map_kernel, norm_gain, out_weight,
):
    tokens, width = inner_input.shape
    groups = state_maps.shape[2]
    parts = 2 * groups
    heads = step_input.shape[1]
    blocks = tokens // BLK
    slabs = lax.axis_size("seq")
    chans = lax.axis_size("chan")
    features = out_weight.shape[1]
    map_width = parts * STATE

    tail = jnp.concatenate(
        [inner_input[tokens - HALO :], state_maps[tokens - HALO :].reshape(HALO, map_width)], 1
    )
    tail = lax.ppermute(tail, "seq", [(i, i + 1) for i in range(slabs - 1)])
    per_head = jnp.stack([step_bias, log_decay_rate], 1)
    xc, bc, crow, ec, cols, sloc, pay = pl.pallas_call(
        states_kernel,
        grid=(blocks,),
        in_specs=[
            rows(BLK, width),
            rows(BLK * parts, STATE),
            pl.BlockSpec((heads, BLK), lambda b: (0, b)),
            whole((HALO, width + map_width)),
            whole((heads, 2)),
            whole((4, width)),
            whole((4 * parts, STATE)),
        ],
        out_specs=[
            rows(BLK, width),
            rows(BLK, map_width),
            pl.BlockSpec((heads, BLK), lambda b: (0, b)),
            rows(BLK, LANES),
            rows(BLK, LANES),
            pl.BlockSpec((1, STATE, width), lambda b: (b, 0, 0)),
            whole((STATE, width + LANES)),
        ],
        out_shape=[
            jax.ShapeDtypeStruct((tokens, width), BF16),
            jax.ShapeDtypeStruct((tokens, map_width), BF16),
            jax.ShapeDtypeStruct((heads, tokens), F32),
            jax.ShapeDtypeStruct((tokens, LANES), BF16),
            jax.ShapeDtypeStruct((tokens, LANES), F32),
            jax.ShapeDtypeStruct((blocks, STATE, width), BF16),
            jax.ShapeDtypeStruct((STATE, width + LANES), BF16),
        ],
        scratch_shapes=[
            pltpu.VMEM((heads, LANES), F32),
            pltpu.VMEM((STATE, width), F32),
            pltpu.VMEM((HALO, width), F32),
            pltpu.VMEM((parts, HALO, STATE), F32),
            pltpu.VMEM((LANES, width), BF16),
            pltpu.VMEM((BLK * parts, BLK * parts), BF16),
            pltpu.VMEM((BLK, BLK), BF16),
        ],
        compiler_params=params(),
        name="states",
    )(
        inner_input, state_maps.reshape(tokens * parts, STATE), step_input.T, tail, per_head,
        conv_kernel, map_kernel.reshape(4 * parts, STATE),
    )

    part = STATE // slabs
    arrived = lax.all_to_all(
        pay.reshape(slabs, part, width + LANES), "seq", split_axis=0, concat_axis=0, tiled=True
    )

    gain = jnp.repeat(skip_gain, HEAD_DIM).reshape(1, width)

    def local_part(start, count):
        return pl.pallas_call(
            local_kernel,
            grid=(count,),
            in_specs=[
                rows(BLK, width, start),
                rows(BLK, map_width, start),
                pl.BlockSpec((heads, BLK), lambda b: (0, b + start)),
                rows(BLK, LANES, start),
                rows(BLK, LANES, start),
                pl.BlockSpec((1, STATE, width), lambda b: (b + start, 0, 0)),
                whole((1, width)),
            ],
            out_specs=rows(BLK, width),
            out_shape=jax.ShapeDtypeStruct((count * BLK, width), BF16),
            scratch_shapes=[pltpu.VMEM((LANES, width), BF16)],
            compiler_params=params(),
            name="local_part",
        )(xc, bc, crow, ec, cols, sloc, gain)

    half = blocks // 2
    y_halves = [local_part(0, half), local_part(half, blocks - half)]

    entering = pl.pallas_call(
        functools.partial(prefix_kernel, heads=heads),
        out_shape=jax.ShapeDtypeStruct((slabs, part, width), BF16),
        compiler_params=pltpu.CompilerParams(vmem_limit_bytes=VMEM_LIMIT),
        name="prefix",
    )(arrived)
    entering = lax.all_to_all(entering, "seq", split_axis=0, concat_axis=0, tiled=True)
    entering = entering.reshape(STATE, width)

    pieces = []
    per_chunk = blocks // CHUNKS
    norm_row = norm_gain.reshape(1, width)
    for chunk in range(CHUNKS):
        start = chunk * per_chunk
        y_half, y_start = (y_halves[0], start) if start < half else (y_halves[1], start - half)
        shares = pl.pallas_call(
            functools.partial(project_kernel, heads=heads),
            grid=(per_chunk,),
            in_specs=[
                rows(BLK, width, y_start),
                rows(BLK, map_width, start),
                rows(BLK, LANES, start),
                whole((STATE, width)),
                rows(BLK, width, start),
                whole((1, width)),
                whole((width, features)),
            ],
            out_specs=pl.BlockSpec((chans, BLK, features // chans), lambda b: (0, b, 0)),
            out_shape=jax.ShapeDtypeStruct((chans, per_chunk * BLK, features // chans), BF16),
            scratch_shapes=[pltpu.VMEM((LANES, width), BF16)],
            compiler_params=params(),
            name="project",
        )(y_half, bc, cols, entering, gate_input, norm_row, out_weight)
        piece = lax.psum_scatter(shares, "chan", scatter_dimension=0, tiled=True)
        pieces.append(piece.reshape(per_chunk * BLK, features // chans))
    return jnp.concatenate(pieces, 0)


def solution(mesh):
    return jax.shard_map(
        local,
        mesh=mesh,
        in_specs=(
            P("seq", "chan"),
            P("seq", None, "chan", None),
            P("seq", "chan"),
            P("seq", "chan"),
            P("chan"),
            P("chan"),
            P("chan"),
            P(None, "chan"),
            P(None, None, "chan", None),
            P("chan"),
            P("chan", None),
        ),
        out_specs=P("seq", "chan"),
        check_vma=False,
    )
```

```python
import functools

import jax
import jax.numpy as jnp
from jax import lax
from jax.experimental import pallas as pl
from jax.experimental.pallas import tpu as pltpu
from jax.sharding import PartitionSpec as P

HEAD_DIM = 64
STATE = 128
BLK = 128
LANES = 128
HALO = 8
CHUNKS = 2

step_limit = 0.5
epsilon = 1e-05
LOG2E = 1.4426950408889634
F32 = jnp.float32
BF16 = jnp.bfloat16
VMEM_LIMIT = 56 * 1024 * 1024


def silu(v):
    half = 0.5 * v
    return half + half * jnp.tanh(half)


def high_low(v):
    high = v.astype(BF16).astype(F32)
    return high, v - high


def spread(first_row, heads, width):
    row = lax.broadcasted_iota(jnp.int32, (LANES, width), 0) - first_row
    col = lax.broadcasted_iota(jnp.int32, (LANES, width), 1)
    low = jnp.logical_and(col >= row * HEAD_DIM, col < (row + 1) * HEAD_DIM)
    again = row - heads
    high = jnp.logical_and(col >= again * HEAD_DIM, col < (again + 1) * HEAD_DIM)
    return jnp.where(jnp.logical_or(low, high), 1.0, 0.0).astype(BF16)


def dot(a, b):
    return jnp.dot(a, b, preferred_element_type=F32)


def dot_t(a, b):
    return lax.dot_general(a, b, (((1,), (1,)), ((), ())), preferred_element_type=F32)


def column(row):
    count = row.shape[1]
    eye = lax.broadcasted_iota(jnp.int32, (count, count), 0) == lax.broadcasted_iota(
        jnp.int32, (count, count), 1
    )
    return jnp.sum(jnp.where(eye, row, 0.0), axis=1, keepdims=True)


def padded(rows):
    return jnp.concatenate([rows, jnp.zeros((LANES - rows.shape[0], rows.shape[1]), rows.dtype)], 0)


def states_kernel(
    x_ref, maps_ref, step_ref, tail_ref, bias_ref, rate_ref, ck_ref, mk_ref,
    xc_ref, bc_ref, crow_ref, ec_ref, cols_ref, sloc_ref, pay_ref,
    lead, state, prev_x, prev_m, e_w, pick, tri,
):
    b = pl.program_id(0)
    heads = step_ref.shape[0]
    width = x_ref.shape[1]
    parts = mk_ref.shape[0] // 4
    groups = parts // 2
    gw = width // groups

    @pl.when(b == 0)
    def _():
        lead[...] = jnp.zeros_like(lead)
        state[...] = jnp.zeros_like(state)
        prev_x[...] = tail_ref[:, :width].astype(F32)
        for q in range(parts):
            prev_m[q] = tail_ref[:, width + q * STATE : width + (q + 1) * STATE].astype(F32)
        e_w[...] = spread(0, heads, width)
        row = lax.broadcasted_iota(jnp.int32, pick.shape, 0)
        col = lax.broadcasted_iota(jnp.int32, pick.shape, 1)
        source = (row & (BLK - 1)) * parts + row // BLK
        pick[...] = jnp.where(col == source, 1.0, 0.0).astype(BF16)
        row = lax.broadcasted_iota(jnp.int32, tri.shape, 0)
        col = lax.broadcasted_iota(jnp.int32, tri.shape, 1)
        tri[...] = jnp.where(row <= col, 1.0, 0.0).astype(BF16)

    bias, rate = column(bias_ref[...]), -jnp.exp(column(rate_ref[...]))
    v = step_ref[...] + bias
    step = jnp.minimum(jnp.maximum(v, 0.0) + jnp.log1p(jnp.exp(-jnp.abs(v))), step_limit)
    log_step = rate * step
    first, rest = high_low(log_step)
    second, third = high_low(rest)
    sums = dot(jnp.concatenate([first, second, third], 0).astype(BF16), tri[...])
    cum = sums[:heads] + sums[heads : 2 * heads] + sums[2 * heads :]
    total = cum[:, BLK - 1 : BLK]
    weight = jnp.exp(total - cum) * step
    leading = lead[:, 0:1]
    lead[...] = jnp.broadcast_to(leading + total, lead.shape)
    grown = jnp.exp(cum)
    entered = jnp.exp(cum + leading)
    crow_ref[...] = (cum - jnp.log(step)) * LOG2E
    one = padded(jnp.concatenate(high_low(weight), 0)).T
    two = padded(jnp.concatenate(high_low(grown), 0)).T
    three = padded(jnp.concatenate((cum * LOG2E,) + high_low(entered), 0)).T
    ec_ref[...] = two.astype(BF16)
    cols_ref[...] = three
    expanded = dot(
        jnp.concatenate([one, two[BLK - HALO :]], 0).astype(BF16), e_w[...]
    )

    sorted_maps = dot(pick[...], maps_ref[...])
    b_t = []
    for q in range(parts):
        cur = sorted_maps[q * BLK : (q + 1) * BLK]
        full = jnp.concatenate([prev_m[q], cur], 0)
        acc = cur * mk_ref[3 * parts + q : 3 * parts + q + 1]
        for back in range(1, 4):
            k = (3 - back) * parts + q
            acc = acc + pltpu.roll(full, back, 0)[HALO:] * mk_ref[k : k + 1]
        prev_m[q] = cur[BLK - HALO :]
        conv = silu(acc)
        bc_ref[:, q * STATE : (q + 1) * STATE] = conv.astype(BF16)
        if q < groups:
            b_t.append(conv.astype(BF16).astype(F32).T.astype(BF16))

    cw = 256
    for c in range(0, width, cw):
        at = slice(c, c + cw)
        cur = x_ref[:, at].astype(F32)
        full = jnp.concatenate([prev_x[:, at], cur], 0)
        acc = cur * ck_ref[3:4, at]
        for back in range(1, 4):
            acc = acc + pltpu.roll(full, back, 0)[HALO:] * ck_ref[3 - back : 4 - back, at]
        prev_x[:, at] = cur[BLK - HALO :]
        conv = silu(acc).astype(BF16)
        xc_ref[:, at] = conv
        weighted = (conv.astype(F32) * expanded[:BLK, at]).astype(BF16)
        before = state[:, at]
        sloc_ref[0, :, at] = before.astype(BF16)
        after = expanded[BLK + HALO - 1 : BLK + HALO, at] * before + dot(b_t[c // gw], weighted)
        state[:, at] = after
        pay_ref[:, at] = after.astype(BF16)
    pay_ref[:, width:] = jnp.broadcast_to(three[BLK - 1 :], (STATE, LANES)).astype(BF16)


def local_kernel(xc_ref, bc_ref, crow_ref, ec_ref, cols_ref, sloc_ref, skip_ref, y_ref, e_c, gain_ref):
    heads = crow_ref.shape[0]
    width = xc_ref.shape[1]
    groups = bc_ref.shape[1] // (2 * STATE)
    gw = width // groups

    @pl.when(pl.program_id(0) == 0)
    def _():
        e_c[...] = spread(0, heads, width)
        skip = jnp.concatenate(high_low(skip_ref[...]), 1)
        skip = jnp.concatenate([skip, jnp.zeros((1, LANES - 2 * heads), F32)], 1)
        gain_ref[...] = dot(jnp.broadcast_to(skip, (HALO, LANES)).astype(BF16), e_c[...])

    lane = lax.broadcasted_iota(jnp.int32, (BLK, LANES), 1)
    row = lax.broadcasted_iota(jnp.int32, (BLK, BLK), 0)
    left = lane < HEAD_DIM
    causal = row >= lax.broadcasted_iota(jnp.int32, (BLK, BLK), 1)
    for g in range(groups):
        b_g = bc_ref[:, g * STATE : (g + 1) * STATE]
        c_g = bc_ref[:, (groups + g) * STATE : (groups + g + 1) * STATE]
        scores = jnp.where(causal, dot_t(c_g, b_g), 0.0)
        for c in range(g * gw, (g + 1) * gw, LANES):
            at = slice(c, c + LANES)
            mixing = []
            for h in (c // HEAD_DIM, c // HEAD_DIM + 1):
                gap = jnp.minimum(cols_ref[:, h : h + 1] - crow_ref[h : h + 1], 0.0)
                mixing.append((jnp.exp2(gap) * scores).astype(BF16))
            x = xc_ref[:, at]
            nil = jnp.zeros_like(x)
            stacked = jnp.concatenate([jnp.where(left, x, nil), jnp.where(left, nil, x)], 0)
            y = dot(jnp.concatenate(mixing, 1), stacked)
            carry = dot(c_g, sloc_ref[0, :, at])
            y = y + dot(ec_ref[...], e_c[:, at]) * carry + gain_ref[0:1, at] * x.astype(F32)
            y_ref[:, at] = y.astype(BF16)


def prefix_kernel(pay_ref, after_ref, out_ref, *, heads):
    width = out_ref.shape[2]
    decays = dot(pay_ref[:, 0, width:], spread(heads, heads, width))
    running = jnp.zeros(out_ref.shape[1:], F32)
    for slab in range(out_ref.shape[0]):
        out_ref[slab] = running.astype(BF16)
        running = decays[slab : slab + 1] * running + pay_ref[slab, :, :width].astype(F32)


def project_kernel(
    y_ref, bc_ref, cols_ref, enter_ref, gate_ref, gain_ref, w_ref, after_ref, out_ref, e_c, normed,
    *, heads, tiles,
):
    i = pl.program_id(0)
    width = y_ref.shape[1]
    groups = bc_ref.shape[1] // (2 * STATE)
    gw = width // groups

    @pl.when(i == 0)
    def _():
        e_c[...] = spread(heads, heads, width)

    @pl.when(i < tiles)
    def _():
        grown = cols_ref[...].astype(BF16)
        at_rows = pl.ds(pl.multiple_of(i * BLK, BLK), BLK)
        for g in range(groups):
            at = slice(g * gw, (g + 1) * gw)
            c_g = bc_ref[:, (groups + g) * STATE : (groups + g + 1) * STATE]
            carry = dot(c_g, enter_ref[:, at])
            y = y_ref[:, at].astype(F32) + dot(grown, e_c[:, at]) * carry
            gated = y * silu(gate_ref[:, at].astype(F32))
            square_mean = jnp.mean(gated * gated, axis=-1, keepdims=True)
            scaled = gated * lax.rsqrt(square_mean + epsilon) * gain_ref[:, at]
            normed[at_rows, at] = scaled.astype(BF16)

    @pl.when(i >= tiles)
    def _():
        out_ref[0] = dot(normed[...], w_ref[...]).astype(BF16)


def final_kernel(where_ref, own_ref, right_ref, left_ref, *rest):
    out_ref = rest[-1]
    total = own_ref[0].astype(F32) + right_ref[...].astype(F32) + left_ref[...].astype(F32)
    out_ref[...] = total.astype(BF16)


def along_line(shares, count, mine):
    up = down = None
    for s in range(count - 1):
        up_for = jnp.minimum(count - 1 - s + mine, count - 1)
        down_for = jnp.maximum(mine - (count - 1) + s, 0)
        up_part = lax.dynamic_index_in_dim(shares, up_for, 0, keepdims=False)
        down_part = lax.dynamic_index_in_dim(shares, down_for, 0, keepdims=False)
        if s:
            up_part = (up_part.astype(F32) + up.astype(F32)).astype(BF16)
            down_part = (down_part.astype(F32) + down.astype(F32)).astype(BF16)
        up = lax.ppermute(up_part, "chan", [(a, a + 1) for a in range(s + 1)])
        down = lax.ppermute(down_part, "chan", [(a, a - 1) for a in range(count - 1 - s, count)])
    return up, down


def params():
    return pltpu.CompilerParams(
        dimension_semantics=("arbitrary",), vmem_limit_bytes=VMEM_LIMIT
    )


def whole(shape):
    return pl.BlockSpec(shape, lambda b: (0,) * len(shape))


def rows(count, width, start=0):
    return pl.BlockSpec((count, width), lambda b: (start + b, 0))


def local(
    inner_input, state_maps, gate_input, step_input, log_decay_rate, step_bias,
    skip_gain, conv_kernel, map_kernel, norm_gain, out_weight,
):
    tokens, width = inner_input.shape
    groups = state_maps.shape[2]
    parts = 2 * groups
    heads = step_input.shape[1]
    blocks = tokens // BLK
    slabs = lax.axis_size("seq")
    chans = lax.axis_size("chan")
    features = out_weight.shape[1]
    map_width = parts * STATE

    tail = jnp.concatenate(
        [inner_input[tokens - HALO :], state_maps[tokens - HALO :].reshape(HALO, map_width)], 1
    )
    tail = lax.ppermute(tail, "seq", [(i, i + 1) for i in range(slabs - 1)])
    xc, bc, crow, ec, cols, sloc, pay = pl.pallas_call(
        states_kernel,
        grid=(blocks,),
        in_specs=[
            rows(BLK, width),
            rows(BLK * parts, STATE),
            pl.BlockSpec((heads, BLK), lambda b: (0, b)),
            whole((HALO, width + map_width)),
            whole((1, heads)),
            whole((1, heads)),
            whole((4, width)),
            whole((4 * parts, STATE)),
        ],
        out_specs=[
            rows(BLK, width),
            rows(BLK, map_width),
            pl.BlockSpec((heads, BLK), lambda b: (0, b)),
            rows(BLK, LANES),
            rows(BLK, LANES),
            pl.BlockSpec((1, STATE, width), lambda b: (b, 0, 0)),
            whole((STATE, width + LANES)),
        ],
        out_shape=[
            jax.ShapeDtypeStruct((tokens, width), BF16),
            jax.ShapeDtypeStruct((tokens, map_width), BF16),
            jax.ShapeDtypeStruct((heads, tokens), F32),
            jax.ShapeDtypeStruct((tokens, LANES), BF16),
            jax.ShapeDtypeStruct((tokens, LANES), F32),
            jax.ShapeDtypeStruct((blocks, STATE, width), BF16),
            jax.ShapeDtypeStruct((STATE, width + LANES), BF16),
        ],
        scratch_shapes=[
            pltpu.VMEM((heads, LANES), F32),
            pltpu.VMEM((STATE, width), F32),
            pltpu.VMEM((HALO, width), F32),
            pltpu.VMEM((parts, HALO, STATE), F32),
            pltpu.VMEM((LANES, width), BF16),
            pltpu.VMEM((BLK * parts, BLK * parts), BF16),
            pltpu.VMEM((BLK, BLK), BF16),
        ],
        compiler_params=params(),
        name="states",
    )(
        inner_input, state_maps.reshape(tokens * parts, STATE), step_input.T, tail,
        step_bias.reshape(1, heads), log_decay_rate.reshape(1, heads), conv_kernel, map_kernel.reshape(4 * parts, STATE),
    )

    part = STATE // slabs
    arrived = lax.all_to_all(
        pay.reshape(slabs, part, width + LANES), "seq", split_axis=0, concat_axis=0, tiled=True
    )

    skip_row = skip_gain.reshape(1, heads)

    def local_part(start, count):
        return pl.pallas_call(
            local_kernel,
            grid=(count,),
            in_specs=[
                rows(BLK, width, start),
                rows(BLK, map_width, start),
                pl.BlockSpec((heads, BLK), lambda b: (0, b + start)),
                rows(BLK, LANES, start),
                rows(BLK, LANES, start),
                pl.BlockSpec((1, STATE, width), lambda b: (b + start, 0, 0)),
                whole((1, heads)),
            ],
            out_specs=rows(BLK, width),
            out_shape=jax.ShapeDtypeStruct((count * BLK, width), BF16),
            scratch_shapes=[pltpu.VMEM((LANES, width), BF16), pltpu.VMEM((HALO, width), F32)],
            compiler_params=params(),
            name="local_part",
        )(xc, bc, crow, ec, cols, sloc, skip_row)

    half = blocks // 2
    y_halves = [local_part(0, half), local_part(half, blocks - half)]

    entering = pl.pallas_call(
        functools.partial(prefix_kernel, heads=heads),
        out_shape=jax.ShapeDtypeStruct((slabs, part, width), BF16),
        in_specs=[pl.BlockSpec(memory_space=pltpu.VMEM), pl.BlockSpec(memory_space=pl.ANY)],
        out_specs=pl.BlockSpec(memory_space=pltpu.VMEM),
        compiler_params=pltpu.CompilerParams(vmem_limit_bytes=VMEM_LIMIT),
        name="prefix",
    )(arrived, y_halves[0])
    entering = lax.all_to_all(entering, "seq", split_axis=0, concat_axis=0, tiled=True)
    entering = entering.reshape(STATE, width)

    per_chunk = blocks // CHUNKS
    part_out = features // chans
    norm_row = norm_gain.reshape(1, width)
    mine = lax.axis_index("chan")
    where = mine.reshape(1).astype(jnp.int32)
    out = None
    sums = []
    for chunk in range(CHUNKS):
        start = chunk * per_chunk
        y_half, y_start = (y_halves[0], start) if start < half else (y_halves[1], start - half)

        def tile(width, start):
            return pl.BlockSpec(
                (BLK, width), lambda i: (start + jnp.minimum(i, per_chunk - 1), 0)
            )

        shares = pl.pallas_call(
            functools.partial(project_kernel, heads=heads, tiles=per_chunk),
            grid=(per_chunk + chans,),
            in_specs=[
                tile(width, y_start),
                tile(map_width, start),
                tile(LANES, start),
                whole((STATE, width)),
                tile(width, start),
                whole((1, width)),
                pl.BlockSpec((width, part_out), lambda i: (0, jnp.maximum(i - per_chunk, 0))),
                pl.BlockSpec(memory_space=pl.ANY),
            ],
            out_specs=pl.BlockSpec(
                (1, per_chunk * BLK, part_out), lambda i: (jnp.maximum(i - per_chunk, 0), 0, 0)
            ),
            out_shape=jax.ShapeDtypeStruct((chans, per_chunk * BLK, part_out), BF16),
            scratch_shapes=[
                pltpu.VMEM((LANES, width), BF16),
                pltpu.VMEM((per_chunk * BLK, width), BF16),
            ],
            compiler_params=params(),
            name="project",
        )(y_half, bc, cols, entering, gate_input, norm_row, out_weight, y_halves[1])
        sums.append((start, shares) + along_line(shares, chans, mine))

    for start, shares, up, down in sums:
        count = shares.shape[1] // BLK

        def plain(i, where):
            return (i, 0)

        def placed(i, where, start=start):
            return (start + i, 0)

        operands = [where, shares, up, down]
        in_specs = [
            pl.BlockSpec((1, BLK, part_out), lambda i, where: (where[0], i, 0)),
            pl.BlockSpec((BLK, part_out), plain),
            pl.BlockSpec((BLK, part_out), plain),
        ]
        aliases = {}
        if out is not None:
            aliases = {len(operands): 0}
            operands.append(out)
            in_specs.append(pl.BlockSpec(memory_space=pl.ANY))
        out = pl.pallas_call(
            final_kernel,
            grid_spec=pltpu.PrefetchScalarGridSpec(
                num_scalar_prefetch=1,
                grid=(count,),
                in_specs=in_specs,
                out_specs=pl.BlockSpec((BLK, part_out), placed),
            ),
            out_shape=jax.ShapeDtypeStruct((tokens, part_out), BF16),
            input_output_aliases=aliases,
            compiler_params=params(),
            name="final",
        )(*operands)
    return out


def solution(mesh):
    return jax.shard_map(
        local,
        mesh=mesh,
        in_specs=(
            P("seq", "chan"),
            P("seq", None, "chan", None),
            P("seq", "chan"),
            P("seq", "chan"),
            P("chan"),
            P("chan"),
            P("chan"),
            P(None, "chan"),
            P(None, None, "chan", None),
            P("chan"),
            P("chan", None),
        ),
        out_specs=P("seq", "chan"),
        check_vma=False,
    )
```

```python
import functools

import jax
import jax.numpy as jnp
import numpy as np
from jax import lax
from jax.experimental import pallas as pl
from jax.experimental.pallas import tpu as pltpu
from jax.sharding import PartitionSpec as P

HEAD_DIM = 64
STATE = 128
BLK = 128
LANES = 128
HALO = 8
WIDE = 256

step_limit = 0.5
epsilon = 1e-05
LOG2E = 1.4426950408889634
F32 = jnp.float32
BF16 = jnp.bfloat16
VMEM_LIMIT = 40 * 1024 * 1024


def silu(v):
    half = 0.5 * v
    return half + half * jnp.tanh(half)


def high_low(v):
    high = v.astype(BF16).astype(F32)
    return high, v - high


def spread(first_row, heads, width):
    result = np.zeros((LANES, width), np.float32)
    for k in range(2 * heads):
        h = k % heads
        result[first_row + k, h * HEAD_DIM : (h + 1) * HEAD_DIM] = 1.0
    return jnp.asarray(result, BF16)


def dot(a, b):
    return jnp.dot(a, b, preferred_element_type=F32)


def dot_t(a, b):
    return lax.dot_general(a, b, (((1,), (1,)), ((), ())), preferred_element_type=F32)


def column(row):
    count = row.shape[1]
    eye = lax.broadcasted_iota(jnp.int32, (count, count), 0) == lax.broadcasted_iota(
        jnp.int32, (count, count), 1
    )
    return jnp.sum(jnp.where(eye, row, 0.0), axis=1, keepdims=True)


def padded(pieces):
    rows = jnp.concatenate(pieces, 0)
    if rows.shape[0] == LANES:
        return rows
    return jnp.concatenate([rows, jnp.zeros((LANES - rows.shape[0], rows.shape[1]), rows.dtype)], 0)


def conv(before, cur, taps):
    full = jnp.concatenate([before, cur], 0)
    acc = cur * taps[3]
    for back in range(1, 4):
        acc = acc + pltpu.roll(full, back, 0)[HALO:] * taps[3 - back]
    return silu(acc).astype(BF16)


def states_kernel(
    x_ref, maps_ref, step_ref, tail_ref, mtail_ref, bias_ref, rate_ref, ck_ref, mk_ref, e_ref,
    xc_ref, bc_ref, bt_ref, crow_ref, cols_ref, w_ref, g_ref, pay_ref,
    weighted,
):
    c = pl.program_id(0)
    heads, tokens = step_ref.shape
    parts = mk_ref.shape[0] // 4
    groups = parts // 2
    blocks = tokens // BLK

    @pl.when(c == 0)
    def _():
        bias, rate = column(bias_ref[...]), -jnp.exp(column(rate_ref[...]))
        v = step_ref[...] + bias
        step = jnp.minimum(jnp.maximum(v, 0.0) + jnp.log1p(jnp.exp(-jnp.abs(v))), step_limit)
        log_step = rate * step
        first, rest = high_low(log_step)
        second, third = high_low(rest)
        pieces = []
        for b in range(blocks):
            at = slice(b * BLK, (b + 1) * BLK)
            pieces += [first[:, at], second[:, at], third[:, at]]
        row = lax.broadcasted_iota(jnp.int32, (BLK, BLK), 0)
        col = lax.broadcasted_iota(jnp.int32, (BLK, BLK), 1)
        tri = jnp.where(row <= col, 1.0, 0.0).astype(BF16)
        sums = dot(jnp.concatenate(pieces, 0).astype(BF16), tri)
        cums, leads = [], [jnp.zeros((heads, 1), F32)]
        for b in range(blocks):
            at = 3 * b * heads
            cum = (
                sums[at : at + heads]
                + sums[at + heads : at + 2 * heads]
                + sums[at + 2 * heads : at + 3 * heads]
            )
            cums.append(cum)
            leads.append(leads[-1] + cum[:, BLK - 1 : BLK])
        last = None
        for b in range(blocks):
            at = slice(b * BLK, (b + 1) * BLK)
            cum, step_b = cums[b], step[:, at]
            total = cum[:, BLK - 1 : BLK]
            block_weight = jnp.exp(total - cum) * step_b
            slab_weight = jnp.exp(leads[blocks] - (leads[b] + cum)) * step_b
            grown = jnp.exp(cum)
            entered = jnp.exp(cum + leads[b])
            crow_ref[:, at] = (cum - jnp.log(step_b)) * LOG2E
            w_ref[at, :] = padded(high_low(slab_weight) + high_low(block_weight)).T.astype(BF16)
            last = padded(high_low(grown) + high_low(entered)).T
            g_ref[at, :] = last.astype(BF16)
            cols_ref[at, :] = padded((cum * LOG2E,)).T
        pay_ref[:, heads * HEAD_DIM :] = jnp.broadcast_to(last[BLK - 1 :], (STATE, LANES)).astype(BF16)

        row = lax.broadcasted_iota(jnp.int32, (BLK * parts, BLK * parts), 0)
        col = lax.broadcasted_iota(jnp.int32, (BLK * parts, BLK * parts), 1)
        source = (row & (BLK - 1)) * parts + row // BLK
        pick = jnp.where(col == source, 1.0, 0.0).astype(BF16)
        before = [mtail_ref[:, q * STATE : (q + 1) * STATE].astype(F32) for q in range(parts)]
        for b in range(blocks):
            ordered = dot(pick, maps_ref[b * BLK * parts : (b + 1) * BLK * parts, :])
            for q in range(parts):
                cur = ordered[q * BLK : (q + 1) * BLK]
                taps = [mk_ref[k * parts + q : k * parts + q + 1] for k in range(4)]
                result = conv(before[q], cur, taps)
                before[q] = cur[BLK - HALO :]
                bc_ref[b * BLK : (b + 1) * BLK, q * STATE : (q + 1) * STATE] = result
                if q < groups:
                    bt_ref[q, :, b * BLK : (b + 1) * BLK] = result.astype(F32).T.astype(BF16)

    taps = [ck_ref[k : k + 1] for k in range(4)]
    before = tail_ref[...].astype(F32)
    for b in range(blocks):
        at = slice(b * BLK, (b + 1) * BLK)
        cur = x_ref[at, :].astype(F32)
        result = conv(before, cur, taps)
        before = cur[BLK - HALO :]
        xc_ref[at, :] = result
        weighted[at, :] = (result.astype(F32) * dot(w_ref[at, :], e_ref[...])).astype(BF16)
    step_width = x_ref.shape[1]
    group = c * step_width * groups // (heads * HEAD_DIM)
    at = pl.ds(pl.multiple_of(c * step_width, step_width), step_width)
    pay_ref[:, at] = dot(bt_ref[group], weighted[...]).astype(BF16)


def local_kernel(
    xc_ref, bc_ref, bt_ref, crow_ref, cols_ref, w_ref, g_ref, skip_ref, low_ref, high_ref, *rest
):
    y_ref, state, gain_ref = rest[-3:]
    heads = crow_ref.shape[0]
    width = xc_ref.shape[1]
    groups = bt_ref.shape[0]
    gw = width // groups

    @pl.when(pl.program_id(0) == 0)
    def _():
        state[...] = rest[0][...] if len(rest) > 4 else jnp.zeros_like(state)
        skip = jnp.concatenate(high_low(skip_ref[...]), 1)
        skip = jnp.concatenate([skip, jnp.zeros((1, LANES - 2 * heads), F32)], 1)
        gain_ref[...] = dot(jnp.broadcast_to(skip, (HALO, LANES)).astype(BF16), low_ref[...])

    left = lax.broadcasted_iota(jnp.int32, (BLK, LANES), 1) < HEAD_DIM
    row = lax.broadcasted_iota(jnp.int32, (BLK, BLK), 0)
    causal = row >= lax.broadcasted_iota(jnp.int32, (BLK, BLK), 1)
    for g in range(groups):
        b_g = bc_ref[:, g * STATE : (g + 1) * STATE]
        c_g = bc_ref[:, (groups + g) * STATE : (groups + g + 1) * STATE]
        scores = jnp.where(causal, dot_t(c_g, b_g), 0.0)
        for wide in range(g * gw, (g + 1) * gw, 2 * LANES):
            at_wide = slice(wide, wide + 2 * LANES)
            grown = dot(g_ref[...], low_ref[:, at_wide])
            before = state[:, at_wide]
            carry = grown * dot(c_g, before.astype(BF16))
            x_wide = xc_ref[:, at_wide].astype(F32)
            weighted = (x_wide * dot(w_ref[...], high_ref[:, at_wide])).astype(BF16)
            state[:, at_wide] = grown[BLK - 1 :] * before + dot(bt_ref[g], weighted)
            carry = carry + gain_ref[0:1, at_wide] * x_wide
            for k in range(2):
                at = slice(wide + k * LANES, wide + (k + 1) * LANES)
                mixing = []
                for h in (at.start // HEAD_DIM, at.start // HEAD_DIM + 1):
                    gap = jnp.minimum(cols_ref[:, h : h + 1] - crow_ref[h : h + 1], 0.0)
                    mixing.append((jnp.exp2(gap) * scores).astype(BF16))
                x = xc_ref[:, at]
                nil = jnp.zeros_like(x)
                stacked = jnp.concatenate([jnp.where(left, x, nil), jnp.where(left, nil, x)], 0)
                y = dot(jnp.concatenate(mixing, 1), stacked) + carry[:, k * LANES : (k + 1) * LANES]
                y_ref[:, at] = y.astype(BF16)


def prefix_kernel(pay_ref, e_ref, after_ref, out_ref):
    width = out_ref.shape[2]
    decays = dot(pay_ref[:, 0, width:], e_ref[...])
    running = jnp.zeros(out_ref.shape[1:], F32)
    for slab in range(out_ref.shape[0]):
        out_ref[slab] = running.astype(BF16)
        running = decays[slab : slab + 1] * running + pay_ref[slab, :, :width].astype(F32)


def ends_kernel(
    y_ref, bc_ref, g_ref, enter_ref, gate_ref, gain_ref, w_ref, e_ref, after_ref,
    shares_ref, up_ref, down_ref, normed_ref, *, tiles,
):
    i = pl.program_id(0)
    width = y_ref.shape[1]
    groups = bc_ref.shape[1] // (2 * STATE)
    gw = width // groups

    @pl.when(i < tiles)
    def _():
        at_rows = pl.ds(pl.multiple_of(i * BLK, BLK), BLK)
        for g in range(groups):
            at = slice(g * gw, (g + 1) * gw)
            c_g = bc_ref[:, (groups + g) * STATE : (groups + g + 1) * STATE]
            carry = dot(c_g, enter_ref[:, at])
            y = y_ref[:, at].astype(F32) + dot(g_ref[...], e_ref[:, at]) * carry
            gated = y * silu(gate_ref[:, at].astype(F32))
            square_mean = jnp.mean(gated * gated, axis=-1, keepdims=True)
            scaled = gated * lax.rsqrt(square_mean + epsilon) * gain_ref[:, at]
            normed_ref[at_rows, at] = scaled.astype(BF16)

    @pl.when(i >= tiles)
    def _():
        shares_ref[0] = dot(normed_ref[...], w_ref[...]).astype(BF16)

    @pl.when(i == tiles)
    def _():
        down_ref[...] = shares_ref[0]

    @pl.when(i == tiles + 1)
    def _():
        up_ref[...] = shares_ref[0]


def middle_kernel(normed_ref, w_ref, ends_ref, after_ref, shares_ref):
    shares_ref[0] = dot(normed_ref[...], w_ref[...]).astype(BF16)


def onward_kernel(where_ref, up_own_ref, down_own_ref, up_ref, down_ref, up_out, down_out):
    up_out[...] = (up_own_ref[0].astype(F32) + up_ref[...].astype(F32)).astype(BF16)
    down_out[...] = (down_own_ref[0].astype(F32) + down_ref[...].astype(F32)).astype(BF16)


def final_kernel(where_ref, own_ref, up_ref, down_ref, *rest):
    out_ref = rest[-1]
    total = own_ref[0].astype(F32) + up_ref[...].astype(F32) + down_ref[...].astype(F32)
    out_ref[...] = total.astype(BF16)


def params():
    return pltpu.CompilerParams(
        dimension_semantics=("arbitrary",), vmem_limit_bytes=VMEM_LIMIT
    )


def whole(shape):
    return pl.BlockSpec(shape, lambda *b: (0,) * len(shape))


def unread():
    return pl.BlockSpec(memory_space=pl.ANY)


def shaped(shape, dtype=BF16):
    return jax.ShapeDtypeStruct(shape, dtype)


def local(
    inner_input, state_maps, gate_input, step_input, log_decay_rate, step_bias,
    skip_gain, conv_kernel, map_kernel, norm_gain, out_weight,
):
    tokens, width = inner_input.shape
    groups = state_maps.shape[2]
    parts = 2 * groups
    heads = step_input.shape[1]
    blocks = tokens // BLK
    slabs = lax.axis_size("seq")
    chans = lax.axis_size("chan")
    features = out_weight.shape[1]
    map_width = parts * STATE
    low, high = spread(0, heads, width), spread(2 * heads, heads, width)

    tail = jnp.concatenate(
        [inner_input[tokens - HALO :], state_maps[tokens - HALO :].reshape(HALO, map_width)], 1
    )
    tail = lax.ppermute(tail, "seq", [(i, i + 1) for i in range(slabs - 1)])

    def lanes_at(count):
        return pl.BlockSpec((count, WIDE), lambda c: (0, c))

    xc, bc, bt, crow, cols, w_hl, g_hl, pay = pl.pallas_call(
        states_kernel,
        grid=(width // WIDE,),
        in_specs=[
            lanes_at(tokens),
            whole((tokens * parts, STATE)),
            whole((heads, tokens)),
            lanes_at(HALO),
            pl.BlockSpec((HALO, map_width), lambda c: (0, width // map_width)),
            whole((1, heads)),
            whole((1, heads)),
            lanes_at(4),
            whole((4 * parts, STATE)),
            lanes_at(LANES),
        ],
        out_specs=[
            lanes_at(tokens),
            whole((tokens, map_width)),
            whole((groups, STATE, tokens)),
            whole((heads, tokens)),
            whole((tokens, LANES)),
            whole((tokens, LANES)),
            whole((tokens, LANES)),
            whole((STATE, width + LANES)),
        ],
        out_shape=[
            shaped((tokens, width)),
            shaped((tokens, map_width)),
            shaped((groups, STATE, tokens)),
            shaped((heads, tokens), F32),
            shaped((tokens, LANES), F32),
            shaped((tokens, LANES)),
            shaped((tokens, LANES)),
            shaped((STATE, width + LANES)),
        ],
        scratch_shapes=[pltpu.VMEM((tokens, WIDE), BF16)],
        compiler_params=params(),
        name="states",
    )(
        inner_input, state_maps.reshape(tokens * parts, STATE), step_input.T, tail, tail,
        step_bias.reshape(1, heads), log_decay_rate.reshape(1, heads),
        conv_kernel, map_kernel.reshape(4 * parts, STATE), low,
    )

    part = STATE // slabs
    arrived = lax.all_to_all(
        pay.reshape(slabs, part, width + LANES), "seq", split_axis=0, concat_axis=0, tiled=True
    )

    def local_part(start, count, state, after):
        def tile(width):
            return pl.BlockSpec((BLK, width), lambda b: (start + b, 0))

        operands = [xc, bc, bt, crow, cols, w_hl, g_hl, skip_gain.reshape(1, heads), low, high]
        specs = [
            tile(width),
            tile(map_width),
            pl.BlockSpec((groups, STATE, BLK), lambda b: (0, 0, start + b)),
            pl.BlockSpec((heads, BLK), lambda b: (0, start + b)),
            tile(LANES),
            tile(LANES),
            tile(LANES),
            whole((1, heads)),
            whole((LANES, width)),
            whole((LANES, width)),
        ]
        if state is not None:
            operands.append(state)
            specs.append(whole((STATE, width)))
        operands.append(after)
        specs.append(unread())
        return pl.pallas_call(
            local_kernel,
            grid=(count,),
            in_specs=specs,
            out_specs=[
                pl.BlockSpec((BLK, width), lambda b: (b, 0)),
                whole((STATE, width)),
            ],
            out_shape=[shaped((count * BLK, width)), shaped((STATE, width), F32)],
            scratch_shapes=[pltpu.VMEM((HALO, width), F32)],
            compiler_params=params(),
            name="local_part",
        )(*operands)

    third = (blocks - blocks // 4) // 2
    spans = [(0, blocks // 4), (blocks // 4, third), (blocks // 4 + third, third)]
    y_first, state = local_part(*spans[0], None, pay)
    y_second, state = local_part(*spans[1], state, y_first)

    entering = pl.pallas_call(
        prefix_kernel,
        out_shape=shaped((slabs, part, width)),
        in_specs=[
            pl.BlockSpec(memory_space=pltpu.VMEM),
            pl.BlockSpec(memory_space=pltpu.VMEM),
            unread(),
        ],
        out_specs=pl.BlockSpec(memory_space=pltpu.VMEM),
        compiler_params=pltpu.CompilerParams(vmem_limit_bytes=VMEM_LIMIT),
        name="prefix",
    )(arrived, high, y_first)
    entering = lax.all_to_all(entering, "seq", split_axis=0, concat_axis=0, tiled=True)
    entering = entering.reshape(STATE, width)

    part_out = features // chans
    norm_row = norm_gain.reshape(1, width)
    mine = lax.axis_index("chan").astype(jnp.int32)
    where = mine.reshape(1)

    def project(start, count, y, after):
        def tile(width, start=start):
            return pl.BlockSpec((BLK, width), lambda i: (start + jnp.minimum(i, count - 1), 0))

        def end(i):
            return jnp.where(i <= count, 0, chans - 1)

        size = count * BLK
        shares, up, down, normed = pl.pallas_call(
            functools.partial(ends_kernel, tiles=count),
            grid=(count + 2,),
            in_specs=[
                tile(width, 0),
                tile(map_width),
                tile(LANES),
                whole((STATE, width)),
                tile(width),
                whole((1, width)),
                pl.BlockSpec((width, part_out), lambda i: (0, end(i))),
                whole((LANES, width)),
                unread(),
            ],
            out_specs=[
                pl.BlockSpec((1, size, part_out), lambda i: (end(i), 0, 0)),
                whole((size, part_out)),
                whole((size, part_out)),
                whole((size, width)),
            ],
            out_shape=[
                shaped((chans, size, part_out)),
                shaped((size, part_out)),
                shaped((size, part_out)),
                shaped((size, width)),
            ],
            compiler_params=params(),
            name="project_ends",
        )(y, bc, g_hl, entering, gate_input, norm_row, out_weight, high, after)
        return shares, up, down, normed

    def project_middle(shares, normed, after):
        size = normed.shape[0]
        return pl.pallas_call(
            middle_kernel,
            grid=(chans - 2,),
            in_specs=[
                whole((size, width)),
                pl.BlockSpec((width, part_out), lambda i: (0, i + 1)),
                unread(),
                unread(),
            ],
            out_specs=pl.BlockSpec((1, size, part_out), lambda i: (i + 1, 0, 0)),
            out_shape=shaped((chans, size, part_out)),
            input_output_aliases={2: 0},
            compiler_params=params(),
            name="project_middle",
        )(normed, out_weight, shares, after)

    def permuted(up, down, s):
        up = lax.ppermute(up, "chan", [(a, a + 1) for a in range(s + 1)])
        down = lax.ppermute(down, "chan", [(a, a - 1) for a in range(chans - 1 - s, chans)])
        return up, down

    def onward(shares, up, down, s):
        def plain(i, where):
            return (i, 0)

        return pl.pallas_call(
            onward_kernel,
            grid_spec=pltpu.PrefetchScalarGridSpec(
                num_scalar_prefetch=1,
                grid=(shares.shape[1] // BLK,),
                in_specs=[
                    pl.BlockSpec(
                        (1, BLK, part_out),
                        lambda i, where: (jnp.minimum(chans - 1 - s + where[0], chans - 1), i, 0),
                    ),
                    pl.BlockSpec(
                        (1, BLK, part_out),
                        lambda i, where: (jnp.maximum(where[0] - (chans - 1) + s, 0), i, 0),
                    ),
                    pl.BlockSpec((BLK, part_out), plain),
                    pl.BlockSpec((BLK, part_out), plain),
                ],
                out_specs=[pl.BlockSpec((BLK, part_out), plain)] * 2,
            ),
            out_shape=[shaped(up.shape)] * 2,
            compiler_params=params(),
            name="onward",
        )(where, shares, shares, up, down)

    def final(start, shares, up, down, out):
        def plain(i, where):
            return (i, 0)

        operands = [where, shares, up, down]
        in_specs = [
            pl.BlockSpec((1, BLK, part_out), lambda i, where: (where[0], i, 0)),
            pl.BlockSpec((BLK, part_out), plain),
            pl.BlockSpec((BLK, part_out), plain),
        ]
        aliases = {}
        if out is not None:
            aliases = {len(operands): 0}
            operands.append(out)
            in_specs.append(unread())
        return pl.pallas_call(
            final_kernel,
            grid_spec=pltpu.PrefetchScalarGridSpec(
                num_scalar_prefetch=1,
                grid=(shares.shape[1] // BLK,),
                in_specs=in_specs,
                out_specs=pl.BlockSpec((BLK, part_out), lambda i, where: (start + i, 0)),
            ),
            out_shape=shaped((tokens, part_out)),
            input_output_aliases=aliases,
            compiler_params=params(),
            name="final",
        )(*operands)

    after, y = y_second, y_first
    sums = []
    for k, (start, count) in enumerate(spans):
        shares, up, down, normed = project(start, count, y, after)
        up, down = permuted(up, down, 0)
        shares = project_middle(shares, normed, normed)
        if k == 0:
            y_third, _ = local_part(*spans[2], state, shares)
        for s in range(1, chans - 1):
            up, down = onward(shares, up, down, s)
            up, down = permuted(up, down, s)
        sums.append((start, shares, up, down))
        y = (y_second, y_third, None)[k]
        after = shares
    out = None
    for start, shares, up, down in sums:
        out = final(start, shares, up, down, out)
    return out


def solution(mesh):
    return jax.shard_map(
        local,
        mesh=mesh,
        in_specs=(
            P("seq", "chan"),
            P("seq", None, "chan", None),
            P("seq", "chan"),
            P("seq", "chan"),
            P("chan"),
            P("chan"),
            P("chan"),
            P(None, "chan"),
            P(None, None, "chan", None),
            P("chan"),
            P("chan", None),
        ),
        out_specs=P("seq", "chan"),
        check_vma=False,
    )
```

```python
import functools

import jax
import jax.numpy as jnp
import numpy as np
from jax import lax
from jax.experimental import pallas as pl
from jax.experimental.pallas import tpu as pltpu
from jax.sharding import PartitionSpec as P

HEAD_DIM = 64
STATE = 128
BLK = 128
LANES = 128
HALO = 8
WIDE = 256

step_limit = 0.5
epsilon = 1e-05
LOG2E = 1.4426950408889634
F32 = jnp.float32
BF16 = jnp.bfloat16
VMEM_LIMIT = 58 * 1024 * 1024
SMALL_LIMIT = 10 * 1024 * 1024


def silu(v):
    half = 0.5 * v
    return half + half * jnp.tanh(half)


def high_low(v):
    high = v.astype(BF16).astype(F32)
    return high, v - high


def spread(first_row, heads, width):
    result = np.zeros((LANES, width), np.float32)
    for k in range(2 * heads):
        h = k % heads
        result[first_row + k, h * HEAD_DIM : (h + 1) * HEAD_DIM] = 1.0
    return jnp.asarray(result, BF16)


def dot(a, b):
    return jnp.dot(a, b, preferred_element_type=F32)


def dot_t(a, b):
    return lax.dot_general(a, b, (((1,), (1,)), ((), ())), preferred_element_type=F32)


def column(row):
    count = row.shape[1]
    eye = lax.broadcasted_iota(jnp.int32, (count, count), 0) == lax.broadcasted_iota(
        jnp.int32, (count, count), 1
    )
    return jnp.sum(jnp.where(eye, row, 0.0), axis=1, keepdims=True)


def padded(pieces):
    rows = jnp.concatenate(pieces, 0)
    if rows.shape[0] == LANES:
        return rows
    return jnp.concatenate([rows, jnp.zeros((LANES - rows.shape[0], rows.shape[1]), rows.dtype)], 0)


def conv(before, cur, taps):
    full = jnp.concatenate([before, cur], 0)
    acc = cur * taps[3]
    for back in range(1, 4):
        acc = acc + pltpu.roll(full, back, 0)[HALO:] * taps[3 - back]
    return silu(acc).astype(BF16)


def states_kernel(
    x_ref, maps_ref, step_ref, tail_ref, mtail_ref, bias_ref, rate_ref, ck_ref, mk_ref, e_ref,
    xc_ref, bc_ref, bt_ref, crow_ref, cols_ref, w_ref, g_ref, pay_ref,
    weighted,
):
    c = pl.program_id(0)
    heads, tokens = step_ref.shape
    parts = mk_ref.shape[0] // 4
    groups = parts // 2
    blocks = tokens // BLK

    @pl.when(c == 0)
    def _():
        bias, rate = column(bias_ref[...]), -jnp.exp(column(rate_ref[...]))
        v = step_ref[...] + bias
        step = jnp.minimum(jnp.maximum(v, 0.0) + jnp.log1p(jnp.exp(-jnp.abs(v))), step_limit)
        log_step = rate * step
        first, rest = high_low(log_step)
        second, third = high_low(rest)
        pieces = []
        for b in range(blocks):
            at = slice(b * BLK, (b + 1) * BLK)
            pieces += [first[:, at], second[:, at], third[:, at]]
        row = lax.broadcasted_iota(jnp.int32, (BLK, BLK), 0)
        col = lax.broadcasted_iota(jnp.int32, (BLK, BLK), 1)
        tri = jnp.where(row <= col, 1.0, 0.0).astype(BF16)
        sums = dot(jnp.concatenate(pieces, 0).astype(BF16), tri)
        cums, leads = [], [jnp.zeros((heads, 1), F32)]
        for b in range(blocks):
            at = 3 * b * heads
            cum = (
                sums[at : at + heads]
                + sums[at + heads : at + 2 * heads]
                + sums[at + 2 * heads : at + 3 * heads]
            )
            cums.append(cum)
            leads.append(leads[-1] + cum[:, BLK - 1 : BLK])
        last = None
        for b in range(blocks):
            at = slice(b * BLK, (b + 1) * BLK)
            cum, step_b = cums[b], step[:, at]
            total = cum[:, BLK - 1 : BLK]
            block_weight = jnp.exp(total - cum) * step_b
            slab_weight = jnp.exp(leads[blocks] - (leads[b] + cum)) * step_b
            grown = jnp.exp(cum)
            entered = jnp.exp(cum + leads[b])
            crow_ref[:, at] = (cum - jnp.log(step_b)) * LOG2E
            w_ref[at, :] = padded(high_low(slab_weight) + high_low(block_weight)).T.astype(BF16)
            last = padded(high_low(grown) + high_low(entered)).T
            g_ref[at, :] = last.astype(BF16)
            cols_ref[at, :] = padded((cum * LOG2E,)).T
        pay_ref[:, heads * HEAD_DIM :] = jnp.broadcast_to(last[BLK - 1 :], (STATE, LANES)).astype(BF16)

        row = lax.broadcasted_iota(jnp.int32, (BLK * parts, BLK * parts), 0)
        col = lax.broadcasted_iota(jnp.int32, (BLK * parts, BLK * parts), 1)
        source = (row & (BLK - 1)) * parts + row // BLK
        pick = jnp.where(col == source, 1.0, 0.0).astype(BF16)
        before = [mtail_ref[:, q * STATE : (q + 1) * STATE].astype(F32) for q in range(parts)]
        for b in range(blocks):
            ordered = dot(pick, maps_ref[b * BLK * parts : (b + 1) * BLK * parts, :])
            for q in range(parts):
                cur = ordered[q * BLK : (q + 1) * BLK]
                taps = [mk_ref[k * parts + q : k * parts + q + 1] for k in range(4)]
                result = conv(before[q], cur, taps)
                before[q] = cur[BLK - HALO :]
                bc_ref[b * BLK : (b + 1) * BLK, q * STATE : (q + 1) * STATE] = result
                if q < groups:
                    bt_ref[q, :, b * BLK : (b + 1) * BLK] = result.astype(F32).T.astype(BF16)

    taps = [ck_ref[k : k + 1] for k in range(4)]
    before = tail_ref[...].astype(F32)
    for b in range(blocks):
        at = slice(b * BLK, (b + 1) * BLK)
        cur = x_ref[at, :].astype(F32)
        result = conv(before, cur, taps)
        before = cur[BLK - HALO :]
        xc_ref[at, :] = result
        weighted[at, :] = (result.astype(F32) * dot(w_ref[at, :], e_ref[...])).astype(BF16)
    step_width = x_ref.shape[1]
    group = c * step_width * groups // (heads * HEAD_DIM)
    at = pl.ds(pl.multiple_of(c * step_width, step_width), step_width)
    pay_ref[:, at] = dot(bt_ref[group], weighted[...]).astype(BF16)


def local_kernel(
    xc_ref, bc_ref, bt_ref, crow_ref, cols_ref, w_ref, g_ref, skip_ref, low_ref, high_ref, *rest
):
    y_ref, state, gain_ref = rest[-3:]
    heads = crow_ref.shape[0]
    width = xc_ref.shape[1]
    groups = bt_ref.shape[0]
    gw = width // groups

    @pl.when(pl.program_id(0) == 0)
    def _():
        state[...] = rest[0][...] if len(rest) > 4 else jnp.zeros_like(state)
        skip = jnp.concatenate(high_low(skip_ref[...]), 1)
        skip = jnp.concatenate([skip, jnp.zeros((1, LANES - 2 * heads), F32)], 1)
        gain_ref[...] = dot(jnp.broadcast_to(skip, (HALO, LANES)).astype(BF16), low_ref[...])

    left = lax.broadcasted_iota(jnp.int32, (BLK, LANES), 1) < HEAD_DIM
    row = lax.broadcasted_iota(jnp.int32, (BLK, BLK), 0)
    causal = row >= lax.broadcasted_iota(jnp.int32, (BLK, BLK), 1)
    for g in range(groups):
        b_g = bc_ref[:, g * STATE : (g + 1) * STATE]
        c_g = bc_ref[:, (groups + g) * STATE : (groups + g + 1) * STATE]
        scores = jnp.where(causal, dot_t(c_g, b_g), 0.0)
        for wide in range(g * gw, (g + 1) * gw, 2 * LANES):
            at_wide = slice(wide, wide + 2 * LANES)
            grown = dot(g_ref[...], low_ref[:, at_wide])
            before = state[:, at_wide]
            carry = grown * dot(c_g, before.astype(BF16))
            x_wide = xc_ref[:, at_wide].astype(F32)
            weighted = (x_wide * dot(w_ref[...], high_ref[:, at_wide])).astype(BF16)
            state[:, at_wide] = grown[BLK - 1 :] * before + dot(bt_ref[g], weighted)
            carry = carry + gain_ref[0:1, at_wide] * x_wide
            for k in range(2):
                at = slice(wide + k * LANES, wide + (k + 1) * LANES)
                mixing = []
                for h in (at.start // HEAD_DIM, at.start // HEAD_DIM + 1):
                    gap = jnp.minimum(cols_ref[:, h : h + 1] - crow_ref[h : h + 1], 0.0)
                    mixing.append((jnp.exp2(gap) * scores).astype(BF16))
                x = xc_ref[:, at]
                nil = jnp.zeros_like(x)
                stacked = jnp.concatenate([jnp.where(left, x, nil), jnp.where(left, nil, x)], 0)
                y = dot(jnp.concatenate(mixing, 1), stacked) + carry[:, k * LANES : (k + 1) * LANES]
                y_ref[:, at] = y.astype(BF16)


def prefix_kernel(pay_ref, e_ref, after_ref, out_ref):
    width = out_ref.shape[2]
    decays = dot(pay_ref[:, 0, width:], e_ref[...])
    running = jnp.zeros(out_ref.shape[1:], F32)
    for slab in range(out_ref.shape[0]):
        out_ref[slab] = running.astype(BF16)
        running = decays[slab : slab + 1] * running + pay_ref[slab, :, :width].astype(F32)


def norm_tile(y_ref, bc_ref, g_ref, enter_ref, gate_ref, gain_ref, e_ref, normed_ref, i):
    width = y_ref.shape[1]
    groups = bc_ref.shape[1] // (2 * STATE)
    gw = width // groups
    at_rows = pl.ds(pl.multiple_of(i * BLK, BLK), BLK)
    for g in range(groups):
        at = slice(g * gw, (g + 1) * gw)
        c_g = bc_ref[:, (groups + g) * STATE : (groups + g + 1) * STATE]
        carry = dot(c_g, enter_ref[:, at])
        y = y_ref[:, at].astype(F32) + dot(g_ref[...], e_ref[:, at]) * carry
        gated = y * silu(gate_ref[:, at].astype(F32))
        square_mean = jnp.mean(gated * gated, axis=-1, keepdims=True)
        scaled = gated * lax.rsqrt(square_mean + epsilon) * gain_ref[:, at]
        normed_ref[at_rows, at] = scaled.astype(BF16)


def direct_kernel(
    where_ref, y_ref, bc_ref, g_ref, enter_ref, gate_ref, gain_ref, e_ref, w_ref, after_ref,
    *rest, tiles,
):
    *out_refs, normed_ref = rest
    i = pl.program_id(0)

    @pl.when(i < tiles)
    def _():
        norm_tile(y_ref, bc_ref, g_ref, enter_ref, gate_ref, gain_ref, e_ref, normed_ref, i)

    for k, out_ref in enumerate(out_refs):
        @pl.when(i == tiles + k)
        def _(out_ref=out_ref):
            out_ref[...] = dot(normed_ref[...], w_ref[...]).astype(BF16)


def more_kernel(where_ref, normed_ref, w_ref, *out_refs):
    i = pl.program_id(0)
    for k, out_ref in enumerate(out_refs):
        @pl.when(i == k)
        def _(out_ref=out_ref):
            out_ref[...] = dot(normed_ref[...], w_ref[...]).astype(BF16)


def line_kernel(
    y_ref, bc_ref, g_ref, enter_ref, gate_ref, gain_ref, e_ref, w_ref, after_ref,
    shares_ref, up_ref, down_ref, normed_ref, *, tiles,
):
    i = pl.program_id(0)

    @pl.when(i < tiles)
    def _():
        norm_tile(y_ref, bc_ref, g_ref, enter_ref, gate_ref, gain_ref, e_ref, normed_ref, i)

    @pl.when(i >= tiles)
    def _():
        shares_ref[0] = dot(normed_ref[...], w_ref[...]).astype(BF16)

    @pl.when(i == tiles)
    def _():
        down_ref[...] = shares_ref[0]

    @pl.when(i == pl.num_programs(0) - 1)
    def _():
        up_ref[...] = shares_ref[0]


def onward_kernel(where_ref, up_own_ref, down_own_ref, up_ref, down_ref, after_ref, up_out, down_out):
    up_out[...] = (up_own_ref[0].astype(F32) + up_ref[...].astype(F32)).astype(BF16)
    down_out[...] = (down_own_ref[0].astype(F32) + down_ref[...].astype(F32)).astype(BF16)


def final_kernel(where_ref, own_ref, up_ref, down_ref, *rest):
    out_ref = rest[-1]
    total = own_ref[0].astype(F32) + up_ref[...].astype(F32) + down_ref[...].astype(F32)
    out_ref[...] = total.astype(BF16)


def direct_final_kernel(*refs):
    *in_refs, after_ref, out_ref = refs
    total = in_refs[0][...].astype(F32)
    for ref in in_refs[1:]:
        total = total + ref[...].astype(F32)
    out_ref[...] = total.astype(BF16)


def params(limit=VMEM_LIMIT):
    return pltpu.CompilerParams(dimension_semantics=("arbitrary",), vmem_limit_bytes=limit)


def whole(shape):
    return pl.BlockSpec(shape, lambda *b: (0,) * len(shape))


def unread():
    return pl.BlockSpec(memory_space=pl.ANY)


def shaped(shape, dtype=BF16):
    return jax.ShapeDtypeStruct(shape, dtype)


def local(
    inner_input, state_maps, gate_input, step_input, log_decay_rate, step_bias,
    skip_gain, conv_kernel, map_kernel, norm_gain, out_weight,
):
    tokens, width = inner_input.shape
    groups = state_maps.shape[2]
    parts = 2 * groups
    heads = step_input.shape[1]
    blocks = tokens // BLK
    slabs = lax.axis_size("seq")
    chans = lax.axis_size("chan")
    features = out_weight.shape[1]
    map_width = parts * STATE
    low, high = spread(0, heads, width), spread(2 * heads, heads, width)

    tail = jnp.concatenate(
        [inner_input[tokens - HALO :], state_maps[tokens - HALO :].reshape(HALO, map_width)], 1
    )
    tail = lax.ppermute(tail, "seq", [(i, i + 1) for i in range(slabs - 1)])

    def lanes_at(count):
        return pl.BlockSpec((count, WIDE), lambda c: (0, c))

    xc, bc, bt, crow, cols, w_hl, g_hl, pay = pl.pallas_call(
        states_kernel,
        grid=(width // WIDE,),
        in_specs=[
            lanes_at(tokens),
            whole((tokens * parts, STATE)),
            whole((heads, tokens)),
            lanes_at(HALO),
            pl.BlockSpec((HALO, map_width), lambda c: (0, width // map_width)),
            whole((1, heads)),
            whole((1, heads)),
            lanes_at(4),
            whole((4 * parts, STATE)),
            lanes_at(LANES),
        ],
        out_specs=[
            lanes_at(tokens),
            whole((tokens, map_width)),
            whole((groups, STATE, tokens)),
            whole((heads, tokens)),
            whole((tokens, LANES)),
            whole((tokens, LANES)),
            whole((tokens, LANES)),
            whole((STATE, width + LANES)),
        ],
        out_shape=[
            shaped((tokens, width)),
            shaped((tokens, map_width)),
            shaped((groups, STATE, tokens)),
            shaped((heads, tokens), F32),
            shaped((tokens, LANES), F32),
            shaped((tokens, LANES)),
            shaped((tokens, LANES)),
            shaped((STATE, width + LANES)),
        ],
        scratch_shapes=[pltpu.VMEM((tokens, WIDE), BF16)],
        compiler_params=params(),
        name="states",
    )(
        inner_input, state_maps.reshape(tokens * parts, STATE), step_input.T, tail, tail,
        step_bias.reshape(1, heads), log_decay_rate.reshape(1, heads),
        conv_kernel, map_kernel.reshape(4 * parts, STATE), low,
    )

    part = STATE // slabs
    arrived = lax.all_to_all(
        pay.reshape(slabs, part, width + LANES), "seq", split_axis=0, concat_axis=0, tiled=True
    )

    def local_part(start, count, state, after):
        def tile(width):
            return pl.BlockSpec((BLK, width), lambda b: (start + b, 0))

        operands = [xc, bc, bt, crow, cols, w_hl, g_hl, skip_gain.reshape(1, heads), low, high]
        specs = [
            tile(width),
            tile(map_width),
            pl.BlockSpec((groups, STATE, BLK), lambda b: (0, 0, start + b)),
            pl.BlockSpec((heads, BLK), lambda b: (0, start + b)),
            tile(LANES),
            tile(LANES),
            tile(LANES),
            whole((1, heads)),
            whole((LANES, width)),
            whole((LANES, width)),
        ]
        if state is not None:
            operands.append(state)
            specs.append(whole((STATE, width)))
        operands.append(after)
        specs.append(unread())
        return pl.pallas_call(
            local_kernel,
            grid=(count,),
            in_specs=specs,
            out_specs=[
                pl.BlockSpec((BLK, width), lambda b: (b, 0)),
                whole((STATE, width)),
            ],
            out_shape=[shaped((count * BLK, width)), shaped((STATE, width), F32)],
            scratch_shapes=[pltpu.VMEM((HALO, width), F32)],
            compiler_params=params(),
            name="local_part",
        )(*operands)

    third = blocks - blocks * 3 // 8
    spans = [(0, blocks - third), (blocks - third, (third + 1) // 2)]
    spans.append((spans[1][0] + spans[1][1], third // 2))
    y_first, state = local_part(*spans[0], None, pay)
    y_second, state = local_part(*spans[1], state, y_first)

    entering = pl.pallas_call(
        prefix_kernel,
        out_shape=shaped((slabs, part, width)),
        in_specs=[
            pl.BlockSpec(memory_space=pltpu.VMEM),
            pl.BlockSpec(memory_space=pltpu.VMEM),
            unread(),
        ],
        out_specs=pl.BlockSpec(memory_space=pltpu.VMEM),
        compiler_params=pltpu.CompilerParams(vmem_limit_bytes=SMALL_LIMIT),
        name="prefix",
    )(arrived, high, y_first)
    entering = lax.all_to_all(entering, "seq", split_axis=0, concat_axis=0, tiled=True)
    entering = entering.reshape(STATE, width)

    part_out = features // chans
    norm_row = norm_gain.reshape(1, width)
    mine = lax.axis_index("chan").astype(jnp.int32)
    where = mine.reshape(1)

    def norm_operands(start, count, y):
        def tile(width, start=start):
            return pl.BlockSpec((BLK, width), lambda i, *_: (start + jnp.minimum(i, count - 1), 0))

        operands = [y, bc, g_hl, entering, gate_input, norm_row, high]
        specs = [
            tile(width, 0),
            tile(map_width),
            tile(LANES),
            whole((STATE, width)),
            tile(width),
            whole((1, width)),
            whole((LANES, width)),
        ]
        return operands, specs

    def project_direct(start, count, y, after, slots, more_slots):
        operands, specs = norm_operands(start, count, y)
        size = count * BLK

        def weights(slots, first):
            def index(i, where):
                step = i - first
                slot = slots[-1]
                for k in range(len(slots) - 1, -1, -1):
                    slot = jnp.where(step <= k, slots[k], slot)
                return (0, lax.rem(where[0] + slot, chans))

            return pl.BlockSpec((width, part_out), index)

        *shares, normed = pl.pallas_call(
            functools.partial(direct_kernel, tiles=count),
            grid_spec=pltpu.PrefetchScalarGridSpec(
                num_scalar_prefetch=1,
                grid=(count + len(slots),),
                in_specs=specs + [weights(slots, count), unread()],
                out_specs=[whole((size, part_out))] * len(slots) + [whole((size, width))],
            ),
            out_shape=[shaped((size, part_out))] * len(slots) + [shaped((size, width))],
            compiler_params=params(),
            name="project_direct",
        )(where, *operands, out_weight, after)
        more = pl.pallas_call(
            more_kernel,
            grid_spec=pltpu.PrefetchScalarGridSpec(
                num_scalar_prefetch=1,
                grid=(len(more_slots),),
                in_specs=[whole((size, width)), weights(more_slots, 0)],
                out_specs=[whole((size, part_out))] * len(more_slots),
            ),
            out_shape=[shaped((size, part_out))] * len(more_slots),
            compiler_params=params(),
            name="project_more",
        )(where, normed, out_weight)
        return dict(zip(slots + more_slots, shares + list(more)))

    def project_line(start, count, y, after):
        operands, specs = norm_operands(start, count, y)
        size = count * BLK

        def dest(i):
            return jnp.maximum(i - count, 0)

        return pl.pallas_call(
            functools.partial(line_kernel, tiles=count),
            grid=(count + chans,),
            in_specs=specs
            + [pl.BlockSpec((width, part_out), lambda i: (0, dest(i))), unread()],
            out_specs=[
                pl.BlockSpec((1, size, part_out), lambda i: (dest(i), 0, 0)),
                whole((size, part_out)),
                whole((size, part_out)),
            ],
            out_shape=[
                shaped((chans, size, part_out)),
                shaped((size, part_out)),
                shaped((size, part_out)),
            ],
            scratch_shapes=[pltpu.VMEM((size, width), BF16)],
            compiler_params=params(),
            name="project_line",
        )(*operands, out_weight, after)

    def permuted(up, down, s):
        up = lax.ppermute(up, "chan", [(a, a + 1) for a in range(s + 1)])
        down = lax.ppermute(down, "chan", [(a, a - 1) for a in range(chans - 1 - s, chans)])
        return up, down

    def onward(shares, up, down, s, after):
        def plain(i, where):
            return (i, 0)

        return pl.pallas_call(
            onward_kernel,
            grid_spec=pltpu.PrefetchScalarGridSpec(
                num_scalar_prefetch=1,
                grid=(shares.shape[1] // BLK,),
                in_specs=[
                    pl.BlockSpec(
                        (1, BLK, part_out),
                        lambda i, where: (jnp.minimum(chans - 1 - s + where[0], chans - 1), i, 0),
                    ),
                    pl.BlockSpec(
                        (1, BLK, part_out),
                        lambda i, where: (jnp.maximum(where[0] - (chans - 1) + s, 0), i, 0),
                    ),
                    pl.BlockSpec((BLK, part_out), plain),
                    pl.BlockSpec((BLK, part_out), plain),
                    unread(),
                ],
                out_specs=[pl.BlockSpec((BLK, part_out), plain)] * 2,
            ),
            out_shape=[shaped(up.shape)] * 2,
            compiler_params=params(SMALL_LIMIT),
            name="onward",
        )(where, shares, shares, up, down, after)

    def final(start, shares, up, down, out):
        def plain(i, where):
            return (i, 0)

        operands = [where, shares, up, down]
        in_specs = [
            pl.BlockSpec((1, BLK, part_out), lambda i, where: (where[0], i, 0)),
            pl.BlockSpec((BLK, part_out), plain),
            pl.BlockSpec((BLK, part_out), plain),
        ]
        aliases = {}
        if out is not None:
            aliases = {len(operands): 0}
            operands.append(out)
            in_specs.append(unread())
        return pl.pallas_call(
            final_kernel,
            grid_spec=pltpu.PrefetchScalarGridSpec(
                num_scalar_prefetch=1,
                grid=(shares.shape[1] // BLK,),
                in_specs=in_specs,
                out_specs=pl.BlockSpec((BLK, part_out), lambda i, where: (start + i, 0)),
            ),
            out_shape=shaped((tokens, part_out)),
            input_output_aliases=aliases,
            compiler_params=params(SMALL_LIMIT),
            name="final",
        )(*operands)

    order = sorted(range(chans), key=lambda k: (k == 0, -min(k, chans - k), k))
    slots = project_direct(
        *spans[0], y_first, y_second, order[: chans // 2], order[chans // 2 :]
    )
    pieces = [slots[0]]
    for k in order[:-1]:
        turn = [(a, (a + k) % chans) for a in range(chans)]
        pieces.append(lax.ppermute(slots[k], "chan", turn))

    chunks = [project_line(*spans[1], y_second, slots[0])]
    y_third, _ = local_part(*spans[2], state, chunks[0][0])
    chunks.append(project_line(*spans[2], y_third, chunks[0][0]))
    moving = [permuted(up, down, 0) for _, up, down in chunks]
    out = pl.pallas_call(
        direct_final_kernel,
        grid=(spans[0][1],),
        in_specs=[pl.BlockSpec((BLK, part_out), lambda i: (i, 0))] * chans + [unread()],
        out_specs=pl.BlockSpec((BLK, part_out), lambda i: (i, 0)),
        out_shape=shaped((tokens, part_out)),
        compiler_params=params(SMALL_LIMIT),
        name="direct_final",
    )(*pieces, chunks[1][0])
    after = out
    for s in range(1, chans - 1):
        for k in range(2):
            up, down = onward(chunks[k][0], *moving[k], s, after)
            after = up
            moving[k] = permuted(up, down, s)

    for k in range(2):
        out = final(spans[k + 1][0], chunks[k][0], *moving[k], out)
    return out


def solution(mesh):
    return jax.shard_map(
        local,
        mesh=mesh,
        in_specs=(
            P("seq", "chan"),
            P("seq", None, "chan", None),
            P("seq", "chan"),
            P("seq", "chan"),
            P("chan"),
            P("chan"),
            P("chan"),
            P(None, "chan"),
            P(None, None, "chan", None),
            P("chan"),
            P("chan", None),
        ),
        out_specs=P("seq", "chan"),
        check_vma=False,
    )
```

```python
import functools

import jax
import jax.numpy as jnp
import numpy as np
from jax import lax
from jax.experimental import pallas as pl
from jax.experimental.pallas import tpu as pltpu
from jax.sharding import PartitionSpec as P

HEAD_DIM = 64
STATE = 128
BLK = 128
LANES = 128
HALO = 8
ROWS = 16
WIDE = 256

step_limit = 0.5
epsilon = 1e-05
LOG2E = 1.4426950408889634
F32 = jnp.float32
BF16 = jnp.bfloat16
VMEM_LIMIT = 58 * 1024 * 1024
SMALL_LIMIT = 10 * 1024 * 1024


def silu(v):
    half = 0.5 * v
    return half + half * jnp.tanh(half)


def high_low(v):
    high = v.astype(BF16).astype(F32)
    return high, v - high


def spread(first_row, heads, width):
    result = np.zeros((LANES, width), np.float32)
    for k in range(2 * heads):
        h = k % heads
        result[first_row + k, h * HEAD_DIM : (h + 1) * HEAD_DIM] = 1.0
    return jnp.asarray(result, BF16)


def dot(a, b):
    return jnp.dot(a, b, preferred_element_type=F32)


def dot_t(a, b):
    return lax.dot_general(a, b, (((1,), (1,)), ((), ())), preferred_element_type=F32)


def column(row):
    count = row.shape[1]
    eye = lax.broadcasted_iota(jnp.int32, (count, count), 0) == lax.broadcasted_iota(
        jnp.int32, (count, count), 1
    )
    return jnp.sum(jnp.where(eye, row, 0.0), axis=1, keepdims=True)


def padded(pieces):
    rows = jnp.concatenate(pieces, 0)
    if rows.shape[0] == LANES:
        return rows
    return jnp.concatenate([rows, jnp.zeros((LANES - rows.shape[0], rows.shape[1]), rows.dtype)], 0)


def conv(before, cur, taps):
    full = jnp.concatenate([before, cur], 0)
    late = pltpu.roll(full, 1, 0)
    early = taps[1] * full + taps[0] * late
    acc = taps[3] * cur + taps[2] * late[HALO:] + pltpu.roll(early, 2, 0)[HALO:]
    return silu(acc).astype(BF16)


def states_kernel(
    x_ref, maps_ref, step_ref, tail_ref, mtail_ref, bias_ref, rate_ref, ck_ref, mk_ref, e_ref,
    xc_ref, bc_ref, bt_ref, crow_ref, cols_ref, w_ref, g_ref, pay_ref,
    weighted,
):
    c = pl.program_id(0)
    heads, tokens = step_ref.shape
    parts = mk_ref.shape[0] // 4
    groups = parts // 2
    blocks = tokens // BLK

    @pl.when(c == 0)
    def _():
        bias, rate = column(bias_ref[...]), -jnp.exp(column(rate_ref[...]))
        v = step_ref[...] + bias
        step = jnp.minimum(jnp.maximum(v, 0.0) + jnp.log1p(jnp.exp(-jnp.abs(v))), step_limit)
        log_step = rate * step
        first, rest = high_low(log_step)
        second, third = high_low(rest)
        pieces = []
        for b in range(blocks):
            at = slice(b * BLK, (b + 1) * BLK)
            pieces += [first[:, at], second[:, at], third[:, at]]
        row = lax.broadcasted_iota(jnp.int32, (BLK, BLK), 0)
        col = lax.broadcasted_iota(jnp.int32, (BLK, BLK), 1)
        tri = jnp.where(row <= col, 1.0, 0.0).astype(BF16)
        sums = dot(jnp.concatenate(pieces, 0).astype(BF16), tri)
        cums, leads = [], [jnp.zeros((heads, 1), F32)]
        for b in range(blocks):
            at = 3 * b * heads
            cum = (
                sums[at : at + heads]
                + sums[at + heads : at + 2 * heads]
                + sums[at + 2 * heads : at + 3 * heads]
            )
            cums.append(cum)
            leads.append(leads[-1] + cum[:, BLK - 1 : BLK])
        last = None
        for b in range(blocks):
            at = slice(b * BLK, (b + 1) * BLK)
            cum, step_b = cums[b], step[:, at]
            total = cum[:, BLK - 1 : BLK]
            block_weight = jnp.exp(total - cum) * step_b
            slab_weight = jnp.exp(leads[blocks] - (leads[b] + cum)) * step_b
            grown = jnp.exp(cum)
            entered = jnp.exp(cum + leads[b])
            crow_ref[:, at] = (cum - jnp.log(step_b)) * LOG2E
            w_ref[at, :] = padded(high_low(slab_weight) + high_low(block_weight)).T.astype(BF16)
            last = padded(high_low(grown) + high_low(entered)).T
            g_ref[at, :] = last.astype(BF16)
            cols_ref[at, :] = padded((cum * LOG2E,)).T
        pay_ref[:, heads * HEAD_DIM :] = jnp.broadcast_to(last[BLK - 1 :], (STATE, LANES)).astype(BF16)

        row = lax.broadcasted_iota(jnp.int32, (BLK * parts, BLK * parts), 0)
        col = lax.broadcasted_iota(jnp.int32, (BLK * parts, BLK * parts), 1)
        source = (row & (BLK - 1)) * parts + row // BLK
        pick = jnp.where(col == source, 1.0, 0.0).astype(BF16)
        before = [mtail_ref[:, q * STATE : (q + 1) * STATE].astype(F32) for q in range(parts)]
        for b in range(blocks):
            ordered = dot(pick, maps_ref[b * BLK * parts : (b + 1) * BLK * parts, :])
            for q in range(parts):
                cur = ordered[q * BLK : (q + 1) * BLK]
                taps = [mk_ref[k * parts + q : k * parts + q + 1] for k in range(4)]
                result = conv(before[q], cur, taps)
                before[q] = cur[BLK - HALO :]
                bc_ref[b * BLK : (b + 1) * BLK, q * STATE : (q + 1) * STATE] = result
                if q < groups:
                    bt_ref[q, :, b * BLK : (b + 1) * BLK] = result.astype(F32).T.astype(BF16)

    for lane in range(0, x_ref.shape[1], LANES):
        at_lanes = slice(lane, lane + LANES)
        taps = [ck_ref[k : k + 1, at_lanes] for k in range(4)]
        before = tail_ref[:, at_lanes].astype(F32)
        for b in range(blocks):
            at = slice(b * BLK, (b + 1) * BLK)
            cur = x_ref[at, at_lanes].astype(F32)
            result = conv(before, cur, taps)
            before = cur[BLK - HALO :]
            xc_ref[at, at_lanes] = result
            scale = dot(w_ref[at, :], e_ref[:, at_lanes])
            weighted[at, at_lanes] = (result.astype(F32) * scale).astype(BF16)
    step_width = x_ref.shape[1]
    group = c * step_width * groups // (heads * HEAD_DIM)
    at = pl.ds(pl.multiple_of(c * step_width, step_width), step_width)
    pay_ref[:, at] = dot(bt_ref[group], weighted[...]).astype(BF16)


def local_kernel(
    xc_ref, bc_ref, bt_ref, crow_ref, cols_ref, w_ref, g_ref, skip_ref, low_ref, high_ref, *rest
):
    y_ref, state, gain_ref = rest[-3:]
    heads = crow_ref.shape[0]
    width = xc_ref.shape[1]
    groups = bt_ref.shape[0]
    gw = width // groups

    @pl.when(pl.program_id(0) == 0)
    def _():
        state[...] = rest[0][...] if len(rest) > 4 else jnp.zeros_like(state)
        skip = jnp.concatenate(high_low(skip_ref[...]), 1)
        skip = jnp.concatenate([skip, jnp.zeros((1, LANES - 2 * heads), F32)], 1)
        gain_ref[...] = dot(jnp.broadcast_to(skip, (HALO, LANES)).astype(BF16), low_ref[...])

    left = lax.broadcasted_iota(jnp.int32, (BLK, LANES), 1) < HEAD_DIM
    row = lax.broadcasted_iota(jnp.int32, (BLK, BLK), 0)
    causal = row >= lax.broadcasted_iota(jnp.int32, (BLK, BLK), 1)
    for g in range(groups):
        b_g = bc_ref[:, g * STATE : (g + 1) * STATE]
        c_g = bc_ref[:, (groups + g) * STATE : (groups + g + 1) * STATE]
        scores = jnp.where(causal, dot_t(c_g, b_g), 0.0)
        for wide in range(g * gw, (g + 1) * gw, 2 * LANES):
            at_wide = slice(wide, wide + 2 * LANES)
            grown = dot(g_ref[...], low_ref[:, at_wide])
            before = state[:, at_wide]
            carry = grown * dot(c_g, before.astype(BF16))
            x_wide = xc_ref[:, at_wide].astype(F32)
            weighted = (x_wide * dot(w_ref[...], high_ref[:, at_wide])).astype(BF16)
            state[:, at_wide] = grown[BLK - 1 :] * before + dot(bt_ref[g], weighted)
            carry = carry + gain_ref[0:1, at_wide] * x_wide
            for k in range(2):
                at = slice(wide + k * LANES, wide + (k + 1) * LANES)
                mixing = []
                for h in (at.start // HEAD_DIM, at.start // HEAD_DIM + 1):
                    gap = jnp.minimum(cols_ref[:, h : h + 1] - crow_ref[h : h + 1], 0.0)
                    mixing.append((jnp.exp2(gap) * scores).astype(BF16))
                x = xc_ref[:, at]
                nil = jnp.zeros_like(x)
                stacked = jnp.concatenate([jnp.where(left, x, nil), jnp.where(left, nil, x)], 0)
                y = dot(jnp.concatenate(mixing, 1), stacked) + carry[:, k * LANES : (k + 1) * LANES]
                y_ref[:, at] = y.astype(BF16)


def prefix_kernel(pay_ref, e_ref, after_ref, out_ref):
    width = out_ref.shape[2]
    decays = dot(pay_ref[:, 0, width:], e_ref[...])
    running = jnp.zeros(out_ref.shape[1:], F32)
    for slab in range(out_ref.shape[0]):
        out_ref[slab] = running.astype(BF16)
        running = decays[slab : slab + 1] * running + pay_ref[slab, :, :width].astype(F32)


def norm_tile(
    y_ref, bc_ref, g_ref, enter_ref, gate_ref, gain_ref, e_ref, normed_ref, carry, grown, i
):
    width = y_ref.shape[1]
    groups = bc_ref.shape[1] // (2 * STATE)
    gw = width // groups
    grown[...] = dot(g_ref[...], e_ref[...])
    for g in range(groups):
        at = slice(g * gw, (g + 1) * gw)
        carry[:, at] = dot(bc_ref[:, (groups + g) * STATE : (groups + g + 1) * STATE], enter_ref[:, at])
    for r in range(0, BLK, ROWS):
        rows = slice(r, r + ROWS)
        out_rows = pl.ds(pl.multiple_of(i * BLK + r, ROWS), ROWS)
        for g in range(groups):
            at = slice(g * gw, (g + 1) * gw)
            y = y_ref[rows, at].astype(F32) + grown[rows, at] * carry[rows, at]
            gated = y * silu(gate_ref[rows, at].astype(F32))
            square_mean = jnp.mean(gated * gated, axis=-1, keepdims=True)
            scaled = gated * lax.rsqrt(square_mean + epsilon) * gain_ref[:, at]
            normed_ref[out_rows, at] = scaled.astype(BF16)


def direct_kernel(
    where_ref, y_ref, bc_ref, g_ref, enter_ref, gate_ref, gain_ref, e_ref, w_ref, after_ref,
    *rest, tiles,
):
    *out_refs, normed_ref, carry, grown = rest
    i = pl.program_id(0)

    @pl.when(i < tiles)
    def _():
        norm_tile(
            y_ref, bc_ref, g_ref, enter_ref, gate_ref, gain_ref, e_ref, normed_ref, carry, grown, i
        )

    for k, out_ref in enumerate(out_refs):
        @pl.when(i == tiles + k)
        def _(out_ref=out_ref):
            out_ref[...] = dot(normed_ref[...], w_ref[...]).astype(BF16)


def line_kernel(
    y_ref, bc_ref, g_ref, enter_ref, gate_ref, gain_ref, e_ref, w_ref, after_ref,
    shares_ref, up_ref, down_ref, normed_ref, carry, grown, *, tiles,
):
    i = pl.program_id(0)

    @pl.when(i < tiles)
    def _():
        norm_tile(
            y_ref, bc_ref, g_ref, enter_ref, gate_ref, gain_ref, e_ref, normed_ref, carry, grown, i
        )

    @pl.when(i >= tiles)
    def _():
        shares_ref[0] = dot(normed_ref[...], w_ref[...]).astype(BF16)

    @pl.when(i == tiles)
    def _():
        down_ref[...] = shares_ref[0]

    @pl.when(i == pl.num_programs(0) - 1)
    def _():
        up_ref[...] = shares_ref[0]


def onward_kernel(where_ref, up_own_ref, down_own_ref, up_ref, down_ref, after_ref, up_out, down_out):
    up_out[...] = (up_own_ref[0].astype(F32) + up_ref[...].astype(F32)).astype(BF16)
    down_out[...] = (down_own_ref[0].astype(F32) + down_ref[...].astype(F32)).astype(BF16)


def final_kernel(where_ref, own_ref, up_ref, down_ref, *rest):
    out_ref = rest[-1]
    total = own_ref[0].astype(F32) + up_ref[...].astype(F32) + down_ref[...].astype(F32)
    out_ref[...] = total.astype(BF16)


def place_kernel(piece_ref, out_before_ref, out_ref):
    out_ref[...] = piece_ref[...]


def direct_final_kernel(where_ref, normed_ref, w_ref, *refs, count):
    out_ref = refs[-1]
    total = dot(normed_ref[...], w_ref[...])
    for ref in refs[:count]:
        total = total + ref[...].astype(F32)
    out_ref[...] = total.astype(BF16)


def params(limit=VMEM_LIMIT):
    return pltpu.CompilerParams(dimension_semantics=("arbitrary",), vmem_limit_bytes=limit)


def whole(shape):
    return pl.BlockSpec(shape, lambda *b: (0,) * len(shape))


def unread():
    return pl.BlockSpec(memory_space=pl.ANY)


def shaped(shape, dtype=BF16):
    return jax.ShapeDtypeStruct(shape, dtype)


def local(
    inner_input, state_maps, gate_input, step_input, log_decay_rate, step_bias,
    skip_gain, conv_kernel, map_kernel, norm_gain, out_weight,
):
    tokens, width = inner_input.shape
    groups = state_maps.shape[2]
    parts = 2 * groups
    heads = step_input.shape[1]
    blocks = tokens // BLK
    slabs = lax.axis_size("seq")
    chans = lax.axis_size("chan")
    features = out_weight.shape[1]
    map_width = parts * STATE
    low, high = spread(0, heads, width), spread(2 * heads, heads, width)

    tail = jnp.concatenate(
        [inner_input[tokens - HALO :], state_maps[tokens - HALO :].reshape(HALO, map_width)], 1
    )
    tail = lax.ppermute(tail, "seq", [(i, i + 1) for i in range(slabs - 1)])

    def lanes_at(count):
        return pl.BlockSpec((count, WIDE), lambda c: (0, c))

    xc, bc, bt, crow, cols, w_hl, g_hl, pay = pl.pallas_call(
        states_kernel,
        grid=(width // WIDE,),
        in_specs=[
            lanes_at(tokens),
            whole((tokens * parts, STATE)),
            whole((heads, tokens)),
            lanes_at(HALO),
            pl.BlockSpec((HALO, map_width), lambda c: (0, width // map_width)),
            whole((1, heads)),
            whole((1, heads)),
            lanes_at(4),
            whole((4 * parts, STATE)),
            lanes_at(LANES),
        ],
        out_specs=[
            lanes_at(tokens),
            whole((tokens, map_width)),
            whole((groups, STATE, tokens)),
            whole((heads, tokens)),
            whole((tokens, LANES)),
            whole((tokens, LANES)),
            whole((tokens, LANES)),
            whole((STATE, width + LANES)),
        ],
        out_shape=[
            shaped((tokens, width)),
            shaped((tokens, map_width)),
            shaped((groups, STATE, tokens)),
            shaped((heads, tokens), F32),
            shaped((tokens, LANES), F32),
            shaped((tokens, LANES)),
            shaped((tokens, LANES)),
            shaped((STATE, width + LANES)),
        ],
        scratch_shapes=[pltpu.VMEM((tokens, WIDE), BF16)],
        compiler_params=params(),
        name="states",
    )(
        inner_input, state_maps.reshape(tokens * parts, STATE), step_input.T, tail, tail,
        step_bias.reshape(1, heads), log_decay_rate.reshape(1, heads),
        conv_kernel, map_kernel.reshape(4 * parts, STATE), low,
    )

    part = STATE // slabs
    arrived = lax.all_to_all(
        pay.reshape(slabs, part, width + LANES), "seq", split_axis=0, concat_axis=0, tiled=True
    )

    def local_part(start, count, before, after):
        def tile(width):
            return pl.BlockSpec((BLK, width), lambda b: (start + b, 0))

        operands = [xc, bc, bt, crow, cols, w_hl, g_hl, skip_gain.reshape(1, heads), low, high]
        specs = [
            tile(width),
            tile(map_width),
            pl.BlockSpec((groups, STATE, BLK), lambda b: (0, 0, start + b)),
            pl.BlockSpec((heads, BLK), lambda b: (0, start + b)),
            tile(LANES),
            tile(LANES),
            tile(LANES),
            whole((1, heads)),
            whole((LANES, width)),
            whole((LANES, width)),
        ]
        aliases = {}
        if before is not None:
            y, state = before
            aliases = {len(operands) + 1: 0}
            operands += [state, y]
            specs += [whole((STATE, width)), unread()]
        operands.append(after)
        specs.append(unread())
        return pl.pallas_call(
            local_kernel,
            grid=(count,),
            in_specs=specs,
            out_specs=[tile(width), whole((STATE, width))],
            out_shape=[shaped((tokens, width)), shaped((STATE, width), F32)],
            input_output_aliases=aliases,
            scratch_shapes=[pltpu.VMEM((HALO, width), F32)],
            compiler_params=params(),
            name="local_part",
        )(*operands)

    some = (blocks * 3 + 7) // 8
    y_first = local_part(0, some, None, pay)
    entering = pl.pallas_call(
        prefix_kernel,
        out_shape=shaped((slabs, part, width)),
        in_specs=[
            pl.BlockSpec(memory_space=pltpu.VMEM),
            pl.BlockSpec(memory_space=pltpu.VMEM),
            unread(),
        ],
        out_specs=pl.BlockSpec(memory_space=pltpu.VMEM),
        compiler_params=pltpu.CompilerParams(vmem_limit_bytes=SMALL_LIMIT),
        name="prefix",
    )(arrived, high, y_first[1])
    y_second = local_part(some, some, y_first, entering)
    entering = lax.all_to_all(entering, "seq", split_axis=0, concat_axis=0, tiled=True)
    entering = entering.reshape(STATE, width)

    part_out = features // chans
    norm_row = norm_gain.reshape(1, width)
    mine = lax.axis_index("chan").astype(jnp.int32)
    where = mine.reshape(1)

    def norm_operands(start, count, y):
        def tile(width):
            return pl.BlockSpec((BLK, width), lambda i, *_: (start + jnp.minimum(i, count - 1), 0))

        operands = [y, bc, g_hl, entering, gate_input, norm_row, high]
        specs = [
            tile(width),
            tile(map_width),
            tile(LANES),
            whole((STATE, width)),
            tile(width),
            whole((1, width)),
            whole((LANES, width)),
        ]
        return operands, specs

    def project_direct(start, count, y, after, slots):
        operands, specs = norm_operands(start, count, y)
        size = count * BLK

        def weights(i, where):
            step = i - count
            slot = slots[-1]
            for k in range(len(slots) - 1, -1, -1):
                slot = jnp.where(step <= k, slots[k], slot)
            return (0, lax.rem(where[0] + slot, chans))

        return pl.pallas_call(
            functools.partial(direct_kernel, tiles=count),
            grid_spec=pltpu.PrefetchScalarGridSpec(
                num_scalar_prefetch=1,
                grid=(count + len(slots),),
                in_specs=specs + [pl.BlockSpec((width, part_out), weights), unread()],
                out_specs=[whole((size, part_out))] * len(slots) + [whole((size, width))],
                scratch_shapes=[pltpu.VMEM((BLK, width), F32)] * 2,
            ),
            out_shape=[shaped((size, part_out))] * len(slots) + [shaped((size, width))],
            compiler_params=params(),
            name="project_direct",
        )(where, *operands, out_weight, after)

    def direct_final(start, normed, pieces, out, after):
        def tile(width, start=0):
            return pl.BlockSpec((BLK, width), lambda i, where: (start + i, 0))

        operands = [where, normed, out_weight] + pieces + [after]
        specs = [
            tile(width),
            pl.BlockSpec((width, part_out), lambda i, where: (0, where[0])),
        ]
        specs += [tile(part_out)] * len(pieces) + [unread()]
        aliases = {}
        if out is not None:
            aliases = {len(operands): 0}
            operands.append(out)
            specs.append(unread())
        return pl.pallas_call(
            functools.partial(direct_final_kernel, count=len(pieces)),
            grid_spec=pltpu.PrefetchScalarGridSpec(
                num_scalar_prefetch=1,
                grid=(normed.shape[0] // BLK,),
                in_specs=specs,
                out_specs=tile(part_out, start),
            ),
            out_shape=shaped((tokens, part_out)),
            input_output_aliases=aliases,
            compiler_params=params(SMALL_LIMIT),
            name="direct_final",
        )(*operands)

    def project_line(start, count, y, after):
        operands, specs = norm_operands(start, count, y)
        size = count * BLK

        def dest(i):
            return jnp.maximum(i - count, 0)

        return pl.pallas_call(
            functools.partial(line_kernel, tiles=count),
            grid=(count + chans,),
            in_specs=specs
            + [pl.BlockSpec((width, part_out), lambda i: (0, dest(i))), unread()],
            out_specs=[
                pl.BlockSpec((1, size, part_out), lambda i: (dest(i), 0, 0)),
                whole((size, part_out)),
                whole((size, part_out)),
            ],
            out_shape=[
                shaped((chans, size, part_out)),
                shaped((size, part_out)),
                shaped((size, part_out)),
            ],
            scratch_shapes=[pltpu.VMEM((size, width), BF16)] + [pltpu.VMEM((BLK, width), F32)] * 2,
            compiler_params=params(),
            name="project_line",
        )(*operands, out_weight, after)

    def permuted(up, down, s):
        up = lax.ppermute(up, "chan", [(a, a + 1) for a in range(s + 1)])
        down = lax.ppermute(down, "chan", [(a, a - 1) for a in range(chans - 1 - s, chans)])
        return up, down

    def onward(shares, up, down, s, after):
        def plain(i, where):
            return (i, 0)

        return pl.pallas_call(
            onward_kernel,
            grid_spec=pltpu.PrefetchScalarGridSpec(
                num_scalar_prefetch=1,
                grid=(shares.shape[1] // BLK,),
                in_specs=[
                    pl.BlockSpec(
                        (1, BLK, part_out),
                        lambda i, where: (jnp.minimum(chans - 1 - s + where[0], chans - 1), i, 0),
                    ),
                    pl.BlockSpec(
                        (1, BLK, part_out),
                        lambda i, where: (jnp.maximum(where[0] - (chans - 1) + s, 0), i, 0),
                    ),
                    pl.BlockSpec((BLK, part_out), plain),
                    pl.BlockSpec((BLK, part_out), plain),
                    unread(),
                ],
                out_specs=[pl.BlockSpec((BLK, part_out), plain)] * 2,
            ),
            out_shape=[shaped(up.shape)] * 2,
            compiler_params=params(SMALL_LIMIT),
            name="onward",
        )(where, shares, shares, up, down, after)

    def final(start, shares, up, down, out):
        def plain(i, where):
            return (i, 0)

        operands = [where, shares, up, down]
        in_specs = [
            pl.BlockSpec((1, BLK, part_out), lambda i, where: (where[0], i, 0)),
            pl.BlockSpec((BLK, part_out), plain),
            pl.BlockSpec((BLK, part_out), plain),
        ]
        aliases = {}
        if out is not None:
            aliases = {len(operands): 0}
            operands.append(out)
            in_specs.append(unread())
        return pl.pallas_call(
            final_kernel,
            grid_spec=pltpu.PrefetchScalarGridSpec(
                num_scalar_prefetch=1,
                grid=(shares.shape[1] // BLK,),
                in_specs=in_specs,
                out_specs=pl.BlockSpec((BLK, part_out), lambda i, where: (start + i, 0)),
            ),
            out_shape=shaped((tokens, part_out)),
            input_output_aliases=aliases,
            compiler_params=params(SMALL_LIMIT),
            name="final",
        )(*operands)

    quarter = blocks // 4
    order = sorted(range(1, chans), key=lambda k: (-min(k, chans - k), k))
    *slots, normed = project_direct(0, quarter, y_second[0], y_second[1], order)
    pieces = []
    for k, slot in zip(order, slots):
        turn = [(a, (a + k) % chans) for a in range(chans)]
        pieces.append(lax.ppermute(slot, "chan", turn))

    shares, _, _ = project_line(quarter, quarter, y_second[0], normed)
    scattered = lax.psum_scatter(shares, "chan", scatter_dimension=0, tiled=True)

    starts = (2 * quarter, 3 * quarter)
    chunks = [project_line(starts[0], quarter, y_second[0], shares)]
    y_third = local_part(2 * some, blocks - 2 * some, y_second, chunks[0][0])
    chunks.append(project_line(starts[1], quarter, y_third[0], chunks[0][0]))
    moving = [permuted(up, down, 0) for _, up, down in chunks]
    out = direct_final(0, normed, pieces, None, chunks[1][0])
    after = out
    for s in range(1, chans - 1):
        for k in range(2):
            up, down = onward(chunks[k][0], *moving[k], s, after)
            after = up
            moving[k] = permuted(up, down, s)
    out = pl.pallas_call(
        place_kernel,
        grid=(quarter,),
        in_specs=[pl.BlockSpec((BLK, part_out), lambda i: (i, 0)), unread()],
        out_specs=pl.BlockSpec((BLK, part_out), lambda i: (quarter + i, 0)),
        out_shape=shaped((tokens, part_out)),
        input_output_aliases={1: 0},
        compiler_params=params(SMALL_LIMIT),
        name="place",
    )(scattered.reshape(quarter * BLK, part_out), out)
    for k in range(2):
        out = final(starts[k], chunks[k][0], *moving[k], out)
    return out


def solution(mesh):
    return jax.shard_map(
        local,
        mesh=mesh,
        in_specs=(
            P("seq", "chan"),
            P("seq", None, "chan", None),
            P("seq", "chan"),
            P("seq", "chan"),
            P("chan"),
            P("chan"),
            P("chan"),
            P(None, "chan"),
            P(None, None, "chan", None),
            P("chan"),
            P("chan", None),
        ),
        out_specs=P("seq", "chan"),
        check_vma=False,
    )
```

```python
import functools

import jax
import jax.numpy as jnp
import numpy as np
from jax import lax
from jax.experimental import pallas as pl
from jax.experimental.pallas import tpu as pltpu
from jax.sharding import PartitionSpec as P

HEAD_DIM = 64
STATE = 128
BLK = 128
LANES = 128
HALO = 8
ROWS = 16
WIDE = 256

step_limit = 0.5
epsilon = 1e-05
LOG2E = 1.4426950408889634
F32 = jnp.float32
BF16 = jnp.bfloat16
VMEM_LIMIT = 58 * 1024 * 1024
SMALL_LIMIT = 10 * 1024 * 1024


def silu(v):
    half = 0.5 * v
    return half + half * jnp.tanh(half)


def high_low(v):
    high = v.astype(BF16).astype(F32)
    return high, v - high


def spread(first_row, heads, width):
    result = np.zeros((LANES, width), np.float32)
    for k in range(2 * heads):
        h = k % heads
        result[first_row + k, h * HEAD_DIM : (h + 1) * HEAD_DIM] = 1.0
    return jnp.asarray(result, BF16)


def dot(a, b):
    return jnp.dot(a, b, preferred_element_type=F32)


def dot_t(a, b):
    return lax.dot_general(a, b, (((1,), (1,)), ((), ())), preferred_element_type=F32)


def column(row):
    count = row.shape[1]
    eye = lax.broadcasted_iota(jnp.int32, (count, count), 0) == lax.broadcasted_iota(
        jnp.int32, (count, count), 1
    )
    return jnp.sum(jnp.where(eye, row, 0.0), axis=1, keepdims=True)


def padded(pieces):
    rows = jnp.concatenate(pieces, 0)
    if rows.shape[0] == LANES:
        return rows
    return jnp.concatenate([rows, jnp.zeros((LANES - rows.shape[0], rows.shape[1]), rows.dtype)], 0)


def conv(before, cur, taps):
    full = jnp.concatenate([before, cur], 0)
    late = pltpu.roll(full, 1, 0)
    early = taps[1] * full + taps[0] * late
    acc = taps[3] * cur + taps[2] * late[HALO:] + pltpu.roll(early, 2, 0)[HALO:]
    return silu(acc).astype(BF16)


def states_kernel(
    x_ref, maps_ref, step_ref, tail_ref, mtail_ref, bias_ref, rate_ref, ck_ref, mk_ref, e_ref,
    xc_ref, bc_ref, bt_ref, crow_ref, cols_ref, w_ref, g_ref, pay_ref,
    weighted,
):
    c = pl.program_id(0)
    heads, tokens = step_ref.shape
    parts = mk_ref.shape[0] // 4
    groups = parts // 2
    blocks = tokens // BLK

    @pl.when(c == 0)
    def _():
        bias, rate = column(bias_ref[...]), -jnp.exp(column(rate_ref[...]))
        v = step_ref[...] + bias
        step = jnp.minimum(jnp.maximum(v, 0.0) + jnp.log1p(jnp.exp(-jnp.abs(v))), step_limit)
        log_step = rate * step
        first, rest = high_low(log_step)
        second, third = high_low(rest)
        pieces = []
        for b in range(blocks):
            at = slice(b * BLK, (b + 1) * BLK)
            pieces += [first[:, at], second[:, at], third[:, at]]
        row = lax.broadcasted_iota(jnp.int32, (BLK, BLK), 0)
        col = lax.broadcasted_iota(jnp.int32, (BLK, BLK), 1)
        tri = jnp.where(row <= col, 1.0, 0.0).astype(BF16)
        sums = dot(jnp.concatenate(pieces, 0).astype(BF16), tri)
        cums, leads = [], [jnp.zeros((heads, 1), F32)]
        for b in range(blocks):
            at = 3 * b * heads
            cum = (
                sums[at : at + heads]
                + sums[at + heads : at + 2 * heads]
                + sums[at + 2 * heads : at + 3 * heads]
            )
            cums.append(cum)
            leads.append(leads[-1] + cum[:, BLK - 1 : BLK])
        last = None
        for b in range(blocks):
            at = slice(b * BLK, (b + 1) * BLK)
            cum, step_b = cums[b], step[:, at]
            total = cum[:, BLK - 1 : BLK]
            block_weight = jnp.exp(total - cum) * step_b
            slab_weight = jnp.exp(leads[blocks] - (leads[b] + cum)) * step_b
            grown = jnp.exp(cum)
            entered = jnp.exp(cum + leads[b])
            crow_ref[:, at] = (cum - jnp.log(step_b)) * LOG2E
            w_ref[at, :] = padded(high_low(slab_weight) + high_low(block_weight)).T.astype(BF16)
            last = padded(high_low(grown) + high_low(entered)).T
            g_ref[at, :] = last.astype(BF16)
            cols_ref[at, :] = padded((cum * LOG2E,)).T
        pay_ref[:, heads * HEAD_DIM :] = jnp.broadcast_to(last[BLK - 1 :], (STATE, LANES)).astype(BF16)

        row = lax.broadcasted_iota(jnp.int32, (BLK * parts, BLK * parts), 0)
        col = lax.broadcasted_iota(jnp.int32, (BLK * parts, BLK * parts), 1)
        source = (row & (BLK - 1)) * parts + row // BLK
        pick = jnp.where(col == source, 1.0, 0.0).astype(BF16)
        before = [mtail_ref[:, q * STATE : (q + 1) * STATE].astype(F32) for q in range(parts)]
        for b in range(blocks):
            ordered = dot(pick, maps_ref[b * BLK * parts : (b + 1) * BLK * parts, :])
            for q in range(parts):
                cur = ordered[q * BLK : (q + 1) * BLK]
                taps = [mk_ref[k * parts + q : k * parts + q + 1] for k in range(4)]
                result = conv(before[q], cur, taps)
                before[q] = cur[BLK - HALO :]
                bc_ref[b * BLK : (b + 1) * BLK, q * STATE : (q + 1) * STATE] = result
                if q < groups:
                    bt_ref[q, :, b * BLK : (b + 1) * BLK] = result.astype(F32).T.astype(BF16)

    for lane in range(0, x_ref.shape[1], LANES):
        at_lanes = slice(lane, lane + LANES)
        taps = [ck_ref[k : k + 1, at_lanes] for k in range(4)]
        before = tail_ref[:, at_lanes].astype(F32)
        for b in range(blocks):
            at = slice(b * BLK, (b + 1) * BLK)
            cur = x_ref[at, at_lanes].astype(F32)
            result = conv(before, cur, taps)
            before = cur[BLK - HALO :]
            xc_ref[at, at_lanes] = result
            scale = dot(w_ref[at, :], e_ref[:, at_lanes])
            weighted[at, at_lanes] = (result.astype(F32) * scale).astype(BF16)
    step_width = x_ref.shape[1]
    group = c * step_width * groups // (heads * HEAD_DIM)
    at = pl.ds(pl.multiple_of(c * step_width, step_width), step_width)
    pay_ref[:, at] = dot(bt_ref[group], weighted[...]).astype(BF16)


def local_kernel(
    xc_ref, bc_ref, bt_ref, crow_ref, cols_ref, w_ref, g_ref, skip_ref, low_ref, high_ref, *rest
):
    y_ref, state, gain_ref = rest[-3:]
    heads = crow_ref.shape[0]
    width = xc_ref.shape[1]
    groups = bt_ref.shape[0]
    gw = width // groups

    @pl.when(pl.program_id(0) == 0)
    def _():
        state[...] = rest[0][...] if len(rest) > 4 else jnp.zeros_like(state)
        skip = jnp.concatenate(high_low(skip_ref[...]), 1)
        skip = jnp.concatenate([skip, jnp.zeros((1, LANES - 2 * heads), F32)], 1)
        gain_ref[...] = dot(jnp.broadcast_to(skip, (HALO, LANES)).astype(BF16), low_ref[...])

    left = lax.broadcasted_iota(jnp.int32, (BLK, LANES), 1) < HEAD_DIM
    row = lax.broadcasted_iota(jnp.int32, (BLK, BLK), 0)
    causal = row >= lax.broadcasted_iota(jnp.int32, (BLK, BLK), 1)
    for g in range(groups):
        b_g = bc_ref[:, g * STATE : (g + 1) * STATE]
        c_g = bc_ref[:, (groups + g) * STATE : (groups + g + 1) * STATE]
        scores = jnp.where(causal, dot_t(c_g, b_g), 0.0)
        for wide in range(g * gw, (g + 1) * gw, 2 * LANES):
            at_wide = slice(wide, wide + 2 * LANES)
            grown = dot(g_ref[...], low_ref[:, at_wide])
            before = state[:, at_wide]
            carry = grown * dot(c_g, before.astype(BF16))
            x_wide = xc_ref[:, at_wide].astype(F32)
            weighted = (x_wide * dot(w_ref[...], high_ref[:, at_wide])).astype(BF16)
            state[:, at_wide] = grown[BLK - 1 :] * before + dot(bt_ref[g], weighted)
            carry = carry + gain_ref[0:1, at_wide] * x_wide
            for k in range(2):
                at = slice(wide + k * LANES, wide + (k + 1) * LANES)
                mixing = []
                for h in (at.start // HEAD_DIM, at.start // HEAD_DIM + 1):
                    gap = jnp.minimum(cols_ref[:, h : h + 1] - crow_ref[h : h + 1], 0.0)
                    mixing.append((jnp.exp2(gap) * scores).astype(BF16))
                x = xc_ref[:, at]
                nil = jnp.zeros_like(x)
                stacked = jnp.concatenate([jnp.where(left, x, nil), jnp.where(left, nil, x)], 0)
                y = dot(jnp.concatenate(mixing, 1), stacked) + carry[:, k * LANES : (k + 1) * LANES]
                y_ref[:, at] = y.astype(BF16)


def prefix_kernel(pay_ref, e_ref, after_ref, out_ref):
    width = out_ref.shape[2]
    decays = dot(pay_ref[:, 0, width:], e_ref[...])
    running = jnp.zeros(out_ref.shape[1:], F32)
    for slab in range(out_ref.shape[0]):
        out_ref[slab] = running.astype(BF16)
        running = decays[slab : slab + 1] * running + pay_ref[slab, :, :width].astype(F32)


def norm_tile(
    y_ref, bc_ref, g_ref, enter_ref, gate_ref, gain_ref, e_ref, normed_ref, carry, grown, i
):
    width = y_ref.shape[1]
    groups = bc_ref.shape[1] // (2 * STATE)
    gw = width // groups
    grown[...] = dot(g_ref[...], e_ref[...])
    for g in range(groups):
        at = slice(g * gw, (g + 1) * gw)
        carry[:, at] = dot(bc_ref[:, (groups + g) * STATE : (groups + g + 1) * STATE], enter_ref[:, at])
    for r in range(0, BLK, ROWS):
        rows = slice(r, r + ROWS)
        out_rows = pl.ds(pl.multiple_of(i * BLK + r, ROWS), ROWS)
        for g in range(groups):
            at = slice(g * gw, (g + 1) * gw)
            y = y_ref[rows, at].astype(F32) + grown[rows, at] * carry[rows, at]
            gated = y * silu(gate_ref[rows, at].astype(F32))
            square_mean = jnp.mean(gated * gated, axis=-1, keepdims=True)
            scaled = gated * lax.rsqrt(square_mean + epsilon) * gain_ref[:, at]
            normed_ref[out_rows, at] = scaled.astype(BF16)


def direct_kernel(
    where_ref, y_ref, bc_ref, g_ref, enter_ref, gate_ref, gain_ref, e_ref, w_ref, after_ref,
    *rest, tiles,
):
    *out_refs, normed_ref, carry, grown = rest
    i = pl.program_id(0)

    @pl.when(i < tiles)
    def _():
        norm_tile(
            y_ref, bc_ref, g_ref, enter_ref, gate_ref, gain_ref, e_ref, normed_ref, carry, grown, i
        )

    for k, out_ref in enumerate(out_refs):
        @pl.when(i == tiles + k)
        def _(out_ref=out_ref):
            out_ref[...] = dot(normed_ref[...], w_ref[...]).astype(BF16)


def line_kernel(
    y_ref, bc_ref, g_ref, enter_ref, gate_ref, gain_ref, e_ref, w_ref, after_ref,
    shares_ref, up_a_ref, up_b_ref, down_a_ref, down_b_ref, normed_ref, carry, grown, *, tiles,
):
    i = pl.program_id(0)

    @pl.when(i < tiles)
    def _():
        norm_tile(
            y_ref, bc_ref, g_ref, enter_ref, gate_ref, gain_ref, e_ref, normed_ref, carry, grown, i
        )

    @pl.when(i >= tiles)
    def _():
        shares_ref[0] = dot(normed_ref[...], w_ref[...]).astype(BF16)

    size = up_a_ref.shape[0]

    @pl.when(i == tiles)
    def _():
        down_a_ref[...] = shares_ref[0, :size]
        down_b_ref[...] = shares_ref[0, size:]

    @pl.when(i == pl.num_programs(0) - 1)
    def _():
        up_a_ref[...] = shares_ref[0, :size]
        up_b_ref[...] = shares_ref[0, size:]


def onward_kernel(where_ref, up_own_ref, down_own_ref, up_ref, down_ref, after_ref, up_out, down_out):
    up_out[...] = (up_own_ref[0].astype(F32) + up_ref[...].astype(F32)).astype(BF16)
    down_out[...] = (down_own_ref[0].astype(F32) + down_ref[...].astype(F32)).astype(BF16)


def final_kernel(where_ref, own_ref, up_ref, down_ref, *rest):
    out_ref = rest[-1]
    total = own_ref[0].astype(F32) + up_ref[...].astype(F32) + down_ref[...].astype(F32)
    out_ref[...] = total.astype(BF16)


def direct_final_kernel(where_ref, normed_ref, w_ref, *refs, count):
    out_ref = refs[-1]
    total = dot(normed_ref[...], w_ref[...])
    for ref in refs[:count]:
        total = total + ref[...].astype(F32)
    out_ref[...] = total.astype(BF16)


def in_hbm(x):
    return pltpu.with_memory_space_constraint(x, pltpu.HBM)


def brief():
    return pl.CostEstimate(flops=1, transcendentals=0, bytes_accessed=1)


def params(limit=VMEM_LIMIT):
    return pltpu.CompilerParams(dimension_semantics=("arbitrary",), vmem_limit_bytes=limit)


def whole(shape):
    return pl.BlockSpec(shape, lambda *b: (0,) * len(shape))


def unread():
    return pl.BlockSpec(memory_space=pl.ANY)


def shaped(shape, dtype=BF16):
    return jax.ShapeDtypeStruct(shape, dtype)


def local(
    inner_input, state_maps, gate_input, step_input, log_decay_rate, step_bias,
    skip_gain, conv_kernel, map_kernel, norm_gain, out_weight,
):
    tokens, width = inner_input.shape
    groups = state_maps.shape[2]
    parts = 2 * groups
    heads = step_input.shape[1]
    blocks = tokens // BLK
    slabs = lax.axis_size("seq")
    chans = lax.axis_size("chan")
    features = out_weight.shape[1]
    map_width = parts * STATE
    low, high = spread(0, heads, width), spread(2 * heads, heads, width)

    tail = jnp.concatenate(
        [inner_input[tokens - HALO :], state_maps[tokens - HALO :].reshape(HALO, map_width)], 1
    )
    tail = lax.ppermute(tail, "seq", [(i, i + 1) for i in range(slabs - 1)])

    def lanes_at(count):
        return pl.BlockSpec((count, WIDE), lambda c: (0, c))

    xc, bc, bt, crow, cols, w_hl, g_hl, pay = pl.pallas_call(
        states_kernel,
        grid=(width // WIDE,),
        in_specs=[
            lanes_at(tokens),
            whole((tokens * parts, STATE)),
            whole((heads, tokens)),
            lanes_at(HALO),
            pl.BlockSpec((HALO, map_width), lambda c: (0, width // map_width)),
            whole((1, heads)),
            whole((1, heads)),
            lanes_at(4),
            whole((4 * parts, STATE)),
            lanes_at(LANES),
        ],
        out_specs=[
            lanes_at(tokens),
            whole((tokens, map_width)),
            whole((groups, STATE, tokens)),
            whole((heads, tokens)),
            whole((tokens, LANES)),
            whole((tokens, LANES)),
            whole((tokens, LANES)),
            whole((STATE, width + LANES)),
        ],
        out_shape=[
            shaped((tokens, width)),
            shaped((tokens, map_width)),
            shaped((groups, STATE, tokens)),
            shaped((heads, tokens), F32),
            shaped((tokens, LANES), F32),
            shaped((tokens, LANES)),
            shaped((tokens, LANES)),
            shaped((STATE, width + LANES)),
        ],
        scratch_shapes=[pltpu.VMEM((tokens, WIDE), BF16)],
        compiler_params=params(),
        name="states",
    )(
        inner_input, state_maps.reshape(tokens * parts, STATE), step_input.T, tail, tail,
        step_bias.reshape(1, heads), log_decay_rate.reshape(1, heads),
        conv_kernel, map_kernel.reshape(4 * parts, STATE), low,
    )

    part = STATE // slabs
    arrived = lax.all_to_all(
        pay.reshape(slabs, part, width + LANES), "seq", split_axis=0, concat_axis=0, tiled=True
    )

    def local_part(start, count, before, after):
        def tile(width):
            return pl.BlockSpec((BLK, width), lambda b: (start + b, 0))

        operands = [xc, bc, bt, crow, cols, w_hl, g_hl, skip_gain.reshape(1, heads), low, high]
        specs = [
            tile(width),
            tile(map_width),
            pl.BlockSpec((groups, STATE, BLK), lambda b: (0, 0, start + b)),
            pl.BlockSpec((heads, BLK), lambda b: (0, start + b)),
            tile(LANES),
            tile(LANES),
            tile(LANES),
            whole((1, heads)),
            whole((LANES, width)),
            whole((LANES, width)),
        ]
        aliases = {}
        if before is not None:
            y, state = before
            aliases = {len(operands) + 1: 0}
            operands += [state, y]
            specs += [whole((STATE, width)), unread()]
        operands.append(after)
        specs.append(unread())
        return pl.pallas_call(
            local_kernel,
            grid=(count,),
            in_specs=specs,
            out_specs=[tile(width), whole((STATE, width))],
            out_shape=[shaped((tokens, width)), shaped((STATE, width), F32)],
            input_output_aliases=aliases,
            scratch_shapes=[pltpu.VMEM((HALO, width), F32)],
            compiler_params=params(),
            cost_estimate=brief(),
            name="local_part",
        )(*operands)

    some = blocks // 4
    y_first = local_part(0, some, None, pay)
    entering = pl.pallas_call(
        prefix_kernel,
        out_shape=shaped((slabs, part, width)),
        in_specs=[
            pl.BlockSpec(memory_space=pltpu.VMEM),
            pl.BlockSpec(memory_space=pltpu.VMEM),
            unread(),
        ],
        out_specs=pl.BlockSpec(memory_space=pltpu.VMEM),
        compiler_params=pltpu.CompilerParams(vmem_limit_bytes=SMALL_LIMIT),
        name="prefix",
    )(arrived, high, y_first[1])
    y_second = local_part(some, some, y_first, entering)
    entering = lax.all_to_all(entering, "seq", split_axis=0, concat_axis=0, tiled=True)
    entering = entering.reshape(STATE, width)

    part_out = features // chans
    norm_row = norm_gain.reshape(1, width)
    mine = lax.axis_index("chan").astype(jnp.int32)
    where = mine.reshape(1)

    def norm_operands(start, count, y):
        def tile(width):
            return pl.BlockSpec((BLK, width), lambda i, *_: (start + jnp.minimum(i, count - 1), 0))

        operands = [y, bc, g_hl, entering, gate_input, norm_row, high]
        specs = [
            tile(width),
            tile(map_width),
            tile(LANES),
            whole((STATE, width)),
            tile(width),
            whole((1, width)),
            whole((LANES, width)),
        ]
        return operands, specs

    def project_direct(start, count, y, after, slots):
        operands, specs = norm_operands(start, count, y)
        size = count * BLK

        def weights(i, where):
            step = i - count
            slot = slots[-1]
            for k in range(len(slots) - 1, -1, -1):
                slot = jnp.where(step <= k, slots[k], slot)
            return (0, lax.rem(where[0] + slot, chans))

        return pl.pallas_call(
            functools.partial(direct_kernel, tiles=count),
            grid_spec=pltpu.PrefetchScalarGridSpec(
                num_scalar_prefetch=1,
                grid=(count + len(slots),),
                in_specs=specs + [pl.BlockSpec((width, part_out), weights), unread()],
                out_specs=[whole((size, part_out))] * len(slots) + [whole((size, width))],
                scratch_shapes=[pltpu.VMEM((BLK, width), F32)] * 2,
            ),
            out_shape=[shaped((size, part_out))] * len(slots) + [shaped((size, width))],
            compiler_params=params(),
            name="project_direct",
        )(where, *operands, out_weight, after)

    def direct_final(start, normed, pieces, out, after):
        def tile(width, start=0):
            return pl.BlockSpec((BLK, width), lambda i, where: (start + i, 0))

        operands = [where, in_hbm(normed), in_hbm(out_weight)] + pieces + [after]
        specs = [
            tile(width),
            pl.BlockSpec((width, part_out), lambda i, where: (0, where[0])),
        ]
        specs += [tile(part_out)] * len(pieces) + [unread()]
        aliases = {}
        if out is not None:
            aliases = {len(operands): 0}
            operands.append(out)
            specs.append(unread())
        return pl.pallas_call(
            functools.partial(direct_final_kernel, count=len(pieces)),
            grid_spec=pltpu.PrefetchScalarGridSpec(
                num_scalar_prefetch=1,
                grid=(normed.shape[0] // BLK,),
                in_specs=specs,
                out_specs=tile(part_out, start),
            ),
            out_shape=shaped((tokens, part_out)),
            input_output_aliases=aliases,
            compiler_params=params(SMALL_LIMIT),
            name="direct_final",
        )(*operands)

    def project_line(start, count, y, after):
        operands, specs = norm_operands(start, count, y)
        size = count * BLK

        def dest(i):
            return jnp.maximum(i - count, 0)

        return pl.pallas_call(
            functools.partial(line_kernel, tiles=count),
            grid=(count + chans,),
            in_specs=specs
            + [pl.BlockSpec((width, part_out), lambda i: (0, dest(i))), unread()],
            out_specs=[
                pl.BlockSpec((1, size, part_out), lambda i: (dest(i), 0, 0)),
            ]
            + [whole((size // 2, part_out))] * 4,
            out_shape=[shaped((chans, size, part_out))] + [shaped((size // 2, part_out))] * 4,
            scratch_shapes=[pltpu.VMEM((size, width), BF16)] + [pltpu.VMEM((BLK, width), F32)] * 2,
            compiler_params=params(),
            cost_estimate=brief(),
            name="project_line",
        )(*operands, out_weight, after)

    def permuted(up, down, s):
        up = lax.ppermute(up, "chan", [(a, a + 1) for a in range(s + 1)])
        down = lax.ppermute(down, "chan", [(a, a - 1) for a in range(chans - 1 - s, chans)])
        return up, down

    def onward(shares, half, up, down, s, after):
        count = up.shape[0] // BLK

        def plain(i, where):
            return (i, 0)

        return pl.pallas_call(
            onward_kernel,
            grid_spec=pltpu.PrefetchScalarGridSpec(
                num_scalar_prefetch=1,
                grid=(count,),
                in_specs=[
                    pl.BlockSpec(
                        (1, BLK, part_out),
                        lambda i, where: (
                            jnp.minimum(chans - 1 - s + where[0], chans - 1), half * count + i, 0
                        ),
                    ),
                    pl.BlockSpec(
                        (1, BLK, part_out),
                        lambda i, where: (
                            jnp.maximum(where[0] - (chans - 1) + s, 0), half * count + i, 0
                        ),
                    ),
                    pl.BlockSpec((BLK, part_out), plain),
                    pl.BlockSpec((BLK, part_out), plain),
                    unread(),
                ],
                out_specs=[pl.BlockSpec((BLK, part_out), plain)] * 2,
            ),
            out_shape=[shaped(up.shape)] * 2,
            compiler_params=params(SMALL_LIMIT),
            name="onward",
        )(where, in_hbm(shares), in_hbm(shares), up, down, after)

    def final(start, shares, half, up, down, out):
        count = up.shape[0] // BLK

        def plain(i, where):
            return (i, 0)

        operands = [where, in_hbm(shares), up, down]
        in_specs = [
            pl.BlockSpec((1, BLK, part_out), lambda i, where: (where[0], half * count + i, 0)),
            pl.BlockSpec((BLK, part_out), plain),
            pl.BlockSpec((BLK, part_out), plain),
        ]
        aliases = {}
        if out is not None:
            aliases = {len(operands): 0}
            operands.append(out)
            in_specs.append(unread())
        return pl.pallas_call(
            final_kernel,
            grid_spec=pltpu.PrefetchScalarGridSpec(
                num_scalar_prefetch=1,
                grid=(count,),
                in_specs=in_specs,
                out_specs=pl.BlockSpec((BLK, part_out), lambda i, where: (start + half * count + i, 0)),
            ),
            out_shape=shaped((tokens, part_out)),
            input_output_aliases=aliases,
            compiler_params=params(SMALL_LIMIT),
            name="final",
        )(*operands)

    half = blocks // 2
    order = sorted(range(1, chans), key=lambda k: (min(k, chans - k), k))
    *slots, normed = project_direct(0, half, y_second[0], y_second[1], order)
    pieces = []
    for k, slot in zip(order, slots):
        turn = [(a, (a + k) % chans) for a in range(chans)]
        pieces.append(lax.ppermute(slot, "chan", turn))

    y_third = local_part(2 * some, blocks - 2 * some, y_second, normed)
    shares, up_a, up_b, down_a, down_b = project_line(half, blocks - half, y_third[0], normed)
    moving = [permuted(up_a, down_a, 0), permuted(up_b, down_b, 0)]
    out = direct_final(0, normed, pieces, None, shares)
    after = out
    for s in range(1, chans - 1):
        for k in range(2):
            up, down = onward(shares, k, *moving[k], s, after)
            after = up
            moving[k] = permuted(up, down, s)
    for k in range(2):
        out = final(half, shares, k, *moving[k], out)
    return out


def solution(mesh):
    return jax.shard_map(
        local,
        mesh=mesh,
        in_specs=(
            P("seq", "chan"),
            P("seq", None, "chan", None),
            P("seq", "chan"),
            P("seq", "chan"),
            P("chan"),
            P("chan"),
            P("chan"),
            P(None, "chan"),
            P(None, None, "chan", None),
            P("chan"),
            P("chan", None),
        ),
        out_specs=P("seq", "chan"),
        check_vma=False,
    )
```

```python
import functools

import jax
import jax.numpy as jnp
import numpy as np
from jax import lax
from jax.experimental import pallas as pl
from jax.experimental.pallas import tpu as pltpu
from jax.sharding import PartitionSpec as P

HEAD_DIM = 64
STATE = 128
BLK = 128
LANES = 128
HALO = 8
ROWS = 16
WIDE = 512

step_limit = 0.5
epsilon = 1e-05
LOG2E = 1.4426950408889634
F32 = jnp.float32
BF16 = jnp.bfloat16
VMEM_LIMIT = 58 * 1024 * 1024
SMALL_LIMIT = 10 * 1024 * 1024


def silu(v):
    half = 0.5 * v
    return half + half * jnp.tanh(half)


def high_low(v):
    high = v.astype(BF16).astype(F32)
    return high, v - high


def spread(heads, width):
    result = np.zeros((LANES, width), np.float32)
    for k in range(2 * heads):
        h = k % heads
        result[k, h * HEAD_DIM : (h + 1) * HEAD_DIM] = 1.0
    return jnp.asarray(result, BF16)


def dot(a, b):
    return jnp.dot(a, b, preferred_element_type=F32)


def dot_t(a, b):
    return lax.dot_general(a, b, (((1,), (1,)), ((), ())), preferred_element_type=F32)


def column(row):
    count = row.shape[1]
    eye = lax.broadcasted_iota(jnp.int32, (count, count), 0) == lax.broadcasted_iota(
        jnp.int32, (count, count), 1
    )
    return jnp.sum(jnp.where(eye, row, 0.0), axis=1, keepdims=True)


def padded(pieces):
    rows = jnp.concatenate(pieces, 0)
    if rows.shape[0] == LANES:
        return rows
    return jnp.concatenate([rows, jnp.zeros((LANES - rows.shape[0], rows.shape[1]), rows.dtype)], 0)


def conv(before, cur, taps):
    full = jnp.concatenate([before, cur], 0)
    late = pltpu.roll(full, 1, 0)
    early = taps[1] * full + taps[0] * late
    acc = taps[3] * cur + taps[2] * late[HALO:] + pltpu.roll(early, 2, 0)[HALO:]
    return silu(acc).astype(BF16)


def states_kernel(
    x_ref, maps_ref, step_ref, tail_ref, mtail_ref, bias_ref, rate_ref, ck_ref, mk_ref, e_ref,
    xc_ref, bc_ref, bt_ref, crow_ref, cols_ref, wrow_ref, g_ref, pay_ref,
    weighted, w_ref,
):
    c = pl.program_id(0)
    heads, tokens = step_ref.shape
    parts = mk_ref.shape[0] // 4
    groups = parts // 2
    blocks = tokens // BLK

    @pl.when(c == 0)
    def _():
        bias, rate = column(bias_ref[...]), -jnp.exp(column(rate_ref[...]))
        v = step_ref[...] + bias
        step = jnp.minimum(jnp.maximum(v, 0.0) + jnp.log1p(jnp.exp(-jnp.abs(v))), step_limit)
        log_step = rate * step
        first, rest = high_low(log_step)
        second, third = high_low(rest)
        pieces = []
        for b in range(blocks):
            at = slice(b * BLK, (b + 1) * BLK)
            pieces += [first[:, at], second[:, at], third[:, at]]
        row = lax.broadcasted_iota(jnp.int32, (BLK, BLK), 0)
        col = lax.broadcasted_iota(jnp.int32, (BLK, BLK), 1)
        tri = jnp.where(row <= col, 1.0, 0.0).astype(BF16)
        sums = dot(jnp.concatenate(pieces, 0).astype(BF16), tri)
        cums, leads = [], [jnp.zeros((heads, 1), F32)]
        for b in range(blocks):
            at = 3 * b * heads
            cum = (
                sums[at : at + heads]
                + sums[at + heads : at + 2 * heads]
                + sums[at + 2 * heads : at + 3 * heads]
            )
            cums.append(cum)
            leads.append(leads[-1] + cum[:, BLK - 1 : BLK])
        last = None
        for b in range(blocks):
            at = slice(b * BLK, (b + 1) * BLK)
            cum, step_b = cums[b], step[:, at]
            total = cum[:, BLK - 1 : BLK]
            wrow_ref[:, at] = jnp.exp(total - cum) * step_b
            slab_weight = jnp.exp(leads[blocks] - (leads[b] + cum)) * step_b
            entered = jnp.exp(cum + leads[b])
            crow_ref[:, at] = (cum - jnp.log(step_b)) * LOG2E
            w_ref[at, :] = padded(high_low(slab_weight)).T.astype(BF16)
            last = padded(high_low(entered)).T
            g_ref[at, :] = last.astype(BF16)
            cols_ref[at, :] = padded((cum * LOG2E,)).T
        pay_ref[:, heads * HEAD_DIM :] = jnp.broadcast_to(last[BLK - 1 :], (STATE, LANES)).astype(BF16)

        row = lax.broadcasted_iota(jnp.int32, (BLK * parts, BLK * parts), 0)
        col = lax.broadcasted_iota(jnp.int32, (BLK * parts, BLK * parts), 1)
        source = (row & (BLK - 1)) * parts + row // BLK
        pick = jnp.where(col == source, 1.0, 0.0).astype(BF16)
        before = [mtail_ref[:, q * STATE : (q + 1) * STATE].astype(F32) for q in range(parts)]
        for b in range(blocks):
            ordered = dot(pick, maps_ref[b * BLK * parts : (b + 1) * BLK * parts, :])
            for q in range(parts):
                cur = ordered[q * BLK : (q + 1) * BLK]
                taps = [mk_ref[k * parts + q : k * parts + q + 1] for k in range(4)]
                result = conv(before[q], cur, taps)
                before[q] = cur[BLK - HALO :]
                bc_ref[b * BLK : (b + 1) * BLK, q * STATE : (q + 1) * STATE] = result
                if q < groups:
                    bt_ref[q, :, b * BLK : (b + 1) * BLK] = result.astype(F32).T.astype(BF16)

    for lane in range(0, x_ref.shape[1], LANES):
        at_lanes = slice(lane, lane + LANES)
        taps = [ck_ref[k : k + 1, at_lanes] for k in range(4)]
        before = tail_ref[:, at_lanes].astype(F32)
        for b in range(blocks):
            at = slice(b * BLK, (b + 1) * BLK)
            cur = x_ref[at, at_lanes].astype(F32)
            result = conv(before, cur, taps)
            before = cur[BLK - HALO :]
            xc_ref[at, at_lanes] = result
            scale = dot(w_ref[at, :], e_ref[:, at_lanes])
            weighted[at, at_lanes] = (result.astype(F32) * scale).astype(BF16)
    step_width = x_ref.shape[1]
    group = c * step_width * groups // (heads * HEAD_DIM)
    at = pl.ds(pl.multiple_of(c * step_width, step_width), step_width)
    pay_ref[:, at] = dot(bt_ref[group], weighted[...]).astype(BF16)


def local_kernel(xc_ref, bc_ref, bt_ref, crow_ref, cols_ref, wrow_ref, skip_ref, *rest):
    y_ref, state = rest[-2:]
    width = xc_ref.shape[1]
    groups = bt_ref.shape[0]
    gw = width // groups

    @pl.when(pl.program_id(0) == 0)
    def _():
        state[...] = rest[0][...] if len(rest) > 3 else jnp.zeros_like(state)

    left = lax.broadcasted_iota(jnp.int32, (BLK, LANES), 1) < HEAD_DIM
    row = lax.broadcasted_iota(jnp.int32, (BLK, BLK), 0)
    causal = row >= lax.broadcasted_iota(jnp.int32, (BLK, BLK), 1)
    for g in range(groups):
        b_g = bc_ref[:, g * STATE : (g + 1) * STATE]
        c_g = bc_ref[:, (groups + g) * STATE : (groups + g + 1) * STATE]
        scores = jnp.where(causal, dot_t(c_g, b_g), 0.0)
        b_t = bt_ref[g].astype(F32)
        for wide in range(g * gw, (g + 1) * gw, 2 * LANES):
            before = state[:, wide : wide + 2 * LANES]
            carry = dot(c_g, before.astype(BF16))
            for k in range(2):
                at = slice(wide + k * LANES, wide + (k + 1) * LANES)
                part = slice(k * LANES, (k + 1) * LANES)
                first = at.start // HEAD_DIM
                mixing, weighted, cums = [], [], []
                for h in (first, first + 1):
                    cum = jnp.broadcast_to(cols_ref[:, h : h + 1], (BLK, BLK))
                    gap = jnp.minimum(cum - crow_ref[h : h + 1], 0.0)
                    mixing.append((jnp.exp2(gap) * scores).astype(BF16))
                    weighted.append((b_t * wrow_ref[h : h + 1]).astype(BF16))
                    cums.append(cum)
                x = xc_ref[:, at]
                nil = jnp.zeros_like(x)
                stacked = jnp.concatenate([jnp.where(left, x, nil), jnp.where(left, nil, x)], 0)
                both = jnp.concatenate(
                    [jnp.concatenate(mixing, 1), jnp.concatenate(weighted, 1)], 0
                )
                result = dot(both, stacked)
                grown = jnp.exp2(jnp.where(left, cums[0], cums[1]))
                skip = jnp.where(left, skip_ref[0, first], skip_ref[0, first + 1])
                y = result[:BLK] + grown * carry[:, part] + skip * x.astype(F32)
                y_ref[:, at] = y.astype(BF16)
                state[:, at] = grown[BLK - 1 :] * before[:, part] + result[BLK:]


def prefix_kernel(pay_ref, e_ref, after_ref, out_ref):
    width = out_ref.shape[2]
    decays = dot(pay_ref[:, 0, width:], e_ref[...])
    running = jnp.zeros(out_ref.shape[1:], F32)
    for slab in range(out_ref.shape[0]):
        out_ref[slab] = running.astype(BF16)
        running = decays[slab : slab + 1] * running + pay_ref[slab, :, :width].astype(F32)


def norm_tile(
    y_ref, bc_ref, g_ref, enter_ref, gate_ref, gain_ref, e_ref, normed_ref, carry, grown, i
):
    width = y_ref.shape[1]
    groups = bc_ref.shape[1] // (2 * STATE)
    gw = width // groups
    grown[...] = dot(g_ref[...], e_ref[...])
    for g in range(groups):
        at = slice(g * gw, (g + 1) * gw)
        carry[:, at] = dot(bc_ref[:, (groups + g) * STATE : (groups + g + 1) * STATE], enter_ref[:, at])
    size = y_ref.shape[0]
    for r in range(0, size, ROWS):
        rows = slice(r, r + ROWS)
        out_rows = pl.ds(pl.multiple_of(i * size + r, ROWS), ROWS)
        for g in range(groups):
            at = slice(g * gw, (g + 1) * gw)
            y = y_ref[rows, at].astype(F32) + grown[rows, at] * carry[rows, at]
            gated = y * silu(gate_ref[rows, at].astype(F32))
            square_mean = jnp.mean(gated * gated, axis=-1, keepdims=True)
            scaled = gated * lax.rsqrt(square_mean + epsilon) * gain_ref[:, at]
            normed_ref[out_rows, at] = scaled.astype(BF16)


def direct_kernel(
    where_ref, y_ref, bc_ref, g_ref, enter_ref, gate_ref, gain_ref, e_ref, w_ref, after_ref,
    *rest, tiles,
):
    *out_refs, normed_ref, carry, grown = rest
    i = pl.program_id(0)

    @pl.when(i < tiles)
    def _():
        norm_tile(
            y_ref, bc_ref, g_ref, enter_ref, gate_ref, gain_ref, e_ref, normed_ref, carry, grown, i
        )

    for k, out_ref in enumerate(out_refs):
        @pl.when(i == tiles + k)
        def _(out_ref=out_ref):
            out_ref[...] = dot(normed_ref[...], w_ref[...]).astype(BF16)


def line_kernel(
    y_ref, bc_ref, g_ref, enter_ref, gate_ref, gain_ref, e_ref, w_ref, after_ref,
    shares_ref, up_a_ref, up_b_ref, down_a_ref, down_b_ref, normed_ref, carry, grown, *, tiles,
):
    i = pl.program_id(0)

    @pl.when(i < tiles)
    def _():
        norm_tile(
            y_ref, bc_ref, g_ref, enter_ref, gate_ref, gain_ref, e_ref, normed_ref, carry, grown, i
        )

    @pl.when(i >= tiles)
    def _():
        shares_ref[0] = dot(normed_ref[...], w_ref[...]).astype(BF16)

    size = up_a_ref.shape[0]

    @pl.when(i == tiles)
    def _():
        down_a_ref[...] = shares_ref[0, :size]
        down_b_ref[...] = shares_ref[0, size:]

    @pl.when(i == pl.num_programs(0) - 1)
    def _():
        up_a_ref[...] = shares_ref[0, :size]
        up_b_ref[...] = shares_ref[0, size:]


def onward_kernel(where_ref, up_own_ref, down_own_ref, up_ref, down_ref, after_ref, up_out, down_out):
    up_out[...] = (up_own_ref[0].astype(F32) + up_ref[...].astype(F32)).astype(BF16)
    down_out[...] = (down_own_ref[0].astype(F32) + down_ref[...].astype(F32)).astype(BF16)


def final_kernel(where_ref, own_ref, up_ref, down_ref, *rest):
    out_ref = rest[-1]
    total = own_ref[0].astype(F32) + up_ref[...].astype(F32) + down_ref[...].astype(F32)
    out_ref[...] = total.astype(BF16)


def direct_final_kernel(where_ref, normed_ref, w_ref, *refs, count):
    out_ref = refs[-1]
    total = dot(normed_ref[...], w_ref[...])
    for ref in refs[:count]:
        total = total + ref[...].astype(F32)
    out_ref[...] = total.astype(BF16)


def in_hbm(x):
    return pltpu.with_memory_space_constraint(x, pltpu.HBM)


def brief():
    return pl.CostEstimate(flops=1, transcendentals=0, bytes_accessed=1)


def params(limit=VMEM_LIMIT):
    return pltpu.CompilerParams(dimension_semantics=("arbitrary",), vmem_limit_bytes=limit)


def whole(shape):
    return pl.BlockSpec(shape, lambda *b: (0,) * len(shape))


def unread():
    return pl.BlockSpec(memory_space=pl.ANY)


def shaped(shape, dtype=BF16):
    return jax.ShapeDtypeStruct(shape, dtype)


def local(
    inner_input, state_maps, gate_input, step_input, log_decay_rate, step_bias,
    skip_gain, conv_kernel, map_kernel, norm_gain, out_weight,
):
    tokens, width = inner_input.shape
    groups = state_maps.shape[2]
    parts = 2 * groups
    heads = step_input.shape[1]
    blocks = tokens // BLK
    slabs = lax.axis_size("seq")
    chans = lax.axis_size("chan")
    features = out_weight.shape[1]
    map_width = parts * STATE
    low = spread(heads, width)

    tail = jnp.concatenate(
        [inner_input[tokens - HALO :], state_maps[tokens - HALO :].reshape(HALO, map_width)], 1
    )
    tail = lax.ppermute(tail, "seq", [(i, i + 1) for i in range(slabs - 1)])

    def lanes_at(count):
        return pl.BlockSpec((count, WIDE), lambda c: (0, c))

    xc, bc, bt, crow, cols, wrow, g_hl, pay = pl.pallas_call(
        states_kernel,
        grid=(width // WIDE,),
        in_specs=[
            lanes_at(tokens),
            whole((tokens * parts, STATE)),
            whole((heads, tokens)),
            lanes_at(HALO),
            pl.BlockSpec((HALO, map_width), lambda c: (0, width // map_width)),
            whole((1, heads)),
            whole((1, heads)),
            lanes_at(4),
            whole((4 * parts, STATE)),
            lanes_at(LANES),
        ],
        out_specs=[
            lanes_at(tokens),
            whole((tokens, map_width)),
            whole((groups, STATE, tokens)),
            whole((heads, tokens)),
            whole((tokens, LANES)),
            whole((heads, tokens)),
            whole((tokens, LANES)),
            whole((STATE, width + LANES)),
        ],
        out_shape=[
            shaped((tokens, width)),
            shaped((tokens, map_width)),
            shaped((groups, STATE, tokens)),
            shaped((heads, tokens), F32),
            shaped((tokens, LANES), F32),
            shaped((heads, tokens), F32),
            shaped((tokens, LANES)),
            shaped((STATE, width + LANES)),
        ],
        scratch_shapes=[pltpu.VMEM((tokens, WIDE), BF16), pltpu.VMEM((tokens, LANES), BF16)],
        compiler_params=params(),
        name="states",
    )(
        inner_input, state_maps.reshape(tokens * parts, STATE), step_input.T, tail, tail,
        step_bias.reshape(1, heads), log_decay_rate.reshape(1, heads),
        conv_kernel, map_kernel.reshape(4 * parts, STATE), low,
    )

    part = STATE // slabs
    arrived = lax.all_to_all(
        pay.reshape(slabs, part, width + LANES), "seq", split_axis=0, concat_axis=0, tiled=True
    )

    def local_part(start, count, before, after):
        def tile(width):
            return pl.BlockSpec((BLK, width), lambda b: (start + b, 0))

        operands = [xc, bc, bt, crow, cols, wrow, skip_gain.reshape(1, heads)]
        specs = [
            tile(width),
            tile(map_width),
            pl.BlockSpec((groups, STATE, BLK), lambda b: (0, 0, start + b)),
            pl.BlockSpec((heads, BLK), lambda b: (0, start + b)),
            tile(LANES),
            pl.BlockSpec((heads, BLK), lambda b: (0, start + b)),
            pl.BlockSpec(memory_space=pltpu.SMEM),
        ]
        aliases = {}
        if before is not None:
            y, state = before
            aliases = {len(operands) + 1: 0}
            operands += [state, in_hbm(y)]
            specs += [whole((STATE, width)), unread()]
        operands.append(in_hbm(after))
        specs.append(unread())
        return pl.pallas_call(
            local_kernel,
            grid=(count,),
            in_specs=specs,
            out_specs=[tile(width), whole((STATE, width))],
            out_shape=[shaped((tokens, width)), shaped((STATE, width), F32)],
            input_output_aliases=aliases,
            compiler_params=params(),
            cost_estimate=brief(),
            name="local_part",
        )(*operands)

    some = blocks // 2
    y_first = local_part(0, some, None, pay)
    entering = pl.pallas_call(
        prefix_kernel,
        out_shape=shaped((slabs, part, width)),
        in_specs=[
            pl.BlockSpec(memory_space=pltpu.VMEM),
            pl.BlockSpec(memory_space=pltpu.VMEM),
            unread(),
        ],
        out_specs=pl.BlockSpec(memory_space=pltpu.VMEM),
        compiler_params=pltpu.CompilerParams(vmem_limit_bytes=SMALL_LIMIT),
        name="prefix",
    )(arrived, low, in_hbm(y_first[0]))
    y_second = local_part(some, some, y_first, entering)
    entering = lax.all_to_all(entering, "seq", split_axis=0, concat_axis=0, tiled=True)
    entering = entering.reshape(STATE, width)

    part_out = features // chans
    norm_row = norm_gain.reshape(1, width)
    mine = lax.axis_index("chan").astype(jnp.int32)
    where = mine.reshape(1)

    def norm_operands(start, count, tokens_each, y):
        def tile(width):
            return pl.BlockSpec((tokens_each, width), lambda i, *_: (start + jnp.minimum(i, count - 1), 0))

        operands = [y, bc, g_hl, entering, gate_input, norm_row, low]
        specs = [
            tile(width),
            tile(map_width),
            tile(LANES),
            whole((STATE, width)),
            tile(width),
            whole((1, width)),
            whole((LANES, width)),
        ]
        return operands, specs

    def project_direct(start, count, tokens_each, y, after, slots):
        operands, specs = norm_operands(start, count, tokens_each, y)
        size = count * tokens_each

        def weights(i, where):
            step = i - count
            slot = slots[-1]
            for k in range(len(slots) - 1, -1, -1):
                slot = jnp.where(step <= k, slots[k], slot)
            return (0, lax.rem(where[0] + slot, chans))

        return pl.pallas_call(
            functools.partial(direct_kernel, tiles=count),
            grid_spec=pltpu.PrefetchScalarGridSpec(
                num_scalar_prefetch=1,
                grid=(count + len(slots),),
                in_specs=specs + [pl.BlockSpec((width, part_out), weights), unread()],
                out_specs=[whole((size, part_out))] * len(slots) + [whole((size, width))],
                scratch_shapes=[pltpu.VMEM((tokens_each, width), F32)] * 2,
            ),
            out_shape=[shaped((size, part_out))] * len(slots) + [shaped((size, width))],
            compiler_params=params(),
            name="project_direct",
        )(where, *operands, out_weight, in_hbm(after))

    def direct_final(start, normed, pieces, out, after):
        def tile(width, start=0):
            return pl.BlockSpec((BLK, width), lambda i, where: (start + i, 0))

        operands = [where, in_hbm(normed), in_hbm(out_weight)] + pieces + [in_hbm(after)]
        specs = [
            tile(width),
            pl.BlockSpec((width, part_out), lambda i, where: (0, where[0])),
        ]
        specs += [tile(part_out)] * len(pieces) + [unread()]
        aliases = {}
        if out is not None:
            aliases = {len(operands): 0}
            operands.append(in_hbm(out))
            specs.append(unread())
        return pl.pallas_call(
            functools.partial(direct_final_kernel, count=len(pieces)),
            grid_spec=pltpu.PrefetchScalarGridSpec(
                num_scalar_prefetch=1,
                grid=(normed.shape[0] // BLK,),
                in_specs=specs,
                out_specs=tile(part_out, start),
            ),
            out_shape=shaped((tokens, part_out)),
            input_output_aliases=aliases,
            compiler_params=params(SMALL_LIMIT),
            name="direct_final",
        )(*operands)

    def project_line(start, count, tokens_each, split, y, after):
        operands, specs = norm_operands(start, count, tokens_each, y)
        size = count * tokens_each

        def dest(i):
            return jnp.maximum(i - count, 0)

        return pl.pallas_call(
            functools.partial(line_kernel, tiles=count),
            grid=(count + chans,),
            in_specs=specs
            + [pl.BlockSpec((width, part_out), lambda i: (0, dest(i))), unread()],
            out_specs=[
                pl.BlockSpec((1, size, part_out), lambda i: (dest(i), 0, 0)),
            ]
            + [whole((k, part_out)) for k in split * 2],
            out_shape=[shaped((chans, size, part_out))] + [shaped((k, part_out)) for k in split * 2],
            scratch_shapes=[pltpu.VMEM((size, width), BF16)] + [pltpu.VMEM((tokens_each, width), F32)] * 2,
            compiler_params=params(),
            cost_estimate=brief(),
            name="project_line",
        )(*operands, out_weight, in_hbm(after))

    def permuted(up, down, s):
        up = lax.ppermute(up, "chan", [(a, a + 1) for a in range(s + 1)])
        down = lax.ppermute(down, "chan", [(a, a - 1) for a in range(chans - 1 - s, chans)])
        return up, down

    def onward(shares, half, up, down, s, after):
        count = up.shape[0] // BLK
        skipped = (shares.shape[1] // BLK - count) * half

        def plain(i, where):
            return (i, 0)

        return pl.pallas_call(
            onward_kernel,
            grid_spec=pltpu.PrefetchScalarGridSpec(
                num_scalar_prefetch=1,
                grid=(count,),
                in_specs=[
                    pl.BlockSpec(
                        (1, BLK, part_out),
                        lambda i, where: (
                            jnp.minimum(chans - 1 - s + where[0], chans - 1), skipped + i, 0
                        ),
                    ),
                    pl.BlockSpec(
                        (1, BLK, part_out),
                        lambda i, where: (
                            jnp.maximum(where[0] - (chans - 1) + s, 0), skipped + i, 0
                        ),
                    ),
                    pl.BlockSpec((BLK, part_out), plain),
                    pl.BlockSpec((BLK, part_out), plain),
                    unread(),
                ],
                out_specs=[pl.BlockSpec((BLK, part_out), plain)] * 2,
            ),
            out_shape=[shaped((count * BLK, part_out))] * 2,
            compiler_params=params(SMALL_LIMIT),
            name="onward",
        )(where, in_hbm(shares), in_hbm(shares), up, down, after)

    def final(start, shares, half, up, down, out):
        count = up.shape[0] // BLK
        skipped = (shares.shape[1] // BLK - count) * half

        def plain(i, where):
            return (i, 0)

        operands = [where, in_hbm(shares), up, down]
        in_specs = [
            pl.BlockSpec((1, BLK, part_out), lambda i, where: (where[0], skipped + i, 0)),
            pl.BlockSpec((BLK, part_out), plain),
            pl.BlockSpec((BLK, part_out), plain),
        ]
        aliases = {}
        if out is not None:
            aliases = {len(operands): 0}
            operands.append(in_hbm(out))
            in_specs.append(unread())
        return pl.pallas_call(
            final_kernel,
            grid_spec=pltpu.PrefetchScalarGridSpec(
                num_scalar_prefetch=1,
                grid=(count,),
                in_specs=in_specs,
                out_specs=pl.BlockSpec((BLK, part_out), lambda i, where: (start + skipped + i, 0)),
            ),
            out_shape=shaped((tokens, part_out)),
            input_output_aliases=aliases,
            compiler_params=params(SMALL_LIMIT),
            name="final",
        )(*operands)

    lead = blocks * 3 // 8
    order = sorted(range(1, chans), key=lambda k: (min(k, chans - k), k))
    *slots, normed = project_direct(0, 2, lead * BLK // 2, y_second[0], y_second[1], order)
    pieces = []
    for k, slot in zip(order, slots):
        turn = [(a, (a + k) % chans) for a in range(chans)]
        pieces.append(lax.ppermute(slot, "chan", turn))

    rest = blocks - lead
    split = [(rest + 1) // 2 * BLK, rest // 2 * BLK]
    shares, up_a, up_b, down_a, down_b = project_line(
        lead, rest, BLK, split, y_second[0], normed
    )
    moving = [permuted(up_a, down_a, 0), permuted(up_b, down_b, 0)]
    out = direct_final(0, normed, pieces, None, shares)
    after = in_hbm(out)
    for s in range(1, chans - 1):
        for k in range(2):
            up, down = onward(shares, k, *moving[k], s, after)
            after = up
            moving[k] = permuted(up, down, s)
    for k in range(2):
        out = final(lead, shares, k, *moving[k], out)
    return out


def solution(mesh):
    return jax.shard_map(
        local,
        mesh=mesh,
        in_specs=(
            P("seq", "chan"),
            P("seq", None, "chan", None),
            P("seq", "chan"),
            P("seq", "chan"),
            P("chan"),
            P("chan"),
            P("chan"),
            P(None, "chan"),
            P(None, None, "chan", None),
            P("chan"),
            P("chan", None),
        ),
        out_specs=P("seq", "chan"),
        check_vma=False,
    )
```

```python
import functools

import jax
import jax.numpy as jnp
import numpy as np
from jax import lax
from jax.experimental import pallas as pl
from jax.experimental.pallas import tpu as pltpu
from jax.sharding import PartitionSpec as P

HEAD_DIM = 64
STATE = 128
BLK = 128
LANES = 128
HALO = 8
ROWS = 16
WIDE = 512

step_limit = 0.5
epsilon = 1e-05
LOG2E = 1.4426950408889634
F32 = jnp.float32
BF16 = jnp.bfloat16
VMEM_LIMIT = 58 * 1024 * 1024
SMALL_LIMIT = 10 * 1024 * 1024


def silu(v):
    half = 0.5 * v
    return half + half * jnp.tanh(half)


def high_low(v):
    high = v.astype(BF16).astype(F32)
    return high, v - high


def spread(heads, width):
    result = np.zeros((LANES, width), np.float32)
    for k in range(2 * heads):
        h = k % heads
        result[k, h * HEAD_DIM : (h + 1) * HEAD_DIM] = 1.0
    return jnp.asarray(result, BF16)


def dot(a, b):
    return jnp.dot(a, b, preferred_element_type=F32)


def dot_t(a, b):
    return lax.dot_general(a, b, (((1,), (1,)), ((), ())), preferred_element_type=F32)


def column(row):
    count = row.shape[1]
    eye = lax.broadcasted_iota(jnp.int32, (count, count), 0) == lax.broadcasted_iota(
        jnp.int32, (count, count), 1
    )
    return jnp.sum(jnp.where(eye, row, 0.0), axis=1, keepdims=True)


def padded(pieces):
    rows = jnp.concatenate(pieces, 0)
    if rows.shape[0] == LANES:
        return rows
    return jnp.concatenate([rows, jnp.zeros((LANES - rows.shape[0], rows.shape[1]), rows.dtype)], 0)


def conv(before, cur, taps):
    full = jnp.concatenate([before, cur], 0)
    late = pltpu.roll(full, 1, 0)
    early = taps[1] * full + taps[0] * late
    acc = taps[3] * cur + taps[2] * late[HALO:] + pltpu.roll(early, 2, 0)[HALO:]
    return silu(acc)


def states_kernel(
    x_ref, maps_ref, step_ref, tail_ref, mtail_ref, bias_ref, rate_ref, ck_ref, mk_ref, e_ref,
    xc_ref, bc_ref, bt_ref, crow_ref, cols_ref, wrow_ref, g_ref, pay_ref,
    weighted, w_ref, scale,
):
    c = pl.program_id(0)
    heads, tokens = step_ref.shape
    parts = mk_ref.shape[0] // 4
    groups = parts // 2
    blocks = tokens // BLK

    @pl.when(c == 0)
    def _():
        bias, rate = column(bias_ref[...]), -jnp.exp(column(rate_ref[...]))
        v = step_ref[...] + bias
        step = jnp.minimum(jnp.maximum(v, 0.0) + jnp.log1p(jnp.exp(-jnp.abs(v))), step_limit)
        log_step = rate * step
        first, rest = high_low(log_step)
        second, third = high_low(rest)
        pieces = []
        for b in range(blocks):
            at = slice(b * BLK, (b + 1) * BLK)
            pieces += [first[:, at], second[:, at], third[:, at]]
        row = lax.broadcasted_iota(jnp.int32, (BLK, BLK), 0)
        col = lax.broadcasted_iota(jnp.int32, (BLK, BLK), 1)
        tri = jnp.where(row <= col, 1.0, 0.0).astype(BF16)
        sums = dot(jnp.concatenate(pieces, 0).astype(BF16), tri)
        cums, leads = [], [jnp.zeros((heads, 1), F32)]
        for b in range(blocks):
            at = 3 * b * heads
            cum = (
                sums[at : at + heads]
                + sums[at + heads : at + 2 * heads]
                + sums[at + 2 * heads : at + 3 * heads]
            )
            cums.append(cum)
            leads.append(leads[-1] + cum[:, BLK - 1 : BLK])
        last = None
        for b in range(blocks):
            at = slice(b * BLK, (b + 1) * BLK)
            cum, step_b = cums[b], step[:, at]
            total = cum[:, BLK - 1 : BLK]
            wrow_ref[:, at] = jnp.exp(total - cum) * step_b
            slab_weight = jnp.exp(leads[blocks] - (leads[b] + cum)) * step_b
            entered = jnp.exp(cum + leads[b])
            crow_ref[:, at] = (cum - jnp.log(step_b)) * LOG2E
            w_ref[at, :] = padded(high_low(slab_weight)).T.astype(BF16)
            last = padded(high_low(entered)).T
            g_ref[at, :] = last.astype(BF16)
            cols_ref[at, :] = padded((cum * LOG2E,)).T
        pay_ref[:, heads * HEAD_DIM :] = jnp.broadcast_to(last[BLK - 1 :], (STATE, LANES)).astype(BF16)

        few = BLK // 2
        row = lax.broadcasted_iota(jnp.int32, (few * parts, few * parts), 0)
        col = lax.broadcasted_iota(jnp.int32, (few * parts, few * parts), 1)
        source = (row & (few - 1)) * parts + row // few
        pick = jnp.where(col == source, 1.0, 0.0).astype(BF16)
        before = [mtail_ref[:, q * STATE : (q + 1) * STATE].astype(F32) for q in range(parts)]
        for b in range(blocks):
            at = 2 * b * few * parts
            mixed = [maps_ref[at + k * few * parts : at + (k + 1) * few * parts] for k in range(2)]
            ordered = dot(pick, jnp.concatenate(mixed, 1))
            for q in range(parts):
                own = ordered[q * few : (q + 1) * few]
                cur = jnp.concatenate([own[:, :STATE], own[:, STATE:]], 0)
                taps = [mk_ref[k * parts + q : k * parts + q + 1] for k in range(4)]
                result = conv(before[q], cur, taps).astype(BF16)
                before[q] = cur[BLK - HALO :]
                bc_ref[b * BLK : (b + 1) * BLK, q * STATE : (q + 1) * STATE] = result
                if q < groups:
                    bt_ref[q, :, b * BLK : (b + 1) * BLK] = result.astype(F32).T.astype(BF16)

    scale[...] = dot(w_ref[...], e_ref[...])
    for lane in range(0, x_ref.shape[1], LANES):
        at_lanes = slice(lane, lane + LANES)
        taps = [ck_ref[k : k + 1, at_lanes] for k in range(4)]
        before = tail_ref[:, at_lanes].astype(F32)
        for b in range(blocks):
            at = slice(b * BLK, (b + 1) * BLK)
            cur = x_ref[at, at_lanes].astype(F32)
            result = conv(before, cur, taps)
            before = cur[BLK - HALO :]
            xc_ref[at, at_lanes] = result.astype(BF16)
            weighted[at, at_lanes] = (result * scale[at, at_lanes]).astype(BF16)
    step_width = x_ref.shape[1]
    group = c * step_width * groups // (heads * HEAD_DIM)
    at = pl.ds(pl.multiple_of(c * step_width, step_width), step_width)
    pay_ref[:, at] = dot(bt_ref[group], weighted[...]).astype(BF16)


def local_kernel(xc_ref, bc_ref, bt_ref, crow_ref, cols_ref, wrow_ref, skip_ref, *rest):
    y_ref, state = rest[-2:]
    width = xc_ref.shape[1]
    groups = bt_ref.shape[0]
    gw = width // groups

    @pl.when(pl.program_id(0) == 0)
    def _():
        state[...] = rest[0][...] if len(rest) > 3 else jnp.zeros_like(state)

    left = lax.broadcasted_iota(jnp.int32, (BLK, LANES), 1) < HEAD_DIM
    row = lax.broadcasted_iota(jnp.int32, (BLK, BLK), 0)
    causal = row >= lax.broadcasted_iota(jnp.int32, (BLK, BLK), 1)
    for g in range(groups):
        b_g = bc_ref[:, g * STATE : (g + 1) * STATE]
        c_g = bc_ref[:, (groups + g) * STATE : (groups + g + 1) * STATE]
        scores = jnp.where(causal, dot_t(c_g, b_g), 0.0)
        b_t = bt_ref[g].astype(F32)
        for wide in range(g * gw, (g + 1) * gw, 2 * LANES):
            before = state[:, wide : wide + 2 * LANES]
            carry = dot(c_g, before.astype(BF16))
            for k in range(2):
                at = slice(wide + k * LANES, wide + (k + 1) * LANES)
                part = slice(k * LANES, (k + 1) * LANES)
                first = at.start // HEAD_DIM
                mixing, weighted, cums = [], [], []
                for h in (first, first + 1):
                    cum = jnp.broadcast_to(cols_ref[:, h : h + 1], (BLK, BLK))
                    gap = jnp.minimum(cum - crow_ref[h : h + 1], 0.0)
                    mixing.append((jnp.exp2(gap) * scores).astype(BF16))
                    weighted.append((b_t * wrow_ref[h : h + 1]).astype(BF16))
                    cums.append(cum)
                x = xc_ref[:, at]
                nil = jnp.zeros_like(x)
                stacked = jnp.concatenate([jnp.where(left, x, nil), jnp.where(left, nil, x)], 0)
                both = jnp.concatenate(
                    [jnp.concatenate(mixing, 1), jnp.concatenate(weighted, 1)], 0
                )
                result = dot(both, stacked)
                grown = jnp.exp2(jnp.where(left, cums[0], cums[1]))
                skip = jnp.where(left, skip_ref[0, first], skip_ref[0, first + 1])
                y = result[:BLK] + grown * carry[:, part] + skip * x.astype(F32)
                y_ref[:, at] = y.astype(BF16)
                state[:, at] = grown[BLK - 1 :] * before[:, part] + result[BLK:]


def prefix_kernel(pay_ref, e_ref, after_ref, out_ref):
    width = out_ref.shape[2]
    decays = dot(pay_ref[:, 0, width:], e_ref[...])
    running = jnp.zeros(out_ref.shape[1:], F32)
    for slab in range(out_ref.shape[0]):
        out_ref[slab] = running.astype(BF16)
        running = decays[slab : slab + 1] * running + pay_ref[slab, :, :width].astype(F32)


def norm_tile(
    y_ref, bc_ref, g_ref, enter_ref, gate_ref, gain_ref, e_ref, normed_ref, carry, grown, i
):
    width = y_ref.shape[1]
    groups = bc_ref.shape[1] // (2 * STATE)
    gw = width // groups
    grown[...] = dot(g_ref[...], e_ref[...])
    for g in range(groups):
        at = slice(g * gw, (g + 1) * gw)
        carry[:, at] = dot(bc_ref[:, (groups + g) * STATE : (groups + g + 1) * STATE], enter_ref[:, at])
    size = y_ref.shape[0]
    for r in range(0, size, ROWS):
        rows = slice(r, r + ROWS)
        out_rows = pl.ds(pl.multiple_of(i * size + r, ROWS), ROWS)
        for g in range(groups):
            at = slice(g * gw, (g + 1) * gw)
            y = y_ref[rows, at].astype(F32) + grown[rows, at] * carry[rows, at]
            gated = y * silu(gate_ref[rows, at].astype(F32))
            square_mean = jnp.mean(gated * gated, axis=-1, keepdims=True)
            scaled = gated * lax.rsqrt(square_mean + epsilon) * gain_ref[:, at]
            normed_ref[out_rows, at] = scaled.astype(BF16)


def direct_kernel(
    where_ref, y_ref, bc_ref, g_ref, enter_ref, gate_ref, gain_ref, e_ref, w_ref, after_ref,
    *rest, tiles,
):
    *out_refs, normed_ref, carry, grown = rest
    i = pl.program_id(0)

    @pl.when(i < tiles)
    def _():
        norm_tile(
            y_ref, bc_ref, g_ref, enter_ref, gate_ref, gain_ref, e_ref, normed_ref, carry, grown, i
        )

    for k, out_ref in enumerate(out_refs):
        @pl.when(i == tiles + k)
        def _(out_ref=out_ref):
            out_ref[...] = dot(normed_ref[...], w_ref[...]).astype(BF16)


def line_kernel(
    y_ref, bc_ref, g_ref, enter_ref, gate_ref, gain_ref, e_ref, w_ref, after_ref,
    shares_ref, up_a_ref, up_b_ref, down_a_ref, down_b_ref, normed_ref, carry, grown, *, tiles,
):
    i = pl.program_id(0)

    @pl.when(i < tiles)
    def _():
        norm_tile(
            y_ref, bc_ref, g_ref, enter_ref, gate_ref, gain_ref, e_ref, normed_ref, carry, grown, i
        )

    @pl.when(i >= tiles)
    def _():
        shares_ref[0] = dot(normed_ref[...], w_ref[...]).astype(BF16)

    size = up_a_ref.shape[0]

    @pl.when(i == tiles)
    def _():
        down_a_ref[...] = shares_ref[0, :size]
        down_b_ref[...] = shares_ref[0, size:]

    @pl.when(i == pl.num_programs(0) - 1)
    def _():
        up_a_ref[...] = shares_ref[0, :size]
        up_b_ref[...] = shares_ref[0, size:]


def onward_kernel(where_ref, up_own_ref, down_own_ref, up_ref, down_ref, *rest):
    up_out, down_out = rest[-2:]
    up_out[...] = (up_own_ref[0].astype(F32) + up_ref[...].astype(F32)).astype(BF16)
    down_out[...] = (down_own_ref[0].astype(F32) + down_ref[...].astype(F32)).astype(BF16)


def final_kernel(where_ref, own_ref, up_ref, down_ref, *rest):
    out_ref = rest[-1]
    total = own_ref[0].astype(F32) + up_ref[...].astype(F32) + down_ref[...].astype(F32)
    out_ref[...] = total.astype(BF16)


def arrived_kernel(*refs):
    refs[-1][...] = jnp.zeros_like(refs[-1])


def direct_final_kernel(where_ref, normed_ref, w_ref, *refs, count):
    out_ref = refs[-1]
    total = dot(normed_ref[...], w_ref[...])
    for ref in refs[:count]:
        total = total + ref[...].astype(F32)
    out_ref[...] = total.astype(BF16)


def in_hbm(x):
    return pltpu.with_memory_space_constraint(x, pltpu.HBM)


def brief():
    return pl.CostEstimate(flops=1, transcendentals=0, bytes_accessed=1)


def params(limit=VMEM_LIMIT):
    return pltpu.CompilerParams(dimension_semantics=("arbitrary",), vmem_limit_bytes=limit)


def whole(shape):
    return pl.BlockSpec(shape, lambda *b: (0,) * len(shape))


def unread():
    return pl.BlockSpec(memory_space=pl.ANY)


def shaped(shape, dtype=BF16):
    return jax.ShapeDtypeStruct(shape, dtype)


def local(
    inner_input, state_maps, gate_input, step_input, log_decay_rate, step_bias,
    skip_gain, conv_kernel, map_kernel, norm_gain, out_weight,
):
    tokens, width = inner_input.shape
    groups = state_maps.shape[2]
    parts = 2 * groups
    heads = step_input.shape[1]
    blocks = tokens // BLK
    slabs = lax.axis_size("seq")
    chans = lax.axis_size("chan")
    features = out_weight.shape[1]
    map_width = parts * STATE
    low = spread(heads, width)

    tail = jnp.concatenate(
        [inner_input[tokens - HALO :], state_maps[tokens - HALO :].reshape(HALO, map_width)], 1
    )
    tail = lax.ppermute(tail, "seq", [(i, i + 1) for i in range(slabs - 1)])

    def lanes_at(count):
        return pl.BlockSpec((count, WIDE), lambda c: (0, c))

    xc, bc, bt, crow, cols, wrow, g_hl, pay = pl.pallas_call(
        states_kernel,
        grid=(width // WIDE,),
        in_specs=[
            lanes_at(tokens),
            whole((tokens * parts, STATE)),
            whole((heads, tokens)),
            lanes_at(HALO),
            pl.BlockSpec((HALO, map_width), lambda c: (0, width // map_width)),
            whole((1, heads)),
            whole((1, heads)),
            lanes_at(4),
            whole((4 * parts, STATE)),
            lanes_at(LANES),
        ],
        out_specs=[
            lanes_at(tokens),
            whole((tokens, map_width)),
            whole((groups, STATE, tokens)),
            whole((heads, tokens)),
            whole((tokens, LANES)),
            whole((heads, tokens)),
            whole((tokens, LANES)),
            whole((STATE, width + LANES)),
        ],
        out_shape=[
            shaped((tokens, width)),
            shaped((tokens, map_width)),
            shaped((groups, STATE, tokens)),
            shaped((heads, tokens), F32),
            shaped((tokens, LANES), F32),
            shaped((heads, tokens), F32),
            shaped((tokens, LANES)),
            shaped((STATE, width + LANES)),
        ],
        scratch_shapes=[
            pltpu.VMEM((tokens, WIDE), BF16),
            pltpu.VMEM((tokens, LANES), BF16),
            pltpu.VMEM((tokens, WIDE), F32),
        ],
        compiler_params=params(),
        name="states",
    )(
        inner_input, state_maps.reshape(tokens * parts, STATE), step_input.T, tail, tail,
        step_bias.reshape(1, heads), log_decay_rate.reshape(1, heads),
        conv_kernel, map_kernel.reshape(4 * parts, STATE), low,
    )

    part = STATE // slabs
    arrived = lax.all_to_all(
        pay.reshape(slabs, part, width + LANES), "seq", split_axis=0, concat_axis=0, tiled=True
    )

    def local_part(start, count, before, after):
        def tile(width):
            return pl.BlockSpec((BLK, width), lambda b: (start + b, 0))

        operands = [xc, bc, bt, crow, cols, wrow, skip_gain.reshape(1, heads)]
        specs = [
            tile(width),
            tile(map_width),
            pl.BlockSpec((groups, STATE, BLK), lambda b: (0, 0, start + b)),
            pl.BlockSpec((heads, BLK), lambda b: (0, start + b)),
            tile(LANES),
            pl.BlockSpec((heads, BLK), lambda b: (0, start + b)),
            pl.BlockSpec(memory_space=pltpu.SMEM),
        ]
        aliases = {}
        if before is not None:
            y, state = before
            aliases = {len(operands) + 1: 0}
            operands += [state, in_hbm(y)]
            specs += [whole((STATE, width)), unread()]
        operands.append(in_hbm(after))
        specs.append(unread())
        return pl.pallas_call(
            local_kernel,
            grid=(count,),
            in_specs=specs,
            out_specs=[tile(width), whole((STATE, width))],
            out_shape=[shaped((tokens, width)), shaped((STATE, width), F32)],
            input_output_aliases=aliases,
            compiler_params=params(),
            cost_estimate=brief(),
            name="local_part",
        )(*operands)

    some = blocks * 3 // 8
    y_first = local_part(0, some, None, pay)
    entering = pl.pallas_call(
        prefix_kernel,
        out_shape=shaped((slabs, part, width)),
        in_specs=[
            pl.BlockSpec(memory_space=pltpu.VMEM),
            pl.BlockSpec(memory_space=pltpu.VMEM),
            unread(),
        ],
        out_specs=pl.BlockSpec(memory_space=pltpu.VMEM),
        compiler_params=pltpu.CompilerParams(vmem_limit_bytes=SMALL_LIMIT),
        name="prefix",
    )(arrived, low, in_hbm(y_first[0]))
    y_second = local_part(some, some, y_first, entering)
    entering = lax.all_to_all(entering, "seq", split_axis=0, concat_axis=0, tiled=True)
    entering = entering.reshape(STATE, width)

    part_out = features // chans
    norm_row = norm_gain.reshape(1, width)
    mine = lax.axis_index("chan").astype(jnp.int32)
    where = mine.reshape(1)

    def norm_operands(start, count, tokens_each, y):
        def tile(width):
            return pl.BlockSpec((tokens_each, width), lambda i, *_: (start + jnp.minimum(i, count - 1), 0))

        operands = [y, bc, g_hl, entering, gate_input, norm_row, low]
        specs = [
            tile(width),
            tile(map_width),
            tile(LANES),
            whole((STATE, width)),
            tile(width),
            whole((1, width)),
            whole((LANES, width)),
        ]
        return operands, specs

    def project_direct(start, count, tokens_each, y, after, slots):
        operands, specs = norm_operands(start, count, tokens_each, y)
        size = count * tokens_each

        def weights(i, where):
            step = i - count
            slot = slots[-1]
            for k in range(len(slots) - 1, -1, -1):
                slot = jnp.where(step <= k, slots[k], slot)
            return (0, lax.rem(where[0] + slot, chans))

        return pl.pallas_call(
            functools.partial(direct_kernel, tiles=count),
            grid_spec=pltpu.PrefetchScalarGridSpec(
                num_scalar_prefetch=1,
                grid=(count + len(slots),),
                in_specs=specs + [pl.BlockSpec((width, part_out), weights), unread()],
                out_specs=[whole((size, part_out))] * len(slots) + [whole((size, width))],
                scratch_shapes=[pltpu.VMEM((tokens_each, width), F32)] * 2,
            ),
            out_shape=[shaped((size, part_out))] * len(slots) + [shaped((size, width))],
            compiler_params=params(),
            name="project_direct",
        )(where, *operands, out_weight, in_hbm(after))

    def direct_final(start, normed, pieces, after):
        def tile(width, start=0):
            return pl.BlockSpec((BLK, width), lambda i, where: (start + i, 0))

        return pl.pallas_call(
            functools.partial(direct_final_kernel, count=len(pieces)),
            grid_spec=pltpu.PrefetchScalarGridSpec(
                num_scalar_prefetch=1,
                grid=(normed.shape[0] // BLK,),
                in_specs=[
                    tile(width),
                    pl.BlockSpec((width, part_out), lambda i, where: (0, where[0])),
                ]
                + [tile(part_out)] * len(pieces)
                + [unread()],
                out_specs=tile(part_out, start),
            ),
            out_shape=shaped((tokens, part_out)),
            compiler_params=params(SMALL_LIMIT),
            name="direct_final",
        )(where, in_hbm(normed), in_hbm(out_weight), *pieces, after)

    def project_line(start, count, tokens_each, split, y, after):
        operands, specs = norm_operands(start, count, tokens_each, y)
        size = count * tokens_each

        def dest(i):
            return jnp.maximum(i - count, 0)

        return pl.pallas_call(
            functools.partial(line_kernel, tiles=count),
            grid=(count + chans,),
            in_specs=specs
            + [pl.BlockSpec((width, part_out), lambda i: (0, dest(i))), unread()],
            out_specs=[
                pl.BlockSpec((1, size, part_out), lambda i: (dest(i), 0, 0)),
            ]
            + [whole((k, part_out)) for k in split * 2],
            out_shape=[shaped((chans, size, part_out))] + [shaped((k, part_out)) for k in split * 2],
            scratch_shapes=[pltpu.VMEM((size, width), BF16)] + [pltpu.VMEM((tokens_each, width), F32)] * 2,
            compiler_params=params(),
            cost_estimate=brief(),
            name="project_line",
        )(*operands, out_weight, in_hbm(after))

    def permuted(up, down, s):
        up = lax.ppermute(up, "chan", [(a, a + 1) for a in range(s + 1)])
        down = lax.ppermute(down, "chan", [(a, a - 1) for a in range(chans - 1 - s, chans)])
        return up, down

    def onward(shares, half, up, down, s, after):
        count = up.shape[0] // BLK
        skipped = (shares.shape[1] // BLK - count) * half

        def plain(i, where):
            return (i, 0)

        return pl.pallas_call(
            onward_kernel,
            grid_spec=pltpu.PrefetchScalarGridSpec(
                num_scalar_prefetch=1,
                grid=(count,),
                in_specs=[
                    pl.BlockSpec(
                        (1, BLK, part_out),
                        lambda i, where: (
                            jnp.minimum(chans - 1 - s + where[0], chans - 1), skipped + i, 0
                        ),
                    ),
                    pl.BlockSpec(
                        (1, BLK, part_out),
                        lambda i, where: (
                            jnp.maximum(where[0] - (chans - 1) + s, 0), skipped + i, 0
                        ),
                    ),
                    pl.BlockSpec((BLK, part_out), plain),
                    pl.BlockSpec((BLK, part_out), plain),
                ]
                + [unread()] * len(after),
                out_specs=[pl.BlockSpec((BLK, part_out), plain)] * 2,
            ),
            out_shape=[shaped((count * BLK, part_out))] * 2,
            compiler_params=params(SMALL_LIMIT),
            name="onward",
        )(where, in_hbm(shares), in_hbm(shares), up, down, *after)

    def final(start, shares, half, up, down, out):
        count = up.shape[0] // BLK
        skipped = (shares.shape[1] // BLK - count) * half

        def plain(i, where):
            return (i, 0)

        operands = [where, in_hbm(shares), up, down]
        in_specs = [
            pl.BlockSpec((1, BLK, part_out), lambda i, where: (where[0], skipped + i, 0)),
            pl.BlockSpec((BLK, part_out), plain),
            pl.BlockSpec((BLK, part_out), plain),
        ]
        aliases = {}
        if out is not None:
            aliases = {len(operands): 0}
            operands.append(in_hbm(out))
            in_specs.append(unread())
        return pl.pallas_call(
            final_kernel,
            grid_spec=pltpu.PrefetchScalarGridSpec(
                num_scalar_prefetch=1,
                grid=(count,),
                in_specs=in_specs,
                out_specs=pl.BlockSpec((BLK, part_out), lambda i, where: (start + skipped + i, 0)),
            ),
            out_shape=shaped((tokens, part_out)),
            input_output_aliases=aliases,
            compiler_params=params(SMALL_LIMIT),
            name="final",
        )(*operands)

    lead = blocks * 3 // 8
    order = sorted(range(1, chans), key=lambda k: (min(k, chans - k), k))
    *slots, normed = project_direct(0, 2, lead * BLK // 2, y_second[0], y_second[1], order)
    pieces = []
    for k, slot in zip(order, slots):
        turn = [(a, (a + k) % chans) for a in range(chans)]
        pieces.append(lax.ppermute(slot, "chan", turn))

    y_third = local_part(2 * some, blocks - 2 * some, y_second, normed)
    rest = blocks - lead
    split = [(rest + 1) // 2 * BLK, rest // 2 * BLK]
    shares, up_a, up_b, down_a, down_b = project_line(
        lead, rest, BLK, split, y_third[0], normed
    )
    moving = [permuted(up_a, down_a, 0), permuted(up_b, down_b, 0)]
    mark = pl.pallas_call(
        arrived_kernel,
        in_specs=[unread()] * (len(pieces) + 1),
        out_specs=pl.BlockSpec(memory_space=pltpu.VMEM),
        out_shape=shaped((HALO, LANES), F32),
        compiler_params=pltpu.CompilerParams(vmem_limit_bytes=SMALL_LIMIT),
        cost_estimate=pl.CostEstimate(flops=20000000000, transcendentals=0, bytes_accessed=1),
        name="arrived",
    )(*pieces, in_hbm(shares))
    after = [mark]
    for s in range(1, chans - 1):
        for k in range(2):
            up, down = onward(shares, k, *moving[k], s, after)
            after = [up]
            moving[k] = permuted(up, down, s)
        if s == 1:
            out = direct_final(0, normed, pieces, up)
            after = [in_hbm(out)]
    for k in range(2):
        out = final(lead, shares, k, *moving[k], out)
    return out


def solution(mesh):
    return jax.shard_map(
        local,
        mesh=mesh,
        in_specs=(
            P("seq", "chan"),
            P("seq", None, "chan", None),
            P("seq", "chan"),
            P("seq", "chan"),
            P("chan"),
            P("chan"),
            P("chan"),
            P(None, "chan"),
            P(None, None, "chan", None),
            P("chan"),
            P("chan", None),
        ),
        out_specs=P("seq", "chan"),
        check_vma=False,
    )
```

```python
import functools
import math

import jax
import jax.numpy as jnp
import numpy as np
from jax import lax
from jax.experimental import pallas as pl
from jax.experimental.pallas import tpu as pltpu
from jax.sharding import PartitionSpec as P

HEAD_DIM = 64
STATE = 128
BLK = 128
LANES = 128
HALO = 8
ROWS = 16
WIDE = 512

step_limit = 0.5
epsilon = 1e-05
LOG2E = 1.4426950408889634
F32 = jnp.float32
BF16 = jnp.bfloat16
VMEM_LIMIT = 58 * 1024 * 1024
SMALL_LIMIT = 10 * 1024 * 1024


def silu(v):
    half = 0.5 * v
    return half + half * jnp.tanh(half)


def high_low(v):
    high = v.astype(BF16).astype(F32)
    return high, v - high


def spread(heads, width):
    result = np.zeros((LANES, width), np.float32)
    for k in range(2 * heads):
        h = k % heads
        result[k, h * HEAD_DIM : (h + 1) * HEAD_DIM] = 1.0
    return jnp.asarray(result, BF16)


def dot(a, b):
    return jnp.dot(a, b, preferred_element_type=F32)


def dot_t(a, b):
    return lax.dot_general(a, b, (((1,), (1,)), ((), ())), preferred_element_type=F32)


def column(row):
    count = row.shape[1]
    eye = lax.broadcasted_iota(jnp.int32, (count, count), 0) == lax.broadcasted_iota(
        jnp.int32, (count, count), 1
    )
    return jnp.sum(jnp.where(eye, row, 0.0), axis=1, keepdims=True)


def padded(pieces):
    rows = jnp.concatenate(pieces, 0)
    if rows.shape[0] == LANES:
        return rows
    return jnp.concatenate([rows, jnp.zeros((LANES - rows.shape[0], rows.shape[1]), rows.dtype)], 0)


def conv(before, cur, taps):
    full = jnp.concatenate([before, cur], 0)
    late = pltpu.roll(full, 1, 0)
    early = taps[1] * full + taps[0] * late
    acc = taps[3] * cur + taps[2] * late[HALO:] + pltpu.roll(early, 2, 0)[HALO:]
    return silu(acc)


def states_kernel(
    x_ref, maps_ref, step_ref, tail_ref, mtail_ref, bias_ref, rate_ref, ck_ref, mk_ref, e_ref,
    xc_ref, pay_ref, *rest,
):
    outs, (bc_ref, bt_ref, crow_ref, cols_ref, wrow_ref, g_ref) = rest[:6], rest[6:12]
    weighted, w_ref, scale, sems = rest[12:]
    copies = [
        pltpu.make_async_copy(kept, out, sems.at[k])
        for k, (kept, out) in enumerate(zip(rest[6:12], outs))
    ]
    c = pl.program_id(0)
    heads, tokens = step_ref.shape
    parts = mk_ref.shape[0] // 4
    groups = parts // 2
    blocks = tokens // BLK

    @pl.when(c == 0)
    def _():
        bias, rate = column(bias_ref[...]), -jnp.exp(column(rate_ref[...]))
        v = step_ref[...] + bias
        step = jnp.minimum(jnp.maximum(v, 0.0) + jnp.log1p(jnp.exp(-jnp.abs(v))), step_limit)
        log_step = rate * step
        first, rest = high_low(log_step)
        second, third = high_low(rest)
        pieces = []
        for b in range(blocks):
            at = slice(b * BLK, (b + 1) * BLK)
            pieces += [first[:, at], second[:, at], third[:, at]]
        row = lax.broadcasted_iota(jnp.int32, (BLK, BLK), 0)
        col = lax.broadcasted_iota(jnp.int32, (BLK, BLK), 1)
        tri = jnp.where(row <= col, 1.0, 0.0).astype(BF16)
        sums = dot(jnp.concatenate(pieces, 0).astype(BF16), tri)
        cums, leads = [], [jnp.zeros((heads, 1), F32)]
        for b in range(blocks):
            at = 3 * b * heads
            cum = (
                sums[at : at + heads]
                + sums[at + heads : at + 2 * heads]
                + sums[at + 2 * heads : at + 3 * heads]
            )
            cums.append(cum)
            leads.append(leads[-1] + cum[:, BLK - 1 : BLK])
        last = None
        for b in range(blocks):
            at = slice(b * BLK, (b + 1) * BLK)
            cum, step_b = cums[b], step[:, at]
            total = cum[:, BLK - 1 : BLK]
            wrow_ref[:, at] = jnp.exp(total - cum) * step_b
            slab_weight = jnp.exp(leads[blocks] - (leads[b] + cum)) * step_b
            entered = jnp.exp(cum + leads[b])
            crow_ref[:, at] = (cum - jnp.log(step_b)) * LOG2E
            w_ref[at, :] = padded(high_low(slab_weight)).T.astype(BF16)
            last = padded(high_low(entered)).T
            g_ref[at, :] = last.astype(BF16)
            cols_ref[at, :] = padded((cum * LOG2E,)).T
        pay_ref[:, heads * HEAD_DIM :] = jnp.broadcast_to(last[BLK - 1 :], (STATE, LANES)).astype(BF16)

        few = BLK // 2
        row = lax.broadcasted_iota(jnp.int32, (few * parts, few * parts), 0)
        col = lax.broadcasted_iota(jnp.int32, (few * parts, few * parts), 1)
        source = (row & (few - 1)) * parts + row // few
        pick = jnp.where(col == source, 1.0, 0.0).astype(BF16)
        before = [mtail_ref[:, q * STATE : (q + 1) * STATE].astype(F32) for q in range(parts)]
        for b in range(blocks):
            at = 2 * b * few * parts
            mixed = [maps_ref[at + k * few * parts : at + (k + 1) * few * parts] for k in range(2)]
            ordered = dot(pick, jnp.concatenate(mixed, 1))
            for q in range(parts):
                own = ordered[q * few : (q + 1) * few]
                cur = jnp.concatenate([own[:, :STATE], own[:, STATE:]], 0)
                taps = [mk_ref[k * parts + q : k * parts + q + 1] for k in range(4)]
                result = conv(before[q], cur, taps).astype(BF16)
                before[q] = cur[BLK - HALO :]
                bc_ref[b * BLK : (b + 1) * BLK, q * STATE : (q + 1) * STATE] = result
                if q < groups:
                    bt_ref[q, :, b * BLK : (b + 1) * BLK] = result.astype(F32).T.astype(BF16)

        for copy in copies:
            copy.start()

    scale[...] = dot(w_ref[...], e_ref[...])
    for lane in range(0, x_ref.shape[1], LANES):
        at_lanes = slice(lane, lane + LANES)
        taps = [ck_ref[k : k + 1, at_lanes] for k in range(4)]
        before = tail_ref[:, at_lanes].astype(F32)
        for b in range(blocks):
            at = slice(b * BLK, (b + 1) * BLK)
            cur = x_ref[at, at_lanes].astype(F32)
            result = conv(before, cur, taps)
            before = cur[BLK - HALO :]
            xc_ref[at, at_lanes] = result.astype(BF16)
            weighted[at, at_lanes] = (result * scale[at, at_lanes]).astype(BF16)
    step_width = x_ref.shape[1]
    group = c * step_width * groups // (heads * HEAD_DIM)
    at = pl.ds(pl.multiple_of(c * step_width, step_width), step_width)
    pay_ref[:, at] = dot(bt_ref[group], weighted[...]).astype(BF16)

    @pl.when(c == pl.num_programs(0) - 1)
    def _():
        for copy in copies:
            copy.wait()


def local_kernel(xc_ref, bc_ref, bt_ref, crow_ref, cols_ref, wrow_ref, skip_ref, *rest):
    y_ref, state = rest[-2:]
    width = xc_ref.shape[1]
    groups = bt_ref.shape[0]
    gw = width // groups

    @pl.when(pl.program_id(0) == 0)
    def _():
        state[...] = rest[0][...] if len(rest) > 3 else jnp.zeros_like(state)

    left = lax.broadcasted_iota(jnp.int32, (BLK, LANES), 1) < HEAD_DIM
    row = lax.broadcasted_iota(jnp.int32, (BLK, BLK), 0)
    causal = row >= lax.broadcasted_iota(jnp.int32, (BLK, BLK), 1)
    for g in range(groups):
        b_g = bc_ref[:, g * STATE : (g + 1) * STATE]
        c_g = bc_ref[:, (groups + g) * STATE : (groups + g + 1) * STATE]
        scores = jnp.where(causal, dot_t(c_g, b_g), 0.0)
        b_t = bt_ref[g].astype(F32)
        for wide in range(g * gw, (g + 1) * gw, 2 * LANES):
            before = state[:, wide : wide + 2 * LANES]
            carry = dot(c_g, before.astype(BF16))
            for k in range(2):
                at = slice(wide + k * LANES, wide + (k + 1) * LANES)
                part = slice(k * LANES, (k + 1) * LANES)
                first = at.start // HEAD_DIM
                mixing, weighted, cums = [], [], []
                for h in (first, first + 1):
                    cum = jnp.broadcast_to(cols_ref[:, h : h + 1], (BLK, BLK))
                    gap = jnp.minimum(cum - crow_ref[h : h + 1], 0.0)
                    mixing.append((jnp.exp2(gap) * scores).astype(BF16))
                    weighted.append((b_t * wrow_ref[h : h + 1]).astype(BF16))
                    cums.append(cum)
                x = xc_ref[:, at]
                nil = jnp.zeros_like(x)
                stacked = jnp.concatenate([jnp.where(left, x, nil), jnp.where(left, nil, x)], 0)
                both = jnp.concatenate(
                    [jnp.concatenate(mixing, 1), jnp.concatenate(weighted, 1)], 0
                )
                result = dot(both, stacked)
                grown = jnp.exp2(jnp.where(left, cums[0], cums[1]))
                skip = jnp.where(left, skip_ref[0, first], skip_ref[0, first + 1])
                y = result[:BLK] + grown * carry[:, part] + skip * x.astype(F32)
                y_ref[:, at] = y.astype(BF16)
                state[:, at] = grown[BLK - 1 :] * before[:, part] + result[BLK:]


def prefix_kernel(pay_ref, e_ref, after_ref, out_ref):
    width = out_ref.shape[2]
    decays = dot(pay_ref[:, 0, width:], e_ref[...])
    running = jnp.zeros(out_ref.shape[1:], F32)
    for slab in range(out_ref.shape[0]):
        out_ref[slab] = running.astype(BF16)
        running = decays[slab : slab + 1] * running + pay_ref[slab, :, :width].astype(F32)


def norm_tile(
    y_ref, bc_ref, g_ref, enter_ref, gate_ref, gain_ref, e_ref, normed_ref, carry, grown, i
):
    width = y_ref.shape[1]
    groups = bc_ref.shape[1] // (2 * STATE)
    gw = width // groups
    grown[...] = dot(g_ref[...], e_ref[...])
    for g in range(groups):
        at = slice(g * gw, (g + 1) * gw)
        carry[:, at] = dot(bc_ref[:, (groups + g) * STATE : (groups + g + 1) * STATE], enter_ref[:, at])
    size = y_ref.shape[0]
    for r in range(0, size, ROWS):
        rows = slice(r, r + ROWS)
        out_rows = pl.ds(pl.multiple_of(i * size + r, ROWS), ROWS)
        for g in range(groups):
            at = slice(g * gw, (g + 1) * gw)
            y = y_ref[rows, at].astype(F32) + grown[rows, at] * carry[rows, at]
            gated = y * silu(gate_ref[rows, at].astype(F32))
            square_mean = jnp.mean(gated * gated, axis=-1, keepdims=True)
            scaled = gated * lax.rsqrt(square_mean + epsilon) * gain_ref[:, at]
            normed_ref[out_rows, at] = scaled.astype(BF16)


def direct_kernel(
    where_ref, y_ref, bc_ref, g_ref, enter_ref, gate_ref, gain_ref, e_ref, w_ref, after_ref,
    *rest, tiles,
):
    *out_refs, normed_ref, carry, grown = rest
    i = pl.program_id(0)

    @pl.when(i < tiles)
    def _():
        norm_tile(
            y_ref, bc_ref, g_ref, enter_ref, gate_ref, gain_ref, e_ref, normed_ref, carry, grown, i
        )

    for k, out_ref in enumerate(out_refs):
        @pl.when(i == tiles + k)
        def _(out_ref=out_ref):
            out_ref[...] = dot(normed_ref[...], w_ref[...]).astype(BF16)


def ends_kernel(
    y_ref, bc_ref, g_ref, enter_ref, gate_ref, gain_ref, e_ref, w_ref, after_ref,
    shares_ref, up_ref, down_ref, normed_ref, carry, grown, *, tiles,
):
    i = pl.program_id(0)

    @pl.when(i < tiles)
    def _():
        norm_tile(
            y_ref, bc_ref, g_ref, enter_ref, gate_ref, gain_ref, e_ref, normed_ref, carry, grown, i
        )

    @pl.when(i >= tiles)
    def _():
        shares_ref[0] = dot(normed_ref[...], w_ref[...]).astype(BF16)

    @pl.when(i == tiles)
    def _():
        down_ref[...] = shares_ref[0]

    @pl.when(i == tiles + 1)
    def _():
        up_ref[...] = shares_ref[0]


def middle_kernel(normed_ref, w_ref, ends_ref, shares_ref):
    shares_ref[0] = dot(normed_ref[...], w_ref[...]).astype(BF16)


def onward_kernel(where_ref, up_own_ref, down_own_ref, up_ref, down_ref, *rest):
    up_out, down_out = rest[-2:]
    up_out[...] = (up_own_ref[0].astype(F32) + up_ref[...].astype(F32)).astype(BF16)
    down_out[...] = (down_own_ref[0].astype(F32) + down_ref[...].astype(F32)).astype(BF16)


def final_kernel(where_ref, own_ref, up_ref, down_ref, *rest):
    out_ref = rest[-1]
    total = own_ref[0].astype(F32) + up_ref[...].astype(F32) + down_ref[...].astype(F32)
    out_ref[...] = total.astype(BF16)


def arrived_kernel(*refs):
    refs[-1][...] = jnp.zeros_like(refs[-1])


def direct_final_kernel(where_ref, normed_ref, w_ref, *refs, count):
    out_ref = refs[-1]
    total = dot(normed_ref[...], w_ref[...])
    for ref in refs[:count]:
        total = total + ref[...].astype(F32)
    out_ref[...] = total.astype(BF16)


def in_hbm(x):
    return pltpu.with_memory_space_constraint(x, pltpu.HBM)


def brief():
    return pl.CostEstimate(flops=1, transcendentals=0, bytes_accessed=1)


def params(limit=VMEM_LIMIT):
    return pltpu.CompilerParams(dimension_semantics=("arbitrary",), vmem_limit_bytes=limit)


def whole(shape):
    return pl.BlockSpec(shape, lambda *b: (0,) * len(shape))


def unread():
    return pl.BlockSpec(memory_space=pl.ANY)


def shaped(shape, dtype=BF16):
    return jax.ShapeDtypeStruct(shape, dtype)


def local(
    inner_input, state_maps, gate_input, step_input, log_decay_rate, step_bias,
    skip_gain, conv_kernel, map_kernel, norm_gain, out_weight,
):
    tokens, width = inner_input.shape
    groups = state_maps.shape[2]
    parts = 2 * groups
    heads = step_input.shape[1]
    blocks = tokens // BLK
    slabs = lax.axis_size("seq")
    chans = lax.axis_size("chan")
    features = out_weight.shape[1]
    map_width = parts * STATE
    low = spread(heads, width)

    tail = jnp.concatenate(
        [inner_input[tokens - HALO :], state_maps[tokens - HALO :].reshape(HALO, map_width)], 1
    )
    tail = lax.ppermute(tail, "seq", [(i, i + 1) for i in range(slabs - 1)])

    def lanes_at(count):
        return pl.BlockSpec((count, WIDE), lambda c: (0, c))

    kept = [
        ((tokens, map_width), BF16),
        ((groups, STATE, tokens), BF16),
        ((heads, tokens), F32),
        ((tokens, LANES), F32),
        ((heads, tokens), F32),
        ((tokens, LANES), BF16),
    ]
    xc, pay, bc, bt, crow, cols, wrow, g_hl = pl.pallas_call(
        states_kernel,
        grid=(width // WIDE,),
        in_specs=[
            lanes_at(tokens),
            whole((tokens * parts, STATE)),
            whole((heads, tokens)),
            lanes_at(HALO),
            pl.BlockSpec((HALO, map_width), lambda c: (0, width // map_width)),
            whole((1, heads)),
            whole((1, heads)),
            lanes_at(4),
            whole((4 * parts, STATE)),
            lanes_at(LANES),
        ],
        out_specs=[lanes_at(tokens), whole((STATE, width + LANES))] + [unread()] * 6,
        out_shape=[shaped((tokens, width)), shaped((STATE, width + LANES))]
        + [shaped(*k) for k in kept],
        scratch_shapes=[pltpu.VMEM(*k) for k in kept]
        + [
            pltpu.VMEM((tokens, WIDE), BF16),
            pltpu.VMEM((tokens, LANES), BF16),
            pltpu.VMEM((tokens, WIDE), F32),
            pltpu.SemaphoreType.DMA((6,)),
        ],
        compiler_params=params(),
        name="states",
    )(
        inner_input, state_maps.reshape(tokens * parts, STATE), step_input.T, tail, tail,
        step_bias.reshape(1, heads), log_decay_rate.reshape(1, heads),
        conv_kernel, map_kernel.reshape(4 * parts, STATE), low,
    )

    part = STATE // slabs
    arrived = lax.all_to_all(
        pay.reshape(slabs, part, width + LANES), "seq", split_axis=0, concat_axis=0, tiled=True
    )

    def local_part(start, count, before, after):
        def tile(width):
            return pl.BlockSpec((BLK, width), lambda b: (start + b, 0))

        operands = [xc, bc, bt, crow, cols, wrow, skip_gain.reshape(1, heads)]
        specs = [
            tile(width),
            tile(map_width),
            pl.BlockSpec((groups, STATE, BLK), lambda b: (0, 0, start + b)),
            pl.BlockSpec((heads, BLK), lambda b: (0, start + b)),
            tile(LANES),
            pl.BlockSpec((heads, BLK), lambda b: (0, start + b)),
            pl.BlockSpec(memory_space=pltpu.SMEM),
        ]
        aliases = {}
        if before is not None:
            y, state = before
            aliases = {len(operands) + 1: 0}
            operands += [state, in_hbm(y)]
            specs += [whole((STATE, width)), unread()]
        operands.append(in_hbm(after))
        specs.append(unread())
        return pl.pallas_call(
            local_kernel,
            grid=(count,),
            in_specs=specs,
            out_specs=[tile(width), whole((STATE, width))],
            out_shape=[shaped((tokens, width)), shaped((STATE, width), F32)],
            input_output_aliases=aliases,
            compiler_params=params(),
            cost_estimate=brief(),
            name="local_part",
        )(*operands)

    some = blocks * 3 // 8
    y_first = local_part(0, some, None, pay)
    entering = pl.pallas_call(
        prefix_kernel,
        out_shape=shaped((slabs, part, width)),
        in_specs=[
            pl.BlockSpec(memory_space=pltpu.VMEM),
            pl.BlockSpec(memory_space=pltpu.VMEM),
            unread(),
        ],
        out_specs=pl.BlockSpec(memory_space=pltpu.VMEM),
        compiler_params=pltpu.CompilerParams(vmem_limit_bytes=SMALL_LIMIT),
        name="prefix",
    )(arrived, low, in_hbm(y_first[0]))
    y_second = local_part(some, some, y_first, entering)
    entering = lax.all_to_all(entering, "seq", split_axis=0, concat_axis=0, tiled=True)
    entering = entering.reshape(STATE, width)

    part_out = features // chans
    norm_row = norm_gain.reshape(1, width)
    mine = lax.axis_index("chan").astype(jnp.int32)
    where = mine.reshape(1)

    def norm_operands(start, count, tokens_each, y):
        def tile(width):
            return pl.BlockSpec((tokens_each, width), lambda i, *_: (start + jnp.minimum(i, count - 1), 0))

        operands = [y, bc, g_hl, entering, gate_input, norm_row, low]
        specs = [
            tile(width),
            tile(map_width),
            tile(LANES),
            whole((STATE, width)),
            tile(width),
            whole((1, width)),
            whole((LANES, width)),
        ]
        return operands, specs

    def project_direct(start, count, tokens_each, y, after, slots):
        operands, specs = norm_operands(start, count, tokens_each, y)
        size = count * tokens_each

        def weights(i, where):
            step = i - count
            slot = slots[-1]
            for k in range(len(slots) - 1, -1, -1):
                slot = jnp.where(step <= k, slots[k], slot)
            return (0, lax.rem(where[0] + slot, chans))

        return pl.pallas_call(
            functools.partial(direct_kernel, tiles=count),
            grid_spec=pltpu.PrefetchScalarGridSpec(
                num_scalar_prefetch=1,
                grid=(count + len(slots),),
                in_specs=specs + [pl.BlockSpec((width, part_out), weights), unread()],
                out_specs=[whole((size, part_out))] * len(slots) + [whole((size, width))],
                scratch_shapes=[pltpu.VMEM((tokens_each, width), F32)] * 2,
            ),
            out_shape=[shaped((size, part_out))] * len(slots) + [shaped((size, width))],
            compiler_params=params(),
            name="project_direct",
        )(where, *operands, out_weight, in_hbm(after))

    def direct_final(start, normed, pieces, after):
        def tile(width, start=0):
            return pl.BlockSpec((BLK, width), lambda i, where: (start + i, 0))

        return pl.pallas_call(
            functools.partial(direct_final_kernel, count=len(pieces)),
            grid_spec=pltpu.PrefetchScalarGridSpec(
                num_scalar_prefetch=1,
                grid=(normed.shape[0] // BLK,),
                in_specs=[
                    tile(width),
                    pl.BlockSpec((width, part_out), lambda i, where: (0, where[0])),
                ]
                + [tile(part_out)] * len(pieces)
                + [unread()],
                out_specs=tile(part_out, start),
            ),
            out_shape=shaped((tokens, part_out)),
            compiler_params=params(SMALL_LIMIT),
            name="direct_final",
        )(where, in_hbm(normed), in_hbm(out_weight), *pieces, after)

    def project_ends(start, count, tokens_each, y, after):
        operands, specs = norm_operands(start, count, tokens_each, y)
        size = count * tokens_each

        def dest(i):
            return jnp.where(i <= count, 0, chans - 1)

        return pl.pallas_call(
            functools.partial(ends_kernel, tiles=count),
            grid=(count + 2,),
            in_specs=specs
            + [pl.BlockSpec((width, part_out), lambda i: (0, dest(i))), unread()],
            out_specs=[
                pl.BlockSpec((1, size, part_out), lambda i: (dest(i), 0, 0)),
                whole((size, part_out)),
                whole((size, part_out)),
                whole((size, width)),
            ],
            out_shape=[
                shaped((chans, size, part_out)),
                shaped((size, part_out)),
                shaped((size, part_out)),
                shaped((size, width)),
            ],
            scratch_shapes=[pltpu.VMEM((tokens_each, width), F32)] * 2,
            compiler_params=params(),
            cost_estimate=brief(),
            name="project_ends",
        )(*operands, out_weight, in_hbm(after))

    def project_middle(shares, normed):
        size = normed.shape[0]
        return pl.pallas_call(
            middle_kernel,
            grid=(chans - 2,),
            in_specs=[
                whole((size, width)),
                pl.BlockSpec((width, part_out), lambda i: (0, i + 1)),
                unread(),
            ],
            out_specs=pl.BlockSpec((1, size, part_out), lambda i: (i + 1, 0, 0)),
            out_shape=shaped((chans, size, part_out)),
            input_output_aliases={2: 0},
            compiler_params=params(),
            cost_estimate=brief(),
            name="project_middle",
        )(normed, out_weight, in_hbm(shares))

    def permuted(up, down, s):
        up = lax.ppermute(up, "chan", [(a, a + 1) for a in range(s + 1)])
        down = lax.ppermute(down, "chan", [(a, a - 1) for a in range(chans - 1 - s, chans)])
        return up, down

    def onward(shares, part, up, down, s, after):
        first, count = part
        tile = math.gcd(first, count) if first else count
        skipped = first // tile
        held = skipped if s == 1 else 0

        def plain(i, where):
            return (i, 0)

        def arrived(i, where):
            return (held + i, 0)

        def own(index):
            return pl.BlockSpec(
                (1, tile, part_out), lambda i, where: (index(where[0]), skipped + i, 0)
            )

        return pl.pallas_call(
            onward_kernel,
            grid_spec=pltpu.PrefetchScalarGridSpec(
                num_scalar_prefetch=1,
                grid=(count // tile,),
                in_specs=[
                    own(lambda me: jnp.minimum(chans - 1 - s + me, chans - 1)),
                    own(lambda me: jnp.maximum(me - (chans - 1) + s, 0)),
                    pl.BlockSpec((tile, part_out), arrived),
                    pl.BlockSpec((tile, part_out), arrived),
                ]
                + [unread()] * len(after),
                out_specs=[pl.BlockSpec((tile, part_out), plain)] * 2,
            ),
            out_shape=[shaped((count, part_out))] * 2,
            compiler_params=params(SMALL_LIMIT),
            name="onward",
        )(where, in_hbm(shares), in_hbm(shares), up, down, *after)

    def final(start, shares, part, up, down, out):
        count, skipped = part[1] // BLK, part[0] // BLK

        def plain(i, where):
            return (i, 0)

        operands = [where, in_hbm(shares), up, down]
        in_specs = [
            pl.BlockSpec((1, BLK, part_out), lambda i, where: (where[0], skipped + i, 0)),
            pl.BlockSpec((BLK, part_out), plain),
            pl.BlockSpec((BLK, part_out), plain),
        ]
        aliases = {}
        if out is not None:
            aliases = {len(operands): 0}
            operands.append(in_hbm(out))
            in_specs.append(unread())
        return pl.pallas_call(
            final_kernel,
            grid_spec=pltpu.PrefetchScalarGridSpec(
                num_scalar_prefetch=1,
                grid=(count,),
                in_specs=in_specs,
                out_specs=pl.BlockSpec((BLK, part_out), lambda i, where: (start + skipped + i, 0)),
            ),
            out_shape=shaped((tokens, part_out)),
            input_output_aliases=aliases,
            compiler_params=params(SMALL_LIMIT),
            name="final",
        )(*operands)

    lead = blocks * 3 // 8
    order = sorted(range(1, chans), key=lambda k: (min(k, chans - k), k))
    *slots, normed = project_direct(0, 2, lead * BLK // 2, y_second[0], y_second[1], order)
    pieces = []
    for k, slot in zip(order, slots):
        turn = [(a, (a + k) % chans) for a in range(chans)]
        pieces.append(lax.ppermute(slot, "chan", turn))

    y_third = local_part(2 * some, blocks - 2 * some, y_second, normed)
    rest = blocks - lead
    some = (rest + 1) // 2 * BLK
    parts_of = [(0, some), (some, rest * BLK - some)]
    shares, up, down, line_normed = project_ends(lead, rest, BLK, y_third[0], normed)
    moving = [permuted(up, down, 0)] * 2
    shares = project_middle(shares, line_normed)
    mark = pl.pallas_call(
        arrived_kernel,
        in_specs=[unread()] * (len(pieces) + 1),
        out_specs=pl.BlockSpec(memory_space=pltpu.VMEM),
        out_shape=shaped((HALO, LANES), F32),
        compiler_params=pltpu.CompilerParams(vmem_limit_bytes=SMALL_LIMIT),
        cost_estimate=pl.CostEstimate(flops=20000000000, transcendentals=0, bytes_accessed=1),
        name="arrived",
    )(*pieces, in_hbm(shares))
    after = [mark]
    for s in range(1, chans - 1):
        for k in range(2):
            up, down = onward(shares, parts_of[k], *moving[k], s, after)
            after = [up]
            moving[k] = permuted(up, down, s)
        if s == 1:
            out = direct_final(0, normed, pieces, up)
            after = [in_hbm(out)]
    for k in range(2):
        out = final(lead, shares, parts_of[k], *moving[k], out)
    return out


def solution(mesh):
    return jax.shard_map(
        local,
        mesh=mesh,
        in_specs=(
            P("seq", "chan"),
            P("seq", None, "chan", None),
            P("seq", "chan"),
            P("seq", "chan"),
            P("chan"),
            P("chan"),
            P("chan"),
            P(None, "chan"),
            P(None, None, "chan", None),
            P("chan"),
            P("chan", None),
        ),
        out_specs=P("seq", "chan"),
        check_vma=False,
    )
```

```python
import functools
import math

import jax
import jax.numpy as jnp
import numpy as np
from jax import lax
from jax.experimental import pallas as pl
from jax.experimental.pallas import tpu as pltpu
from jax.sharding import PartitionSpec as P

HEAD_DIM = 64
STATE = 128
BLK = 128
LANES = 128
HALO = 8
ROWS = 16
WIDE = 512

step_limit = 0.5
epsilon = 1e-05
LOG2E = 1.4426950408889634
F32 = jnp.float32
BF16 = jnp.bfloat16
VMEM_LIMIT = 40 * 1024 * 1024
SMALL_LIMIT = 10 * 1024 * 1024


def silu(v):
    half = 0.5 * v
    return half + half * jnp.tanh(half)


def high_low(v):
    high = v.astype(BF16).astype(F32)
    return high, v - high


def spread(heads, width):
    result = np.zeros((LANES, width), np.float32)
    for k in range(2 * heads):
        h = k % heads
        result[k, h * HEAD_DIM : (h + 1) * HEAD_DIM] = 1.0
    return jnp.asarray(result, BF16)


def dot(a, b):
    return jnp.dot(a, b, preferred_element_type=F32)


def dot_t(a, b):
    return lax.dot_general(a, b, (((1,), (1,)), ((), ())), preferred_element_type=F32)


def column(row):
    count = row.shape[1]
    eye = lax.broadcasted_iota(jnp.int32, (count, count), 0) == lax.broadcasted_iota(
        jnp.int32, (count, count), 1
    )
    return jnp.sum(jnp.where(eye, row, 0.0), axis=1, keepdims=True)


def padded(pieces):
    rows = jnp.concatenate(pieces, 0)
    if rows.shape[0] == LANES:
        return rows
    return jnp.concatenate([rows, jnp.zeros((LANES - rows.shape[0], rows.shape[1]), rows.dtype)], 0)


def conv(before, cur, taps):
    full = jnp.concatenate([before, cur], 0)
    late = pltpu.roll(full, 1, 0)
    early = taps[1] * full + taps[0] * late
    acc = taps[3] * cur + taps[2] * late[HALO:] + pltpu.roll(early, 2, 0)[HALO:]
    return silu(acc)


def states_kernel(
    x_ref, maps_ref, step_ref, tail_ref, mtail_ref, bias_ref, rate_ref, ck_ref, mk_ref, e_ref,
    xc_ref, pay_ref, *rest,
):
    outs, (bc_ref, bt_ref, crow_ref, cols_ref, wrow_ref, g_ref) = rest[:6], rest[6:12]
    weighted, w_ref, scale, plain, early, sems = rest[12:]
    copies = [
        pltpu.make_async_copy(kept, out, sems.at[k])
        for k, (kept, out) in enumerate(zip(rest[6:12], outs))
    ]
    c = pl.program_id(0)
    heads, tokens = step_ref.shape
    parts = mk_ref.shape[0] // 4
    groups = parts // 2
    blocks = tokens // BLK

    @pl.when(c == 0)
    def _():
        bias, rate = column(bias_ref[...]), -jnp.exp(column(rate_ref[...]))
        v = step_ref[...] + bias
        step = jnp.minimum(jnp.maximum(v, 0.0) + jnp.log1p(jnp.exp(-jnp.abs(v))), step_limit)
        log_step = rate * step
        first, rest = high_low(log_step)
        second, third = high_low(rest)
        pieces = []
        for b in range(blocks):
            at = slice(b * BLK, (b + 1) * BLK)
            pieces += [first[:, at], second[:, at], third[:, at]]
        row = lax.broadcasted_iota(jnp.int32, (BLK, BLK), 0)
        col = lax.broadcasted_iota(jnp.int32, (BLK, BLK), 1)
        tri = jnp.where(row <= col, 1.0, 0.0).astype(BF16)
        sums = dot(jnp.concatenate(pieces, 0).astype(BF16), tri)
        cums, leads = [], [jnp.zeros((heads, 1), F32)]
        for b in range(blocks):
            at = 3 * b * heads
            cum = (
                sums[at : at + heads]
                + sums[at + heads : at + 2 * heads]
                + sums[at + 2 * heads : at + 3 * heads]
            )
            cums.append(cum)
            leads.append(leads[-1] + cum[:, BLK - 1 : BLK])
        last = None
        for b in range(blocks):
            at = slice(b * BLK, (b + 1) * BLK)
            cum, step_b = cums[b], step[:, at]
            total = cum[:, BLK - 1 : BLK]
            wrow_ref[:, at] = jnp.exp(total - cum) * step_b
            slab_weight = jnp.exp(leads[blocks] - (leads[b] + cum)) * step_b
            entered = jnp.exp(cum + leads[b])
            crow_ref[:, at] = (cum - jnp.log(step_b)) * LOG2E
            w_ref[at, :] = padded(high_low(slab_weight)).T.astype(BF16)
            last = padded(high_low(entered)).T
            g_ref[at, :] = last.astype(BF16)
            cols_ref[at, :] = padded((cum * LOG2E,)).T
        pay_ref[:, heads * HEAD_DIM :] = jnp.broadcast_to(last[BLK - 1 :], (STATE, LANES)).astype(BF16)

        few = BLK // 2
        row = lax.broadcasted_iota(jnp.int32, (few * parts, few * parts), 0)
        col = lax.broadcasted_iota(jnp.int32, (few * parts, few * parts), 1)
        source = (row & (few - 1)) * parts + row // few
        pick = jnp.where(col == source, 1.0, 0.0).astype(BF16)
        before = [mtail_ref[:, q * STATE : (q + 1) * STATE].astype(F32) for q in range(parts)]
        for b in range(blocks):
            at = 2 * b * few * parts
            mixed = [maps_ref[at + k * few * parts : at + (k + 1) * few * parts] for k in range(2)]
            ordered = dot(pick, jnp.concatenate(mixed, 1))
            for q in range(parts):
                own = ordered[q * few : (q + 1) * few]
                cur = jnp.concatenate([own[:, :STATE], own[:, STATE:]], 0)
                taps = [mk_ref[k * parts + q : k * parts + q + 1] for k in range(4)]
                result = conv(before[q], cur, taps).astype(BF16)
                before[q] = cur[BLK - HALO :]
                bc_ref[b * BLK : (b + 1) * BLK, q * STATE : (q + 1) * STATE] = result
                if q < groups:
                    bt_ref[q, :, b * BLK : (b + 1) * BLK] = result.astype(F32).T.astype(BF16)

        for copy in copies:
            copy.start()

    scale[...] = dot(w_ref[...], e_ref[...])
    for lane in range(0, x_ref.shape[1], LANES):
        at_lanes = slice(lane, lane + LANES)
        taps = [ck_ref[k : k + 1, at_lanes] for k in range(4)]
        tail = tail_ref[:, at_lanes].astype(F32)
        plain[:HALO] = tail
        early[:HALO] = taps[1] * tail + taps[0] * pltpu.roll(tail, 1, 0)
        plain[HALO:] = x_ref[:, at_lanes].astype(F32)
        for b in range(blocks):
            at = b * BLK
            late = plain[at + HALO - 1 : at + HALO - 1 + BLK]
            early[at + HALO : at + HALO + BLK] = (
                taps[1] * plain[at + HALO : at + HALO + BLK] + taps[0] * late
            )
            acc = (
                taps[3] * plain[at + HALO : at + HALO + BLK]
                + taps[2] * late
                + early[at + HALO - 2 : at + HALO - 2 + BLK]
            )
            result = silu(acc)
            xc_ref[at : at + BLK, at_lanes] = result.astype(BF16)
            scaled = result * scale[at : at + BLK, at_lanes]
            weighted[at : at + BLK, at_lanes] = scaled.astype(BF16)
    step_width = x_ref.shape[1]
    group = c * step_width * groups // (heads * HEAD_DIM)
    at = pl.ds(pl.multiple_of(c * step_width, step_width), step_width)
    pay_ref[:, at] = dot(bt_ref[group], weighted[...]).astype(BF16)

    @pl.when(c == pl.num_programs(0) - 1)
    def _():
        for copy in copies:
            copy.wait()


def local_kernel(xc_ref, bc_ref, bt_ref, crow_ref, cols_ref, wrow_ref, skip_ref, *rest):
    y_ref, state = rest[-2:]
    width = xc_ref.shape[1]
    groups = bt_ref.shape[0]
    gw = width // groups

    @pl.when(pl.program_id(0) == 0)
    def _():
        state[...] = rest[0][...] if len(rest) > 3 else jnp.zeros_like(state)

    left = lax.broadcasted_iota(jnp.int32, (BLK, LANES), 1) < HEAD_DIM
    row = lax.broadcasted_iota(jnp.int32, (BLK, BLK), 0)
    causal = row >= lax.broadcasted_iota(jnp.int32, (BLK, BLK), 1)
    for g in range(groups):
        b_g = bc_ref[:, g * STATE : (g + 1) * STATE]
        c_g = bc_ref[:, (groups + g) * STATE : (groups + g + 1) * STATE]
        scores = jnp.where(causal, dot_t(c_g, b_g), 0.0)
        b_t = bt_ref[g].astype(F32)
        for wide in range(g * gw, (g + 1) * gw, 2 * LANES):
            before = state[:, wide : wide + 2 * LANES]
            carry = dot(c_g, before.astype(BF16))
            for k in range(2):
                at = slice(wide + k * LANES, wide + (k + 1) * LANES)
                part = slice(k * LANES, (k + 1) * LANES)
                first = at.start // HEAD_DIM
                mixing, weighted, cums = [], [], []
                for h in (first, first + 1):
                    cum = jnp.broadcast_to(cols_ref[:, h : h + 1], (BLK, BLK))
                    gap = jnp.minimum(cum - crow_ref[h : h + 1], 0.0)
                    mixing.append((jnp.exp2(gap) * scores).astype(BF16))
                    weighted.append((b_t * wrow_ref[h : h + 1]).astype(BF16))
                    cums.append(cum)
                x = xc_ref[:, at]
                nil = jnp.zeros_like(x)
                stacked = jnp.concatenate([jnp.where(left, x, nil), jnp.where(left, nil, x)], 0)
                both = jnp.concatenate(
                    [jnp.concatenate(mixing, 1), jnp.concatenate(weighted, 1)], 0
                )
                result = dot(both, stacked)
                grown = jnp.exp2(jnp.where(left, cums[0], cums[1]))
                skip = jnp.where(left, skip_ref[0, first], skip_ref[0, first + 1])
                y = result[:BLK] + grown * carry[:, part] + skip * x.astype(F32)
                y_ref[:, at] = y.astype(BF16)
                state[:, at] = grown[BLK - 1 :] * before[:, part] + result[BLK:]


def prefix_kernel(pay_ref, e_ref, after_ref, out_ref):
    width = out_ref.shape[2]
    decays = dot(pay_ref[:, 0, width:], e_ref[...])
    running = jnp.zeros(out_ref.shape[1:], F32)
    for slab in range(out_ref.shape[0]):
        out_ref[slab] = running.astype(BF16)
        running = decays[slab : slab + 1] * running + pay_ref[slab, :, :width].astype(F32)


def norm_tile(
    y_ref, bc_ref, g_ref, enter_ref, gate_ref, gain_ref, e_ref, normed_ref, carry, grown, i
):
    width = y_ref.shape[1]
    groups = bc_ref.shape[1] // (2 * STATE)
    gw = width // groups
    grown[...] = dot(g_ref[...], e_ref[...])
    for g in range(groups):
        at = slice(g * gw, (g + 1) * gw)
        carry[:, at] = dot(bc_ref[:, (groups + g) * STATE : (groups + g + 1) * STATE], enter_ref[:, at])
    size = y_ref.shape[0]
    for r in range(0, size, ROWS):
        rows = slice(r, r + ROWS)
        out_rows = pl.ds(pl.multiple_of(i * size + r, ROWS), ROWS)
        for g in range(groups):
            at = slice(g * gw, (g + 1) * gw)
            y = y_ref[rows, at].astype(F32) + grown[rows, at] * carry[rows, at]
            gated = y * silu(gate_ref[rows, at].astype(F32))
            square_mean = jnp.mean(gated * gated, axis=-1, keepdims=True)
            scaled = gated * lax.rsqrt(square_mean + epsilon) * gain_ref[:, at]
            normed_ref[out_rows, at] = scaled.astype(BF16)


def direct_kernel(
    where_ref, y_ref, bc_ref, g_ref, enter_ref, gate_ref, gain_ref, e_ref, w_ref, after_ref,
    *rest, tiles,
):
    *out_refs, normed_ref, carry, grown = rest
    i = pl.program_id(0)

    @pl.when(i < tiles)
    def _():
        norm_tile(
            y_ref, bc_ref, g_ref, enter_ref, gate_ref, gain_ref, e_ref, normed_ref, carry, grown, i
        )

    for k, out_ref in enumerate(out_refs):
        @pl.when(i == tiles + k)
        def _(out_ref=out_ref):
            out_ref[...] = dot(normed_ref[...], w_ref[...]).astype(BF16)


def ends_kernel(
    y_ref, bc_ref, g_ref, enter_ref, gate_ref, gain_ref, e_ref, w_ref, after_ref,
    shares_ref, up_ref, down_ref, normed_ref, carry, grown, *, tiles,
):
    i = pl.program_id(0)

    @pl.when(i < tiles)
    def _():
        norm_tile(
            y_ref, bc_ref, g_ref, enter_ref, gate_ref, gain_ref, e_ref, normed_ref, carry, grown, i
        )

    @pl.when(i >= tiles)
    def _():
        shares_ref[0] = dot(normed_ref[...], w_ref[...]).astype(BF16)

    @pl.when(i == tiles)
    def _():
        down_ref[...] = shares_ref[0]

    @pl.when(i == tiles + 1)
    def _():
        up_ref[...] = shares_ref[0]


def middle_kernel(normed_ref, w_ref, ends_ref, shares_ref):
    shares_ref[0] = dot(normed_ref[...], w_ref[...]).astype(BF16)


def onward_kernel(where_ref, up_own_ref, down_own_ref, up_ref, down_ref, *rest):
    up_out, down_out = rest[-2:]
    up_out[...] = (up_own_ref[0].astype(F32) + up_ref[...].astype(F32)).astype(BF16)
    down_out[...] = (down_own_ref[0].astype(F32) + down_ref[...].astype(F32)).astype(BF16)


def final_kernel(where_ref, own_ref, up_ref, down_ref, *rest):
    out_ref = rest[-1]
    total = own_ref[0].astype(F32) + up_ref[...].astype(F32) + down_ref[...].astype(F32)
    out_ref[...] = total.astype(BF16)


def arrived_kernel(*refs):
    refs[-1][...] = jnp.zeros_like(refs[-1])


def direct_final_kernel(where_ref, normed_ref, w_ref, *refs, count):
    out_ref = refs[-1]
    total = dot(normed_ref[...], w_ref[...])
    for ref in refs[:count]:
        total = total + ref[...].astype(F32)
    out_ref[...] = total.astype(BF16)


def in_hbm(x):
    return pltpu.with_memory_space_constraint(x, pltpu.HBM)


def brief():
    return pl.CostEstimate(flops=1, transcendentals=0, bytes_accessed=1)


def params(limit=VMEM_LIMIT):
    return pltpu.CompilerParams(dimension_semantics=("arbitrary",), vmem_limit_bytes=limit)


def whole(shape):
    return pl.BlockSpec(shape, lambda *b: (0,) * len(shape))


def unread():
    return pl.BlockSpec(memory_space=pl.ANY)


def shaped(shape, dtype=BF16):
    return pltpu.HBM(shape, dtype)


def local(
    inner_input, state_maps, gate_input, step_input, log_decay_rate, step_bias,
    skip_gain, conv_kernel, map_kernel, norm_gain, out_weight,
):
    tokens, width = inner_input.shape
    groups = state_maps.shape[2]
    parts = 2 * groups
    heads = step_input.shape[1]
    blocks = tokens // BLK
    slabs = lax.axis_size("seq")
    chans = lax.axis_size("chan")
    features = out_weight.shape[1]
    map_width = parts * STATE
    low = spread(heads, width)

    tail = jnp.concatenate(
        [inner_input[tokens - HALO :], state_maps[tokens - HALO :].reshape(HALO, map_width)], 1
    )
    tail = lax.ppermute(tail, "seq", [(i, i + 1) for i in range(slabs - 1)])

    def lanes_at(count):
        return pl.BlockSpec((count, WIDE), lambda c: (0, c))

    kept = [
        ((tokens, map_width), BF16),
        ((groups, STATE, tokens), BF16),
        ((heads, tokens), F32),
        ((tokens, LANES), F32),
        ((heads, tokens), F32),
        ((tokens, LANES), BF16),
    ]
    xc, pay, bc, bt, crow, cols, wrow, g_hl = pl.pallas_call(
        states_kernel,
        grid=(width // WIDE,),
        in_specs=[
            lanes_at(tokens),
            whole((tokens * parts, STATE)),
            whole((heads, tokens)),
            lanes_at(HALO),
            pl.BlockSpec((HALO, map_width), lambda c: (0, width // map_width)),
            whole((1, heads)),
            whole((1, heads)),
            lanes_at(4),
            whole((4 * parts, STATE)),
            lanes_at(LANES),
        ],
        out_specs=[lanes_at(tokens), whole((STATE, width + LANES))] + [unread()] * 6,
        out_shape=[shaped((tokens, width)), shaped((STATE, width + LANES))]
        + [shaped(*k) for k in kept],
        scratch_shapes=[pltpu.VMEM(*k) for k in kept]
        + [
            pltpu.VMEM((tokens, WIDE), BF16),
            pltpu.VMEM((tokens, LANES), BF16),
            pltpu.VMEM((tokens, WIDE), F32),
            pltpu.VMEM((HALO + tokens, LANES), F32),
            pltpu.VMEM((HALO + tokens, LANES), F32),
            pltpu.SemaphoreType.DMA((6,)),
        ],
        compiler_params=params(),
        name="states",
    )(
        in_hbm(inner_input), in_hbm(state_maps.reshape(tokens * parts, STATE)),
        in_hbm(step_input.T), tail, tail,
        in_hbm(step_bias.reshape(1, heads)), in_hbm(log_decay_rate.reshape(1, heads)),
        in_hbm(conv_kernel), in_hbm(map_kernel.reshape(4 * parts, STATE)), in_hbm(low),
    )

    part = STATE // slabs
    arrived = lax.all_to_all(
        pay.reshape(slabs, part, width + LANES), "seq", split_axis=0, concat_axis=0, tiled=True
    )

    def local_part(start, count, before, after):
        def tile(width):
            return pl.BlockSpec((BLK, width), lambda b: (start + b, 0))

        operands = [in_hbm(k) for k in (xc, bc, bt, crow, cols, wrow)]
        operands.append(skip_gain.reshape(1, heads))
        specs = [
            tile(width),
            tile(map_width),
            pl.BlockSpec((groups, STATE, BLK), lambda b: (0, 0, start + b)),
            pl.BlockSpec((heads, BLK), lambda b: (0, start + b)),
            tile(LANES),
            pl.BlockSpec((heads, BLK), lambda b: (0, start + b)),
            pl.BlockSpec(memory_space=pltpu.SMEM),
        ]
        aliases = {}
        if before is not None:
            y, state = before
            aliases = {len(operands) + 1: 0}
            operands += [in_hbm(state), in_hbm(y)]
            specs += [whole((STATE, width)), unread()]
        operands.append(in_hbm(after))
        specs.append(unread())
        return pl.pallas_call(
            local_kernel,
            grid=(count,),
            in_specs=specs,
            out_specs=[tile(width), whole((STATE, width))],
            out_shape=[shaped((tokens, width)), shaped((STATE, width), F32)],
            input_output_aliases=aliases,
            compiler_params=params(),
            cost_estimate=brief(),
            name="local_part",
        )(*operands)

    some = blocks * 3 // 8
    y_first = local_part(0, some, None, pay)
    entering = pl.pallas_call(
        prefix_kernel,
        out_shape=shaped((slabs, part, width)),
        in_specs=[
            pl.BlockSpec(memory_space=pltpu.VMEM),
            pl.BlockSpec(memory_space=pltpu.VMEM),
            unread(),
        ],
        out_specs=pl.BlockSpec(memory_space=pltpu.VMEM),
        compiler_params=pltpu.CompilerParams(vmem_limit_bytes=SMALL_LIMIT),
        name="prefix",
    )(arrived, low, in_hbm(y_first[0]))
    y_second = local_part(some, some, y_first, entering)
    entering = lax.all_to_all(entering, "seq", split_axis=0, concat_axis=0, tiled=True)
    entering = entering.reshape(STATE, width)

    part_out = features // chans
    norm_row = norm_gain.reshape(1, width)
    mine = lax.axis_index("chan").astype(jnp.int32)
    where = mine.reshape(1)

    def norm_operands(start, count, tokens_each, y):
        def tile(width):
            return pl.BlockSpec((tokens_each, width), lambda i, *_: (start + jnp.minimum(i, count - 1), 0))

        operands = [in_hbm(k) for k in (y, bc, g_hl)] + [entering]
        operands += [in_hbm(k) for k in (gate_input, norm_row, low)]
        specs = [
            tile(width),
            tile(map_width),
            tile(LANES),
            whole((STATE, width)),
            tile(width),
            whole((1, width)),
            whole((LANES, width)),
        ]
        return operands, specs

    def project_direct(start, count, tokens_each, y, after, slots):
        operands, specs = norm_operands(start, count, tokens_each, y)
        size = count * tokens_each

        def weights(i, where):
            step = i - count
            slot = slots[-1]
            for k in range(len(slots) - 1, -1, -1):
                slot = jnp.where(step <= k, slots[k], slot)
            return (0, lax.rem(where[0] + slot, chans))

        return pl.pallas_call(
            functools.partial(direct_kernel, tiles=count),
            grid_spec=pltpu.PrefetchScalarGridSpec(
                num_scalar_prefetch=1,
                grid=(count + len(slots),),
                in_specs=specs + [pl.BlockSpec((width, part_out), weights), unread()],
                out_specs=[whole((size, part_out))] * len(slots) + [whole((size, width))],
                scratch_shapes=[pltpu.VMEM((tokens_each, width), F32)] * 2,
            ),
            out_shape=[shaped((size, part_out))] * len(slots) + [shaped((size, width))],
            compiler_params=params(),
            name="project_direct",
        )(where, *operands, out_weight, in_hbm(after))

    def direct_final(start, normed, pieces, after):
        def tile(width, start=0):
            return pl.BlockSpec((BLK, width), lambda i, where: (start + i, 0))

        return pl.pallas_call(
            functools.partial(direct_final_kernel, count=len(pieces)),
            grid_spec=pltpu.PrefetchScalarGridSpec(
                num_scalar_prefetch=1,
                grid=(normed.shape[0] // BLK,),
                in_specs=[
                    tile(width),
                    pl.BlockSpec((width, part_out), lambda i, where: (0, where[0])),
                ]
                + [tile(part_out)] * len(pieces)
                + [unread()],
                out_specs=tile(part_out, start),
            ),
            out_shape=shaped((tokens, part_out)),
            compiler_params=params(SMALL_LIMIT),
            name="direct_final",
        )(where, in_hbm(normed), in_hbm(out_weight), *pieces, after)

    def project_ends(start, count, tokens_each, y, after):
        operands, specs = norm_operands(start, count, tokens_each, y)
        size = count * tokens_each

        def dest(i):
            return jnp.where(i <= count, 0, chans - 1)

        return pl.pallas_call(
            functools.partial(ends_kernel, tiles=count),
            grid=(count + 2,),
            in_specs=specs
            + [pl.BlockSpec((width, part_out), lambda i: (0, dest(i))), unread()],
            out_specs=[
                pl.BlockSpec((1, size, part_out), lambda i: (dest(i), 0, 0)),
                whole((size, part_out)),
                whole((size, part_out)),
                whole((size, width)),
            ],
            out_shape=[
                shaped((chans, size, part_out)),
                shaped((size, part_out)),
                shaped((size, part_out)),
                shaped((size, width)),
            ],
            scratch_shapes=[pltpu.VMEM((tokens_each, width), F32)] * 2,
            compiler_params=params(),
            cost_estimate=brief(),
            name="project_ends",
        )(*operands, out_weight, in_hbm(after))

    def project_middle(shares, normed):
        size = normed.shape[0]
        return pl.pallas_call(
            middle_kernel,
            grid=(chans - 2,),
            in_specs=[
                whole((size, width)),
                pl.BlockSpec((width, part_out), lambda i: (0, i + 1)),
                unread(),
            ],
            out_specs=pl.BlockSpec((1, size, part_out), lambda i: (i + 1, 0, 0)),
            out_shape=shaped((chans, size, part_out)),
            input_output_aliases={2: 0},
            compiler_params=params(),
            cost_estimate=brief(),
            name="project_middle",
        )(in_hbm(normed), out_weight, in_hbm(shares))

    def permuted(up, down, s):
        up = lax.ppermute(up, "chan", [(a, a + 1) for a in range(s + 1)])
        down = lax.ppermute(down, "chan", [(a, a - 1) for a in range(chans - 1 - s, chans)])
        return up, down

    def onward(shares, part, up, down, s, after):
        first, count = part
        tile = math.gcd(first, count) if first else count
        skipped = first // tile
        held = skipped if s == 1 else 0

        def plain(i, where):
            return (i, 0)

        def arrived(i, where):
            return (held + i, 0)

        def own(index):
            return pl.BlockSpec(
                (1, tile, part_out), lambda i, where: (index(where[0]), skipped + i, 0)
            )

        return pl.pallas_call(
            onward_kernel,
            grid_spec=pltpu.PrefetchScalarGridSpec(
                num_scalar_prefetch=1,
                grid=(count // tile,),
                in_specs=[
                    own(lambda me: jnp.minimum(chans - 1 - s + me, chans - 1)),
                    own(lambda me: jnp.maximum(me - (chans - 1) + s, 0)),
                    pl.BlockSpec((tile, part_out), arrived),
                    pl.BlockSpec((tile, part_out), arrived),
                ]
                + [unread()] * len(after),
                out_specs=[pl.BlockSpec((tile, part_out), plain)] * 2,
            ),
            out_shape=[jax.ShapeDtypeStruct((count, part_out), BF16)] * 2,
            compiler_params=params(SMALL_LIMIT),
            name="onward",
        )(where, in_hbm(shares), in_hbm(shares), up, down, *after)

    def final(start, shares, part, up, down, out):
        count, skipped = part[1] // BLK, part[0] // BLK

        def plain(i, where):
            return (i, 0)

        operands = [where, in_hbm(shares), up, down]
        in_specs = [
            pl.BlockSpec((1, BLK, part_out), lambda i, where: (where[0], skipped + i, 0)),
            pl.BlockSpec((BLK, part_out), plain),
            pl.BlockSpec((BLK, part_out), plain),
        ]
        aliases = {}
        if out is not None:
            aliases = {len(operands): 0}
            operands.append(in_hbm(out))
            in_specs.append(unread())
        return pl.pallas_call(
            final_kernel,
            grid_spec=pltpu.PrefetchScalarGridSpec(
                num_scalar_prefetch=1,
                grid=(count,),
                in_specs=in_specs,
                out_specs=pl.BlockSpec((BLK, part_out), lambda i, where: (start + skipped + i, 0)),
            ),
            out_shape=shaped((tokens, part_out)),
            input_output_aliases=aliases,
            compiler_params=params(SMALL_LIMIT),
            name="final",
        )(*operands)

    lead = blocks * 3 // 8
    order = sorted(range(1, chans), key=lambda k: (min(k, chans - k), k))
    *slots, normed = project_direct(0, 2, lead * BLK // 2, y_second[0], y_second[1], order)
    pieces = []
    for k, slot in zip(order, slots):
        turn = [(a, (a + k) % chans) for a in range(chans)]
        pieces.append(lax.ppermute(slot, "chan", turn))

    y_third = local_part(2 * some, blocks - 2 * some, y_second, normed)
    rest = blocks - lead
    some = (rest + 1) // 2 * BLK
    parts_of = [(0, some), (some, rest * BLK - some)]
    shares, up, down, line_normed = project_ends(lead, rest, BLK, y_third[0], normed)
    moving = [permuted(up, down, 0)] * 2
    shares = project_middle(shares, line_normed)
    mark = pl.pallas_call(
        arrived_kernel,
        in_specs=[unread()] * (len(pieces) + 1),
        out_specs=pl.BlockSpec(memory_space=pltpu.VMEM),
        out_shape=jax.ShapeDtypeStruct((HALO, LANES), F32),
        compiler_params=pltpu.CompilerParams(vmem_limit_bytes=SMALL_LIMIT),
        cost_estimate=pl.CostEstimate(flops=20000000000, transcendentals=0, bytes_accessed=1),
        name="arrived",
    )(*pieces, in_hbm(shares))
    after = [mark]
    for s in range(1, chans - 1):
        for k in range(2):
            up, down = onward(shares, parts_of[k], *moving[k], s, after)
            after = [up]
            moving[k] = permuted(up, down, s)
        if s == 1:
            out = direct_final(0, normed, pieces, up)
            after = [in_hbm(out)]
    for k in range(2):
        out = final(lead, shares, parts_of[k], *moving[k], out)
    return out


def solution(mesh):
    return jax.shard_map(
        local,
        mesh=mesh,
        in_specs=(
            P("seq", "chan"),
            P("seq", None, "chan", None),
            P("seq", "chan"),
            P("seq", "chan"),
            P("chan"),
            P("chan"),
            P("chan"),
            P(None, "chan"),
            P(None, None, "chan", None),
            P("chan"),
            P("chan", None),
        ),
        out_specs=P("seq", "chan"),
        check_vma=False,
    )
```

```python
import functools
import math

import jax
import jax.numpy as jnp
import numpy as np
from jax import lax
from jax.experimental import pallas as pl
from jax.experimental.pallas import tpu as pltpu
from jax.sharding import PartitionSpec as P

HEAD_DIM = 64
STATE = 128
BLK = 128
LANES = 128
HALO = 8
ROWS = 16
WIDE = 512

step_limit = 0.5
epsilon = 1e-05
LOG2E = 1.4426950408889634
F32 = jnp.float32
BF16 = jnp.bfloat16
VMEM_LIMIT = 40 * 1024 * 1024
SMALL_LIMIT = 10 * 1024 * 1024


def silu(v):
    return v * pl.reciprocal(1.0 + jnp.exp2(v * -LOG2E), approx=True)


def high_low(v):
    high = v.astype(BF16).astype(F32)
    return high, v - high


def spread(heads, width):
    result = np.zeros((LANES, width), np.float32)
    for k in range(2 * heads):
        h = k % heads
        result[k, h * HEAD_DIM : (h + 1) * HEAD_DIM] = 1.0
    return jnp.asarray(result, BF16)


def dot(a, b):
    return jnp.dot(a, b, preferred_element_type=F32)


def dot_t(a, b):
    return lax.dot_general(a, b, (((1,), (1,)), ((), ())), preferred_element_type=F32)


def column(row):
    count = row.shape[1]
    eye = lax.broadcasted_iota(jnp.int32, (count, count), 0) == lax.broadcasted_iota(
        jnp.int32, (count, count), 1
    )
    return jnp.sum(jnp.where(eye, row, 0.0), axis=1, keepdims=True)


def padded(pieces):
    rows = jnp.concatenate(pieces, 0)
    if rows.shape[0] == LANES:
        return rows
    return jnp.concatenate([rows, jnp.zeros((LANES - rows.shape[0], rows.shape[1]), rows.dtype)], 0)


def conv(before, cur, taps):
    full = jnp.concatenate([before, cur], 0)
    late = pltpu.roll(full, 1, 0)
    early = taps[1] * full + taps[0] * late
    acc = taps[3] * cur + taps[2] * late[HALO:] + pltpu.roll(early, 2, 0)[HALO:]
    return silu(acc)


def states_kernel(
    x_ref, maps_ref, step_ref, tail_ref, mtail_ref, bias_ref, rate_ref, ck_ref, mk_ref, e_ref,
    xc_ref, pay_ref, *rest,
):
    outs, (bc_ref, bt_ref, crow_ref, cols_ref, wrow_ref, g_ref) = rest[:6], rest[6:12]
    weighted, w_ref, scale, plain, early, sems = rest[12:]
    copies = [
        pltpu.make_async_copy(kept, out, sems.at[k])
        for k, (kept, out) in enumerate(zip(rest[6:12], outs))
    ]
    c = pl.program_id(0)
    heads, tokens = step_ref.shape
    parts = mk_ref.shape[0] // 4
    groups = parts // 2
    blocks = tokens // BLK

    @pl.when(c == 0)
    def _():
        bias, rate = column(bias_ref[...]), -jnp.exp(column(rate_ref[...]))
        v = step_ref[...] + bias
        step = jnp.minimum(jnp.maximum(v, 0.0) + jnp.log1p(jnp.exp(-jnp.abs(v))), step_limit)
        log_step = rate * step
        first, rest = high_low(log_step)
        second, third = high_low(rest)
        pieces = []
        for b in range(blocks):
            at = slice(b * BLK, (b + 1) * BLK)
            pieces += [first[:, at], second[:, at], third[:, at]]
        row = lax.broadcasted_iota(jnp.int32, (BLK, BLK), 0)
        col = lax.broadcasted_iota(jnp.int32, (BLK, BLK), 1)
        tri = jnp.where(row <= col, 1.0, 0.0).astype(BF16)
        sums = dot(jnp.concatenate(pieces, 0).astype(BF16), tri)
        cums, leads = [], [jnp.zeros((heads, 1), F32)]
        for b in range(blocks):
            at = 3 * b * heads
            cum = (
                sums[at : at + heads]
                + sums[at + heads : at + 2 * heads]
                + sums[at + 2 * heads : at + 3 * heads]
            )
            cums.append(cum)
            leads.append(leads[-1] + cum[:, BLK - 1 : BLK])
        last = None
        for b in range(blocks):
            at = slice(b * BLK, (b + 1) * BLK)
            cum, step_b = cums[b], step[:, at]
            total = cum[:, BLK - 1 : BLK]
            wrow_ref[:, at] = jnp.exp(total - cum) * step_b
            slab_weight = jnp.exp(leads[blocks] - (leads[b] + cum)) * step_b
            entered = jnp.exp(cum + leads[b])
            crow_ref[:, at] = (cum - jnp.log(step_b)) * LOG2E
            w_ref[at, :] = padded(high_low(slab_weight)).T.astype(BF16)
            last = padded(high_low(entered)).T
            g_ref[at, :] = last.astype(BF16)
            cols_ref[at, :] = padded((cum * LOG2E,)).T
        pay_ref[:, heads * HEAD_DIM :] = jnp.broadcast_to(last[BLK - 1 :], (STATE, LANES)).astype(BF16)

        few = BLK // 2
        row = lax.broadcasted_iota(jnp.int32, (few * parts, few * parts), 0)
        col = lax.broadcasted_iota(jnp.int32, (few * parts, few * parts), 1)
        source = (row & (few - 1)) * parts + row // few
        pick = jnp.where(col == source, 1.0, 0.0).astype(BF16)
        before = [mtail_ref[:, q * STATE : (q + 1) * STATE].astype(F32) for q in range(parts)]
        for b in range(blocks):
            at = 2 * b * few * parts
            mixed = [maps_ref[at + k * few * parts : at + (k + 1) * few * parts] for k in range(2)]
            ordered = dot(pick, jnp.concatenate(mixed, 1))
            for q in range(parts):
                own = ordered[q * few : (q + 1) * few]
                cur = jnp.concatenate([own[:, :STATE], own[:, STATE:]], 0)
                taps = [mk_ref[k * parts + q : k * parts + q + 1] for k in range(4)]
                result = conv(before[q], cur, taps).astype(BF16)
                before[q] = cur[BLK - HALO :]
                bc_ref[b * BLK : (b + 1) * BLK, q * STATE : (q + 1) * STATE] = result
                if q < groups:
                    bt_ref[q, :, b * BLK : (b + 1) * BLK] = result.astype(F32).T.astype(BF16)

        for copy in copies:
            copy.start()

    scale[...] = dot(w_ref[...], e_ref[...])
    for lane in range(0, x_ref.shape[1], LANES):
        at_lanes = slice(lane, lane + LANES)
        taps = [ck_ref[k : k + 1, at_lanes] for k in range(4)]
        tail = tail_ref[:, at_lanes].astype(F32)
        plain[:HALO] = tail
        early[:HALO] = taps[1] * tail + taps[0] * pltpu.roll(tail, 1, 0)
        plain[HALO:] = x_ref[:, at_lanes].astype(F32)
        for b in range(blocks):
            at = b * BLK
            late = plain[at + HALO - 1 : at + HALO - 1 + BLK]
            early[at + HALO : at + HALO + BLK] = (
                taps[1] * plain[at + HALO : at + HALO + BLK] + taps[0] * late
            )
            acc = (
                taps[3] * plain[at + HALO : at + HALO + BLK]
                + taps[2] * late
                + early[at + HALO - 2 : at + HALO - 2 + BLK]
            )
            result = silu(acc)
            xc_ref[at : at + BLK, at_lanes] = result.astype(BF16)
            scaled = result * scale[at : at + BLK, at_lanes]
            weighted[at : at + BLK, at_lanes] = scaled.astype(BF16)
    step_width = x_ref.shape[1]
    group = c * step_width * groups // (heads * HEAD_DIM)
    at = pl.ds(pl.multiple_of(c * step_width, step_width), step_width)
    pay_ref[:, at] = dot(bt_ref[group], weighted[...]).astype(BF16)

    @pl.when(c == pl.num_programs(0) - 1)
    def _():
        for copy in copies:
            copy.wait()


def local_kernel(xc_ref, bc_ref, bt_ref, crow_ref, cols_ref, wrow_ref, skip_ref, *rest):
    y_ref, state = rest[-2:]
    width = xc_ref.shape[1]
    groups = bt_ref.shape[0]
    gw = width // groups

    @pl.when(pl.program_id(0) == 0)
    def _():
        state[...] = rest[0][...] if len(rest) > 3 else jnp.zeros_like(state)

    left = lax.broadcasted_iota(jnp.int32, (BLK, LANES), 1) < HEAD_DIM
    row = lax.broadcasted_iota(jnp.int32, (BLK, BLK), 0)
    causal = row >= lax.broadcasted_iota(jnp.int32, (BLK, BLK), 1)
    for g in range(groups):
        b_g = bc_ref[:, g * STATE : (g + 1) * STATE]
        c_g = bc_ref[:, (groups + g) * STATE : (groups + g + 1) * STATE]
        scores = jnp.where(causal, dot_t(c_g, b_g), 0.0)
        b_t = bt_ref[g].astype(F32)
        for wide in range(g * gw, (g + 1) * gw, 2 * LANES):
            before = state[:, wide : wide + 2 * LANES]
            carry = dot(c_g, before.astype(BF16))
            for k in range(2):
                at = slice(wide + k * LANES, wide + (k + 1) * LANES)
                part = slice(k * LANES, (k + 1) * LANES)
                first = at.start // HEAD_DIM
                mixing, weighted, cums = [], [], []
                for h in (first, first + 1):
                    cum = jnp.broadcast_to(cols_ref[:, h : h + 1], (BLK, BLK))
                    gap = jnp.minimum(cum - crow_ref[h : h + 1], 0.0)
                    mixing.append((jnp.exp2(gap) * scores).astype(BF16))
                    weighted.append((b_t * wrow_ref[h : h + 1]).astype(BF16))
                    cums.append(cum)
                x = xc_ref[:, at]
                nil = jnp.zeros_like(x)
                stacked = jnp.concatenate([jnp.where(left, x, nil), jnp.where(left, nil, x)], 0)
                both = jnp.concatenate(
                    [jnp.concatenate(mixing, 1), jnp.concatenate(weighted, 1)], 0
                )
                result = dot(both, stacked)
                grown = jnp.exp2(jnp.where(left, cums[0], cums[1]))
                skip = jnp.where(left, skip_ref[0, first], skip_ref[0, first + 1])
                y = result[:BLK] + grown * carry[:, part] + skip * x.astype(F32)
                y_ref[:, at] = y.astype(BF16)
                state[:, at] = grown[BLK - 1 :] * before[:, part] + result[BLK:]


def prefix_kernel(pay_ref, e_ref, after_ref, out_ref):
    width = out_ref.shape[2]
    decays = dot(pay_ref[:, 0, width:], e_ref[...])
    running = jnp.zeros(out_ref.shape[1:], F32)
    for slab in range(out_ref.shape[0]):
        out_ref[slab] = running.astype(BF16)
        running = decays[slab : slab + 1] * running + pay_ref[slab, :, :width].astype(F32)


def norm_tile(
    y_ref, bc_ref, g_ref, enter_ref, gate_ref, gain_ref, e_ref, normed_ref, carry, grown, i
):
    width = y_ref.shape[1]
    groups = bc_ref.shape[1] // (2 * STATE)
    gw = width // groups
    grown[...] = dot(g_ref[...], e_ref[...])
    for g in range(groups):
        at = slice(g * gw, (g + 1) * gw)
        carry[:, at] = dot(bc_ref[:, (groups + g) * STATE : (groups + g + 1) * STATE], enter_ref[:, at])
    size = y_ref.shape[0]
    for r in range(0, size, ROWS):
        rows = slice(r, r + ROWS)
        out_rows = pl.ds(pl.multiple_of(i * size + r, ROWS), ROWS)
        for g in range(groups):
            at = slice(g * gw, (g + 1) * gw)
            y = y_ref[rows, at].astype(F32) + grown[rows, at] * carry[rows, at]
            gated = y * silu(gate_ref[rows, at].astype(F32))
            square_mean = jnp.mean(gated * gated, axis=-1, keepdims=True)
            scaled = gated * lax.rsqrt(square_mean + epsilon) * gain_ref[:, at]
            normed_ref[out_rows, at] = scaled.astype(BF16)


def direct_kernel(
    where_ref, y_ref, bc_ref, g_ref, enter_ref, gate_ref, gain_ref, e_ref, w_ref, after_ref,
    *rest, tiles,
):
    *out_refs, normed_ref, carry, grown = rest
    i = pl.program_id(0)

    @pl.when(i < tiles)
    def _():
        norm_tile(
            y_ref, bc_ref, g_ref, enter_ref, gate_ref, gain_ref, e_ref, normed_ref, carry, grown, i
        )

    for k, out_ref in enumerate(out_refs):
        @pl.when(i == tiles + k)
        def _(out_ref=out_ref):
            out_ref[...] = dot(normed_ref[...], w_ref[...]).astype(BF16)


def ends_kernel(
    y_ref, bc_ref, g_ref, enter_ref, gate_ref, gain_ref, e_ref, w_ref, after_ref,
    shares_ref, up_ref, down_ref, normed_ref, carry, grown, *, tiles,
):
    i = pl.program_id(0)

    @pl.when(i < tiles)
    def _():
        norm_tile(
            y_ref, bc_ref, g_ref, enter_ref, gate_ref, gain_ref, e_ref, normed_ref, carry, grown, i
        )

    @pl.when(i >= tiles)
    def _():
        shares_ref[0] = dot(normed_ref[...], w_ref[...]).astype(BF16)

    @pl.when(i == tiles)
    def _():
        down_ref[...] = shares_ref[0]

    @pl.when(i == tiles + 1)
    def _():
        up_ref[...] = shares_ref[0]


def middle_kernel(normed_ref, w_ref, ends_ref, shares_ref):
    shares_ref[0] = dot(normed_ref[...], w_ref[...]).astype(BF16)


def onward_kernel(where_ref, up_own_ref, down_own_ref, up_ref, down_ref, *rest):
    up_out, down_out = rest[-2:]
    up_out[...] = (up_own_ref[0].astype(F32) + up_ref[...].astype(F32)).astype(BF16)
    down_out[...] = (down_own_ref[0].astype(F32) + down_ref[...].astype(F32)).astype(BF16)


def final_kernel(where_ref, own_ref, up_ref, down_ref, *rest):
    out_ref = rest[-1]
    total = own_ref[0].astype(F32) + up_ref[...].astype(F32) + down_ref[...].astype(F32)
    out_ref[...] = total.astype(BF16)


def arrived_kernel(*refs):
    refs[-1][...] = jnp.zeros_like(refs[-1])


def direct_final_kernel(where_ref, normed_ref, w_ref, *refs, count):
    out_ref = refs[-1]
    total = dot(normed_ref[...], w_ref[...])
    for ref in refs[:count]:
        total = total + ref[...].astype(F32)
    out_ref[...] = total.astype(BF16)


def in_hbm(x):
    return pltpu.with_memory_space_constraint(x, pltpu.HBM)


def brief():
    return pl.CostEstimate(flops=1, transcendentals=0, bytes_accessed=1)


def params(limit=VMEM_LIMIT):
    return pltpu.CompilerParams(dimension_semantics=("arbitrary",), vmem_limit_bytes=limit)


def whole(shape):
    return pl.BlockSpec(shape, lambda *b: (0,) * len(shape))


def unread():
    return pl.BlockSpec(memory_space=pl.ANY)


def shaped(shape, dtype=BF16):
    return pltpu.HBM(shape, dtype)


def local(
    inner_input, state_maps, gate_input, step_input, log_decay_rate, step_bias,
    skip_gain, conv_kernel, map_kernel, norm_gain, out_weight,
):
    tokens, width = inner_input.shape
    groups = state_maps.shape[2]
    parts = 2 * groups
    heads = step_input.shape[1]
    blocks = tokens // BLK
    slabs = lax.axis_size("seq")
    chans = lax.axis_size("chan")
    features = out_weight.shape[1]
    map_width = parts * STATE
    low = spread(heads, width)

    tail = jnp.concatenate(
        [inner_input[tokens - HALO :], state_maps[tokens - HALO :].reshape(HALO, map_width)], 1
    )
    tail = lax.ppermute(tail, "seq", [(i, i + 1) for i in range(slabs - 1)])

    def lanes_at(count):
        return pl.BlockSpec((count, WIDE), lambda c: (0, c))

    kept = [
        ((tokens, map_width), BF16),
        ((groups, STATE, tokens), BF16),
        ((heads, tokens), F32),
        ((tokens, LANES), F32),
        ((heads, tokens), F32),
        ((tokens, LANES), BF16),
    ]
    xc, pay, bc, bt, crow, cols, wrow, g_hl = pl.pallas_call(
        states_kernel,
        grid=(width // WIDE,),
        in_specs=[
            lanes_at(tokens),
            whole((tokens * parts, STATE)),
            whole((heads, tokens)),
            lanes_at(HALO),
            pl.BlockSpec((HALO, map_width), lambda c: (0, width // map_width)),
            whole((1, heads)),
            whole((1, heads)),
            lanes_at(4),
            whole((4 * parts, STATE)),
            lanes_at(LANES),
        ],
        out_specs=[lanes_at(tokens), whole((STATE, width + LANES))] + [unread()] * 6,
        out_shape=[shaped((tokens, width)), shaped((STATE, width + LANES))]
        + [shaped(*k) for k in kept],
        scratch_shapes=[pltpu.VMEM(*k) for k in kept]
        + [
            pltpu.VMEM((tokens, WIDE), BF16),
            pltpu.VMEM((tokens, LANES), BF16),
            pltpu.VMEM((tokens, WIDE), F32),
            pltpu.VMEM((HALO + tokens, LANES), F32),
            pltpu.VMEM((HALO + tokens, LANES), F32),
            pltpu.SemaphoreType.DMA((6,)),
        ],
        compiler_params=params(),
        name="states",
    )(
        in_hbm(inner_input), in_hbm(state_maps.reshape(tokens * parts, STATE)),
        in_hbm(step_input.T), tail, tail,
        in_hbm(step_bias.reshape(1, heads)), in_hbm(log_decay_rate.reshape(1, heads)),
        in_hbm(conv_kernel), in_hbm(map_kernel.reshape(4 * parts, STATE)), in_hbm(low),
    )

    part = STATE // slabs
    arrived = lax.all_to_all(
        pay.reshape(slabs, part, width + LANES), "seq", split_axis=0, concat_axis=0, tiled=True
    )

    def local_part(start, count, before, after):
        def tile(width):
            return pl.BlockSpec((BLK, width), lambda b: (start + b, 0))

        operands = [in_hbm(k) for k in (xc, bc, bt, crow, cols, wrow)]
        operands.append(skip_gain.reshape(1, heads))
        specs = [
            tile(width),
            tile(map_width),
            pl.BlockSpec((groups, STATE, BLK), lambda b: (0, 0, start + b)),
            pl.BlockSpec((heads, BLK), lambda b: (0, start + b)),
            tile(LANES),
            pl.BlockSpec((heads, BLK), lambda b: (0, start + b)),
            pl.BlockSpec(memory_space=pltpu.SMEM),
        ]
        aliases = {}
        if before is not None:
            y, state = before
            aliases = {len(operands) + 1: 0}
            operands += [in_hbm(state), in_hbm(y)]
            specs += [whole((STATE, width)), unread()]
        operands.append(in_hbm(after))
        specs.append(unread())
        return pl.pallas_call(
            local_kernel,
            grid=(count,),
            in_specs=specs,
            out_specs=[tile(width), whole((STATE, width))],
            out_shape=[shaped((tokens, width)), shaped((STATE, width), F32)],
            input_output_aliases=aliases,
            compiler_params=params(),
            cost_estimate=brief(),
            name="local_part",
        )(*operands)

    some = blocks * 3 // 8
    y_first = local_part(0, some, None, pay)
    entering = pl.pallas_call(
        prefix_kernel,
        out_shape=shaped((slabs, part, width)),
        in_specs=[
            pl.BlockSpec(memory_space=pltpu.VMEM),
            pl.BlockSpec(memory_space=pltpu.VMEM),
            unread(),
        ],
        out_specs=pl.BlockSpec(memory_space=pltpu.VMEM),
        compiler_params=pltpu.CompilerParams(vmem_limit_bytes=SMALL_LIMIT),
        name="prefix",
    )(arrived, low, in_hbm(y_first[0]))
    y_second = local_part(some, some, y_first, entering)
    entering = lax.all_to_all(entering, "seq", split_axis=0, concat_axis=0, tiled=True)
    entering = entering.reshape(STATE, width)

    part_out = features // chans
    norm_row = norm_gain.reshape(1, width)
    mine = lax.axis_index("chan").astype(jnp.int32)
    where = mine.reshape(1)

    def norm_operands(start, count, tokens_each, y):
        def tile(width):
            return pl.BlockSpec((tokens_each, width), lambda i, *_: (start + jnp.minimum(i, count - 1), 0))

        operands = [in_hbm(k) for k in (y, bc, g_hl)] + [entering]
        operands += [in_hbm(k) for k in (gate_input, norm_row, low)]
        specs = [
            tile(width),
            tile(map_width),
            tile(LANES),
            whole((STATE, width)),
            tile(width),
            whole((1, width)),
            whole((LANES, width)),
        ]
        return operands, specs

    def project_direct(start, count, tokens_each, y, after, slots):
        operands, specs = norm_operands(start, count, tokens_each, y)
        size = count * tokens_each

        def weights(i, where):
            step = i - count
            slot = slots[-1]
            for k in range(len(slots) - 1, -1, -1):
                slot = jnp.where(step <= k, slots[k], slot)
            return (0, lax.rem(where[0] + slot, chans))

        return pl.pallas_call(
            functools.partial(direct_kernel, tiles=count),
            grid_spec=pltpu.PrefetchScalarGridSpec(
                num_scalar_prefetch=1,
                grid=(count + len(slots),),
                in_specs=specs + [pl.BlockSpec((width, part_out), weights), unread()],
                out_specs=[whole((size, part_out))] * len(slots) + [whole((size, width))],
                scratch_shapes=[pltpu.VMEM((tokens_each, width), F32)] * 2,
            ),
            out_shape=[shaped((size, part_out))] * len(slots) + [shaped((size, width))],
            compiler_params=params(),
            name="project_direct",
        )(where, *operands, in_hbm(out_weight), in_hbm(after))

    def direct_final(start, normed, pieces, after):
        def tile(width, start=0):
            return pl.BlockSpec((BLK, width), lambda i, where: (start + i, 0))

        return pl.pallas_call(
            functools.partial(direct_final_kernel, count=len(pieces)),
            grid_spec=pltpu.PrefetchScalarGridSpec(
                num_scalar_prefetch=1,
                grid=(normed.shape[0] // BLK,),
                in_specs=[
                    tile(width),
                    pl.BlockSpec((width, part_out), lambda i, where: (0, where[0])),
                ]
                + [tile(part_out)] * len(pieces)
                + [unread()],
                out_specs=tile(part_out, start),
            ),
            out_shape=shaped((tokens, part_out)),
            compiler_params=params(SMALL_LIMIT),
            name="direct_final",
        )(where, in_hbm(normed), in_hbm(out_weight), *pieces, after)

    def project_ends(start, count, tokens_each, y, after):
        operands, specs = norm_operands(start, count, tokens_each, y)
        size = count * tokens_each

        def dest(i):
            return jnp.where(i <= count, 0, chans - 1)

        return pl.pallas_call(
            functools.partial(ends_kernel, tiles=count),
            grid=(count + 2,),
            in_specs=specs
            + [pl.BlockSpec((width, part_out), lambda i: (0, dest(i))), unread()],
            out_specs=[
                pl.BlockSpec((1, size, part_out), lambda i: (dest(i), 0, 0)),
                whole((size, part_out)),
                whole((size, part_out)),
                whole((size, width)),
            ],
            out_shape=[
                shaped((chans, size, part_out)),
                shaped((size, part_out)),
                shaped((size, part_out)),
                shaped((size, width)),
            ],
            scratch_shapes=[pltpu.VMEM((tokens_each, width), F32)] * 2,
            compiler_params=params(),
            cost_estimate=brief(),
            name="project_ends",
        )(*operands, in_hbm(out_weight), in_hbm(after))

    def project_middle(shares, normed):
        size = normed.shape[0]
        return pl.pallas_call(
            middle_kernel,
            grid=(chans - 2,),
            in_specs=[
                whole((size, width)),
                pl.BlockSpec((width, part_out), lambda i: (0, i + 1)),
                unread(),
            ],
            out_specs=pl.BlockSpec((1, size, part_out), lambda i: (i + 1, 0, 0)),
            out_shape=shaped((chans, size, part_out)),
            input_output_aliases={2: 0},
            compiler_params=params(),
            cost_estimate=brief(),
            name="project_middle",
        )(in_hbm(normed), in_hbm(out_weight), in_hbm(shares))

    def permuted(up, down, s):
        up = lax.ppermute(up, "chan", [(a, a + 1) for a in range(s + 1)])
        down = lax.ppermute(down, "chan", [(a, a - 1) for a in range(chans - 1 - s, chans)])
        return up, down

    def onward(shares, part, up, down, s, after):
        first, count = part
        tile = math.gcd(first, count) if first else count
        skipped = first // tile
        held = skipped if s == 1 else 0

        def plain(i, where):
            return (i, 0)

        def arrived(i, where):
            return (held + i, 0)

        def own(index):
            return pl.BlockSpec(
                (1, tile, part_out), lambda i, where: (index(where[0]), skipped + i, 0)
            )

        return pl.pallas_call(
            onward_kernel,
            grid_spec=pltpu.PrefetchScalarGridSpec(
                num_scalar_prefetch=1,
                grid=(count // tile,),
                in_specs=[
                    own(lambda me: jnp.minimum(chans - 1 - s + me, chans - 1)),
                    own(lambda me: jnp.maximum(me - (chans - 1) + s, 0)),
                    pl.BlockSpec((tile, part_out), arrived),
                    pl.BlockSpec((tile, part_out), arrived),
                ]
                + [unread()] * len(after),
                out_specs=[pl.BlockSpec((tile, part_out), plain)] * 2,
            ),
            out_shape=[jax.ShapeDtypeStruct((count, part_out), BF16)] * 2,
            compiler_params=params(SMALL_LIMIT),
            name="onward",
        )(where, in_hbm(shares), in_hbm(shares), up, down, *after)

    def final(start, shares, part, up, down, out):
        count, skipped = part[1] // BLK, part[0] // BLK

        def plain(i, where):
            return (i, 0)

        operands = [where, in_hbm(shares), up, down]
        in_specs = [
            pl.BlockSpec((1, BLK, part_out), lambda i, where: (where[0], skipped + i, 0)),
            pl.BlockSpec((BLK, part_out), plain),
            pl.BlockSpec((BLK, part_out), plain),
        ]
        aliases = {}
        if out is not None:
            aliases = {len(operands): 0}
            operands.append(in_hbm(out))
            in_specs.append(unread())
        return pl.pallas_call(
            final_kernel,
            grid_spec=pltpu.PrefetchScalarGridSpec(
                num_scalar_prefetch=1,
                grid=(count,),
                in_specs=in_specs,
                out_specs=pl.BlockSpec((BLK, part_out), lambda i, where: (start + skipped + i, 0)),
            ),
            out_shape=shaped((tokens, part_out)),
            input_output_aliases=aliases,
            compiler_params=params(SMALL_LIMIT),
            name="final",
        )(*operands)

    lead = blocks * 3 // 8
    order = sorted(range(1, chans), key=lambda k: (min(k, chans - k), k))
    *slots, normed = project_direct(0, 2, lead * BLK // 2, y_second[0], y_second[1], order)
    pieces = []
    for k, slot in zip(order, slots):
        turn = [(a, (a + k) % chans) for a in range(chans)]
        pieces.append(lax.ppermute(slot, "chan", turn))

    y_third = local_part(2 * some, blocks - 2 * some, y_second, normed)
    rest = blocks - lead
    some = (rest + 1) // 2 * BLK
    parts_of = [(0, some), (some, rest * BLK - some)]
    shares, up, down, line_normed = project_ends(lead, rest, BLK, y_third[0], normed)
    moving = [permuted(up, down, 0)] * 2
    shares = project_middle(shares, line_normed)
    mark = pl.pallas_call(
        arrived_kernel,
        in_specs=[unread()] * (len(pieces) + 1),
        out_specs=pl.BlockSpec(memory_space=pltpu.VMEM),
        out_shape=jax.ShapeDtypeStruct((HALO, LANES), F32),
        compiler_params=pltpu.CompilerParams(vmem_limit_bytes=SMALL_LIMIT),
        cost_estimate=pl.CostEstimate(flops=20000000000, transcendentals=0, bytes_accessed=1),
        name="arrived",
    )(*pieces, in_hbm(shares))
    after = [mark]
    for s in range(1, chans - 1):
        for k in range(2):
            up, down = onward(shares, parts_of[k], *moving[k], s, after)
            after = [up]
            moving[k] = permuted(up, down, s)
        if s == 1:
            out = direct_final(0, normed, pieces, up)
            after = [in_hbm(out)]
    for k in range(2):
        out = final(lead, shares, parts_of[k], *moving[k], out)
    return out


def solution(mesh):
    return jax.shard_map(
        local,
        mesh=mesh,
        in_specs=(
            P("seq", "chan"),
            P("seq", None, "chan", None),
            P("seq", "chan"),
            P("seq", "chan"),
            P("chan"),
            P("chan"),
            P("chan"),
            P(None, "chan"),
            P(None, None, "chan", None),
            P("chan"),
            P("chan", None),
        ),
        out_specs=P("seq", "chan"),
        check_vma=False,
    )
```

```python
import functools
import math

import jax
import jax.numpy as jnp
import numpy as np
from jax import lax
from jax.experimental import pallas as pl
from jax.experimental.pallas import tpu as pltpu
from jax.sharding import PartitionSpec as P

HEAD_DIM = 64
STATE = 128
BLK = 128
LANES = 128
HALO = 8
ROWS = 16
WIDE = 512

step_limit = 0.5
epsilon = 1e-05
LOG2E = 1.4426950408889634
F32 = jnp.float32
BF16 = jnp.bfloat16
VMEM_LIMIT = 40 * 1024 * 1024
SMALL_LIMIT = 10 * 1024 * 1024


def silu(v):
    return v * pl.reciprocal(1.0 + jnp.exp2(v * -LOG2E), approx=True)


def high_low(v):
    high = v.astype(BF16).astype(F32)
    return high, v - high


def spread(heads, width):
    result = np.zeros((LANES, width), np.float32)
    for k in range(2 * heads):
        h = k % heads
        result[k, h * HEAD_DIM : (h + 1) * HEAD_DIM] = 1.0
    return jnp.asarray(result, BF16)


def dot(a, b):
    return jnp.dot(a, b, preferred_element_type=F32)


def dot_t(a, b):
    return lax.dot_general(a, b, (((1,), (1,)), ((), ())), preferred_element_type=F32)


def column(row):
    count = row.shape[1]
    eye = lax.broadcasted_iota(jnp.int32, (count, count), 0) == lax.broadcasted_iota(
        jnp.int32, (count, count), 1
    )
    return jnp.sum(jnp.where(eye, row, 0.0), axis=1, keepdims=True)


def padded(pieces):
    rows = jnp.concatenate(pieces, 0)
    if rows.shape[0] == LANES:
        return rows
    return jnp.concatenate([rows, jnp.zeros((LANES - rows.shape[0], rows.shape[1]), rows.dtype)], 0)


def conv(before, cur, taps):
    full = jnp.concatenate([before, cur], 0)
    late = pltpu.roll(full, 1, 0)
    early = taps[1] * full + taps[0] * late
    acc = taps[3] * cur + taps[2] * late[HALO:] + pltpu.roll(early, 2, 0)[HALO:]
    return silu(acc)


def states_kernel(
    x_ref, maps_ref, step_ref, tail_ref, mtail_ref, bias_ref, rate_ref, ck_ref, mk_ref, e_ref,
    xc_ref, pay_ref, *rest,
):
    outs, (bc_ref, bt_ref, crow_ref, cols_ref, wrow_ref, g_ref) = rest[:6], rest[6:12]
    weighted, w_ref, scale, plain, early, sems = rest[12:]
    copies = [
        pltpu.make_async_copy(kept, out, sems.at[k])
        for k, (kept, out) in enumerate(zip(rest[6:12], outs))
    ]
    c = pl.program_id(0)
    heads, tokens = step_ref.shape
    parts = mk_ref.shape[0] // 4
    groups = parts // 2
    blocks = tokens // BLK

    @pl.when(c == 0)
    def _():
        bias, rate = column(bias_ref[...]), -jnp.exp(column(rate_ref[...]))
        v = step_ref[...] + bias
        step = jnp.minimum(jnp.maximum(v, 0.0) + jnp.log1p(jnp.exp(-jnp.abs(v))), step_limit)
        log_step = rate * step
        first, rest = high_low(log_step)
        second, third = high_low(rest)
        pieces = []
        for b in range(blocks):
            at = slice(b * BLK, (b + 1) * BLK)
            pieces += [first[:, at], second[:, at], third[:, at]]
        row = lax.broadcasted_iota(jnp.int32, (BLK, BLK), 0)
        col = lax.broadcasted_iota(jnp.int32, (BLK, BLK), 1)
        tri = jnp.where(row <= col, 1.0, 0.0).astype(BF16)
        sums = dot(jnp.concatenate(pieces, 0).astype(BF16), tri)
        cums, leads = [], [jnp.zeros((heads, 1), F32)]
        for b in range(blocks):
            at = 3 * b * heads
            cum = (
                sums[at : at + heads]
                + sums[at + heads : at + 2 * heads]
                + sums[at + 2 * heads : at + 3 * heads]
            )
            cums.append(cum)
            leads.append(leads[-1] + cum[:, BLK - 1 : BLK])
        last = None
        for b in range(blocks):
            at = slice(b * BLK, (b + 1) * BLK)
            cum, step_b = cums[b], step[:, at]
            total = cum[:, BLK - 1 : BLK]
            wrow_ref[:, at] = jnp.exp(total - cum) * step_b
            slab_weight = jnp.exp(leads[blocks] - (leads[b] + cum)) * step_b
            entered = jnp.exp(cum + leads[b])
            crow_ref[:, at] = (cum - jnp.log(step_b)) * LOG2E
            w_ref[at, :] = padded(high_low(slab_weight)).T.astype(BF16)
            last = padded(high_low(entered)).T
            g_ref[at, :] = last.astype(BF16)
            cols_ref[at, :] = padded((cum * LOG2E,)).T
        pay_ref[:, heads * HEAD_DIM :] = jnp.broadcast_to(last[BLK - 1 :], (STATE, LANES)).astype(BF16)

        few = BLK // 2
        row = lax.broadcasted_iota(jnp.int32, (few * parts, few * parts), 0)
        col = lax.broadcasted_iota(jnp.int32, (few * parts, few * parts), 1)
        source = (row & (few - 1)) * parts + row // few
        pick = jnp.where(col == source, 1.0, 0.0).astype(BF16)
        before = [mtail_ref[:, q * STATE : (q + 1) * STATE].astype(F32) for q in range(parts)]
        for b in range(blocks):
            at = 2 * b * few * parts
            mixed = [maps_ref[at + k * few * parts : at + (k + 1) * few * parts] for k in range(2)]
            ordered = dot(pick, jnp.concatenate(mixed, 1))
            for q in range(parts):
                own = ordered[q * few : (q + 1) * few]
                cur = jnp.concatenate([own[:, :STATE], own[:, STATE:]], 0)
                taps = [mk_ref[k * parts + q : k * parts + q + 1] for k in range(4)]
                result = conv(before[q], cur, taps).astype(BF16)
                before[q] = cur[BLK - HALO :]
                bc_ref[b * BLK : (b + 1) * BLK, q * STATE : (q + 1) * STATE] = result
                if q < groups:
                    bt_ref[q, :, b * BLK : (b + 1) * BLK] = result.astype(F32).T.astype(BF16)

        for copy in copies:
            copy.start()

    scale[...] = dot(w_ref[...], e_ref[...])
    for lane in range(0, x_ref.shape[1], LANES):
        at_lanes = slice(lane, lane + LANES)
        taps = [ck_ref[k : k + 1, at_lanes] for k in range(4)]
        tail = tail_ref[:, at_lanes].astype(F32)
        plain[:HALO] = tail
        early[:HALO] = taps[1] * tail + taps[0] * pltpu.roll(tail, 1, 0)
        plain[HALO:] = x_ref[:, at_lanes].astype(F32)
        for b in range(blocks):
            at = b * BLK
            late = plain[at + HALO - 1 : at + HALO - 1 + BLK]
            early[at + HALO : at + HALO + BLK] = (
                taps[1] * plain[at + HALO : at + HALO + BLK] + taps[0] * late
            )
            acc = (
                taps[3] * plain[at + HALO : at + HALO + BLK]
                + taps[2] * late
                + early[at + HALO - 2 : at + HALO - 2 + BLK]
            )
            result = silu(acc)
            xc_ref[at : at + BLK, at_lanes] = result.astype(BF16)
            scaled = result * scale[at : at + BLK, at_lanes]
            weighted[at : at + BLK, at_lanes] = scaled.astype(BF16)
    step_width = x_ref.shape[1]
    group = c * step_width * groups // (heads * HEAD_DIM)
    at = pl.ds(pl.multiple_of(c * step_width, step_width), step_width)
    pay_ref[:, at] = dot(bt_ref[group], weighted[...]).astype(BF16)

    @pl.when(c == pl.num_programs(0) - 1)
    def _():
        for copy in copies:
            copy.wait()


def local_kernel(xc_ref, bc_ref, bt_ref, crow_ref, cols_ref, wrow_ref, skip_ref, *rest):
    y_ref, state = rest[-2:]
    width = xc_ref.shape[1]
    groups = bt_ref.shape[0]
    gw = width // groups

    @pl.when(pl.program_id(0) == 0)
    def _():
        state[...] = rest[0][...] if len(rest) > 3 else jnp.zeros_like(state)

    left = lax.broadcasted_iota(jnp.int32, (BLK, LANES), 1) < HEAD_DIM
    row = lax.broadcasted_iota(jnp.int32, (BLK, BLK), 0)
    causal = row >= lax.broadcasted_iota(jnp.int32, (BLK, BLK), 1)
    for g in range(groups):
        b_g = bc_ref[:, g * STATE : (g + 1) * STATE]
        c_g = bc_ref[:, (groups + g) * STATE : (groups + g + 1) * STATE]
        scores = jnp.where(causal, dot_t(c_g, b_g), 0.0)
        b_t = bt_ref[g].astype(F32)
        for wide in range(g * gw, (g + 1) * gw, 2 * LANES):
            before = state[:, wide : wide + 2 * LANES]
            carry = dot(c_g, before.astype(BF16))
            for k in range(2):
                at = slice(wide + k * LANES, wide + (k + 1) * LANES)
                part = slice(k * LANES, (k + 1) * LANES)
                first = at.start // HEAD_DIM
                mixing, weighted, cums = [], [], []
                for h in (first, first + 1):
                    cum = jnp.broadcast_to(cols_ref[:, h : h + 1], (BLK, BLK))
                    gap = jnp.minimum(cum - crow_ref[h : h + 1], 0.0)
                    mixing.append((jnp.exp2(gap) * scores).astype(BF16))
                    weighted.append((b_t * wrow_ref[h : h + 1]).astype(BF16))
                    cums.append(cum)
                x = xc_ref[:, at]
                nil = jnp.zeros_like(x)
                stacked = jnp.concatenate([jnp.where(left, x, nil), jnp.where(left, nil, x)], 0)
                both = jnp.concatenate(
                    [jnp.concatenate(mixing, 1), jnp.concatenate(weighted, 1)], 0
                )
                result = dot(both, stacked)
                grown = jnp.exp2(jnp.where(left, cums[0], cums[1]))
                skip = jnp.where(left, skip_ref[0, first], skip_ref[0, first + 1])
                y = result[:BLK] + grown * carry[:, part] + skip * x.astype(F32)
                y_ref[:, at] = y.astype(BF16)
                state[:, at] = grown[BLK - 1 :] * before[:, part] + result[BLK:]


def prefix_kernel(pay_ref, e_ref, after_ref, out_ref):
    width = out_ref.shape[2]
    decays = dot(pay_ref[:, 0, width:], e_ref[...])
    running = jnp.zeros(out_ref.shape[1:], F32)
    for slab in range(out_ref.shape[0]):
        out_ref[slab] = running.astype(BF16)
        running = decays[slab : slab + 1] * running + pay_ref[slab, :, :width].astype(F32)


def norm_tile(
    y_ref, bc_ref, g_ref, enter_ref, gate_ref, gain_ref, e_ref, normed_ref, carry, grown, i
):
    width = y_ref.shape[1]
    groups = bc_ref.shape[1] // (2 * STATE)
    gw = width // groups
    grown[...] = dot(g_ref[...], e_ref[...])
    for g in range(groups):
        at = slice(g * gw, (g + 1) * gw)
        carry[:, at] = dot(bc_ref[:, (groups + g) * STATE : (groups + g + 1) * STATE], enter_ref[:, at])
    size = y_ref.shape[0]
    for r in range(0, size, ROWS):
        rows = slice(r, r + ROWS)
        out_rows = pl.ds(pl.multiple_of(i * size + r, ROWS), ROWS)
        for g in range(groups):
            at = slice(g * gw, (g + 1) * gw)
            y = y_ref[rows, at].astype(F32) + grown[rows, at] * carry[rows, at]
            gated = y * silu(gate_ref[rows, at].astype(F32))
            square_mean = jnp.mean(gated * gated, axis=-1, keepdims=True)
            scaled = gated * lax.rsqrt(square_mean + epsilon) * gain_ref[:, at]
            normed_ref[out_rows, at] = scaled.astype(BF16)


def direct_kernel(
    where_ref, y_ref, bc_ref, g_ref, enter_ref, gate_ref, gain_ref, e_ref, w_ref, after_ref,
    *rest, tiles, slots, chans,
):
    out_refs, (normed_ref, carry, grown, kept, sems) = rest[:-5], rest[-5:]
    i = pl.program_id(0)
    part = kept.shape[2]

    def fetch(k):
        dest = lax.rem(where_ref[0] + slots[k], chans)
        columns = pl.ds(pl.multiple_of(dest * part, part), part)
        return pltpu.make_async_copy(w_ref.at[:, columns], kept.at[k], sems.at[k])

    @pl.when(i == 0)
    def _():
        for k in range(len(slots)):
            fetch(k).start()

    @pl.when(i < tiles)
    def _():
        norm_tile(
            y_ref, bc_ref, g_ref, enter_ref, gate_ref, gain_ref, e_ref, normed_ref, carry, grown, i
        )

    for k, out_ref in enumerate(out_refs):
        @pl.when(i == tiles + k)
        def _(k=k, out_ref=out_ref):
            fetch(k).wait()
            out_ref[...] = dot(normed_ref[...], kept[k]).astype(BF16)


def ends_kernel(
    y_ref, bc_ref, g_ref, enter_ref, gate_ref, gain_ref, e_ref, w_ref, after_ref,
    shares_ref, up_ref, down_ref, normed_ref, carry, grown, *, tiles,
):
    i = pl.program_id(0)

    @pl.when(i < tiles)
    def _():
        norm_tile(
            y_ref, bc_ref, g_ref, enter_ref, gate_ref, gain_ref, e_ref, normed_ref, carry, grown, i
        )

    @pl.when(i >= tiles)
    def _():
        shares_ref[0] = dot(normed_ref[...], w_ref[...]).astype(BF16)

    @pl.when(i == tiles)
    def _():
        down_ref[...] = shares_ref[0]

    @pl.when(i == tiles + 1)
    def _():
        up_ref[...] = shares_ref[0]


def middle_kernel(normed_ref, w_ref, ends_ref, shares_ref):
    shares_ref[0] = dot(normed_ref[...], w_ref[...]).astype(BF16)


def onward_kernel(where_ref, up_own_ref, down_own_ref, up_ref, down_ref, *rest):
    up_out, down_out = rest[-2:]
    up_out[...] = (up_own_ref[0].astype(F32) + up_ref[...].astype(F32)).astype(BF16)
    down_out[...] = (down_own_ref[0].astype(F32) + down_ref[...].astype(F32)).astype(BF16)


def final_kernel(where_ref, own_ref, up_ref, down_ref, *rest):
    out_ref = rest[-1]
    total = own_ref[0].astype(F32) + up_ref[...].astype(F32) + down_ref[...].astype(F32)
    out_ref[...] = total.astype(BF16)


def arrived_kernel(*refs):
    refs[-1][...] = jnp.zeros_like(refs[-1])


def direct_final_kernel(where_ref, normed_ref, w_ref, *refs, count):
    out_ref = refs[-1]
    total = dot(normed_ref[...], w_ref[...])
    for ref in refs[:count]:
        total = total + ref[...].astype(F32)
    out_ref[...] = total.astype(BF16)


def in_hbm(x):
    return pltpu.with_memory_space_constraint(x, pltpu.HBM)


def brief():
    return pl.CostEstimate(flops=1, transcendentals=0, bytes_accessed=1)


def params(limit=VMEM_LIMIT):
    return pltpu.CompilerParams(dimension_semantics=("arbitrary",), vmem_limit_bytes=limit)


def whole(shape):
    return pl.BlockSpec(shape, lambda *b: (0,) * len(shape))


def unread():
    return pl.BlockSpec(memory_space=pl.ANY)


def shaped(shape, dtype=BF16):
    return pltpu.HBM(shape, dtype)


def local(
    inner_input, state_maps, gate_input, step_input, log_decay_rate, step_bias,
    skip_gain, conv_kernel, map_kernel, norm_gain, out_weight,
):
    tokens, width = inner_input.shape
    groups = state_maps.shape[2]
    parts = 2 * groups
    heads = step_input.shape[1]
    blocks = tokens // BLK
    slabs = lax.axis_size("seq")
    chans = lax.axis_size("chan")
    features = out_weight.shape[1]
    map_width = parts * STATE
    low = spread(heads, width)

    tail = jnp.concatenate(
        [inner_input[tokens - HALO :], state_maps[tokens - HALO :].reshape(HALO, map_width)], 1
    )
    tail = lax.ppermute(tail, "seq", [(i, i + 1) for i in range(slabs - 1)])

    def lanes_at(count):
        return pl.BlockSpec((count, WIDE), lambda c: (0, c))

    kept = [
        ((tokens, map_width), BF16),
        ((groups, STATE, tokens), BF16),
        ((heads, tokens), F32),
        ((tokens, LANES), F32),
        ((heads, tokens), F32),
        ((tokens, LANES), BF16),
    ]
    xc, pay, bc, bt, crow, cols, wrow, g_hl = pl.pallas_call(
        states_kernel,
        grid=(width // WIDE,),
        in_specs=[
            lanes_at(tokens),
            whole((tokens * parts, STATE)),
            whole((heads, tokens)),
            lanes_at(HALO),
            pl.BlockSpec((HALO, map_width), lambda c: (0, width // map_width)),
            whole((1, heads)),
            whole((1, heads)),
            lanes_at(4),
            whole((4 * parts, STATE)),
            lanes_at(LANES),
        ],
        out_specs=[lanes_at(tokens), whole((STATE, width + LANES))] + [unread()] * 6,
        out_shape=[shaped((tokens, width)), shaped((STATE, width + LANES))]
        + [shaped(*k) for k in kept],
        scratch_shapes=[pltpu.VMEM(*k) for k in kept]
        + [
            pltpu.VMEM((tokens, WIDE), BF16),
            pltpu.VMEM((tokens, LANES), BF16),
            pltpu.VMEM((tokens, WIDE), F32),
            pltpu.VMEM((HALO + tokens, LANES), F32),
            pltpu.VMEM((HALO + tokens, LANES), F32),
            pltpu.SemaphoreType.DMA((6,)),
        ],
        compiler_params=params(),
        name="states",
    )(
        in_hbm(inner_input), in_hbm(state_maps.reshape(tokens * parts, STATE)),
        in_hbm(step_input.T), tail, tail,
        in_hbm(step_bias.reshape(1, heads)), in_hbm(log_decay_rate.reshape(1, heads)),
        in_hbm(conv_kernel), in_hbm(map_kernel.reshape(4 * parts, STATE)), in_hbm(low),
    )

    part = STATE // slabs
    arrived = lax.all_to_all(
        pay.reshape(slabs, part, width + LANES), "seq", split_axis=0, concat_axis=0, tiled=True
    )

    def local_part(start, count, before, after):
        def tile(width):
            return pl.BlockSpec((BLK, width), lambda b: (start + b, 0))

        operands = [in_hbm(k) for k in (xc, bc, bt, crow, cols, wrow)]
        operands.append(skip_gain.reshape(1, heads))
        specs = [
            tile(width),
            tile(map_width),
            pl.BlockSpec((groups, STATE, BLK), lambda b: (0, 0, start + b)),
            pl.BlockSpec((heads, BLK), lambda b: (0, start + b)),
            tile(LANES),
            pl.BlockSpec((heads, BLK), lambda b: (0, start + b)),
            pl.BlockSpec(memory_space=pltpu.SMEM),
        ]
        aliases = {}
        if before is not None:
            y, state = before
            aliases = {len(operands) + 1: 0}
            operands += [in_hbm(state), in_hbm(y)]
            specs += [whole((STATE, width)), unread()]
        operands.append(in_hbm(after))
        specs.append(unread())
        return pl.pallas_call(
            local_kernel,
            grid=(count,),
            in_specs=specs,
            out_specs=[tile(width), whole((STATE, width))],
            out_shape=[shaped((tokens, width)), shaped((STATE, width), F32)],
            input_output_aliases=aliases,
            compiler_params=params(),
            cost_estimate=brief(),
            name="local_part",
        )(*operands)

    some = blocks * 3 // 8
    y_first = local_part(0, some, None, pay)
    entering = pl.pallas_call(
        prefix_kernel,
        out_shape=shaped((slabs, part, width)),
        in_specs=[
            pl.BlockSpec(memory_space=pltpu.VMEM),
            pl.BlockSpec(memory_space=pltpu.VMEM),
            unread(),
        ],
        out_specs=pl.BlockSpec(memory_space=pltpu.VMEM),
        compiler_params=pltpu.CompilerParams(vmem_limit_bytes=SMALL_LIMIT),
        name="prefix",
    )(arrived, low, in_hbm(y_first[0]))
    y_second = local_part(some, some, y_first, entering)
    entering = lax.all_to_all(entering, "seq", split_axis=0, concat_axis=0, tiled=True)
    entering = entering.reshape(STATE, width)

    part_out = features // chans
    norm_row = norm_gain.reshape(1, width)
    mine = lax.axis_index("chan").astype(jnp.int32)
    where = mine.reshape(1)

    def norm_operands(start, count, tokens_each, y):
        def tile(width):
            return pl.BlockSpec((tokens_each, width), lambda i, *_: (start + jnp.minimum(i, count - 1), 0))

        operands = [in_hbm(k) for k in (y, bc, g_hl)] + [entering]
        operands += [in_hbm(k) for k in (gate_input, norm_row, low)]
        specs = [
            tile(width),
            tile(map_width),
            tile(LANES),
            whole((STATE, width)),
            tile(width),
            whole((1, width)),
            whole((LANES, width)),
        ]
        return operands, specs

    def project_direct(start, count, tokens_each, y, after, slots):
        operands, specs = norm_operands(start, count, tokens_each, y)
        size = count * tokens_each

        return pl.pallas_call(
            functools.partial(direct_kernel, tiles=count, slots=slots, chans=chans),
            grid_spec=pltpu.PrefetchScalarGridSpec(
                num_scalar_prefetch=1,
                grid=(count + len(slots),),
                in_specs=specs + [unread(), unread()],
                out_specs=[whole((size, part_out))] * len(slots) + [whole((size, width))],
                scratch_shapes=[pltpu.VMEM((tokens_each, width), F32)] * 2
                + [
                    pltpu.VMEM((len(slots), width, part_out), BF16),
                    pltpu.SemaphoreType.DMA((len(slots),)),
                ],
            ),
            out_shape=[shaped((size, part_out))] * len(slots) + [shaped((size, width))],
            compiler_params=params(),
            name="project_direct",
        )(where, *operands, in_hbm(out_weight), in_hbm(after))

    def direct_final(start, normed, pieces, after):
        def tile(width, start=0):
            return pl.BlockSpec((BLK, width), lambda i, where: (start + i, 0))

        return pl.pallas_call(
            functools.partial(direct_final_kernel, count=len(pieces)),
            grid_spec=pltpu.PrefetchScalarGridSpec(
                num_scalar_prefetch=1,
                grid=(normed.shape[0] // BLK,),
                in_specs=[
                    tile(width),
                    pl.BlockSpec((width, part_out), lambda i, where: (0, where[0])),
                ]
                + [tile(part_out)] * len(pieces)
                + [unread()],
                out_specs=tile(part_out, start),
            ),
            out_shape=shaped((tokens, part_out)),
            compiler_params=params(SMALL_LIMIT),
            name="direct_final",
        )(where, in_hbm(normed), in_hbm(out_weight), *pieces, after)

    def project_ends(start, count, tokens_each, y, after):
        operands, specs = norm_operands(start, count, tokens_each, y)
        size = count * tokens_each

        def dest(i):
            return jnp.where(i <= count, 0, chans - 1)

        return pl.pallas_call(
            functools.partial(ends_kernel, tiles=count),
            grid=(count + 2,),
            in_specs=specs
            + [pl.BlockSpec((width, part_out), lambda i: (0, dest(i))), unread()],
            out_specs=[
                pl.BlockSpec((1, size, part_out), lambda i: (dest(i), 0, 0)),
                whole((size, part_out)),
                whole((size, part_out)),
                whole((size, width)),
            ],
            out_shape=[
                shaped((chans, size, part_out)),
                shaped((size, part_out)),
                shaped((size, part_out)),
                shaped((size, width)),
            ],
            scratch_shapes=[pltpu.VMEM((tokens_each, width), F32)] * 2,
            compiler_params=params(),
            cost_estimate=brief(),
            name="project_ends",
        )(*operands, in_hbm(out_weight), in_hbm(after))

    def project_middle(shares, normed):
        size = normed.shape[0]
        return pl.pallas_call(
            middle_kernel,
            grid=(chans - 2,),
            in_specs=[
                whole((size, width)),
                pl.BlockSpec((width, part_out), lambda i: (0, i + 1)),
                unread(),
            ],
            out_specs=pl.BlockSpec((1, size, part_out), lambda i: (i + 1, 0, 0)),
            out_shape=shaped((chans, size, part_out)),
            input_output_aliases={2: 0},
            compiler_params=params(),
            cost_estimate=brief(),
            name="project_middle",
        )(in_hbm(normed), in_hbm(out_weight), in_hbm(shares))

    def permuted(up, down, s):
        up = lax.ppermute(up, "chan", [(a, a + 1) for a in range(s + 1)])
        down = lax.ppermute(down, "chan", [(a, a - 1) for a in range(chans - 1 - s, chans)])
        return up, down

    def onward(shares, part, up, down, s, after):
        first, count = part
        tile = math.gcd(first, count) if first else count
        skipped = first // tile
        held = skipped if s == 1 else 0

        def plain(i, where):
            return (i, 0)

        def arrived(i, where):
            return (held + i, 0)

        def own(index):
            return pl.BlockSpec(
                (1, tile, part_out), lambda i, where: (index(where[0]), skipped + i, 0)
            )

        return pl.pallas_call(
            onward_kernel,
            grid_spec=pltpu.PrefetchScalarGridSpec(
                num_scalar_prefetch=1,
                grid=(count // tile,),
                in_specs=[
                    own(lambda me: jnp.minimum(chans - 1 - s + me, chans - 1)),
                    own(lambda me: jnp.maximum(me - (chans - 1) + s, 0)),
                    pl.BlockSpec((tile, part_out), arrived),
                    pl.BlockSpec((tile, part_out), arrived),
                ]
                + [unread()] * len(after),
                out_specs=[pl.BlockSpec((tile, part_out), plain)] * 2,
            ),
            out_shape=[jax.ShapeDtypeStruct((count, part_out), BF16)] * 2,
            compiler_params=params(SMALL_LIMIT),
            name="onward",
        )(where, in_hbm(shares), in_hbm(shares), up, down, *after)

    def final(start, shares, part, up, down, out):
        count, skipped = part[1] // BLK, part[0] // BLK

        def plain(i, where):
            return (i, 0)

        operands = [where, in_hbm(shares), up, down]
        in_specs = [
            pl.BlockSpec((1, BLK, part_out), lambda i, where: (where[0], skipped + i, 0)),
            pl.BlockSpec((BLK, part_out), plain),
            pl.BlockSpec((BLK, part_out), plain),
        ]
        aliases = {}
        if out is not None:
            aliases = {len(operands): 0}
            operands.append(in_hbm(out))
            in_specs.append(unread())
        return pl.pallas_call(
            final_kernel,
            grid_spec=pltpu.PrefetchScalarGridSpec(
                num_scalar_prefetch=1,
                grid=(count,),
                in_specs=in_specs,
                out_specs=pl.BlockSpec((BLK, part_out), lambda i, where: (start + skipped + i, 0)),
            ),
            out_shape=shaped((tokens, part_out)),
            input_output_aliases=aliases,
            compiler_params=params(SMALL_LIMIT),
            name="final",
        )(*operands)

    lead = blocks * 3 // 8
    order = sorted(range(1, chans), key=lambda k: (min(k, chans - k), k))
    *slots, normed = project_direct(0, 2, lead * BLK // 2, y_second[0], y_second[1], order)
    pieces = []
    for k, slot in zip(order, slots):
        turn = [(a, (a + k) % chans) for a in range(chans)]
        pieces.append(lax.ppermute(slot, "chan", turn))

    y_third = local_part(2 * some, blocks - 2 * some, y_second, normed)
    rest = blocks - lead
    some = (rest + 1) // 2 * BLK
    parts_of = [(0, some), (some, rest * BLK - some)]
    shares, up, down, line_normed = project_ends(lead, rest, BLK, y_third[0], normed)
    moving = [permuted(up, down, 0)] * 2
    shares = project_middle(shares, line_normed)
    mark = pl.pallas_call(
        arrived_kernel,
        in_specs=[unread()] * (len(pieces) + 1),
        out_specs=pl.BlockSpec(memory_space=pltpu.VMEM),
        out_shape=jax.ShapeDtypeStruct((HALO, LANES), F32),
        compiler_params=pltpu.CompilerParams(vmem_limit_bytes=SMALL_LIMIT),
        cost_estimate=pl.CostEstimate(flops=20000000000, transcendentals=0, bytes_accessed=1),
        name="arrived",
    )(*pieces, in_hbm(shares))
    after = [mark]
    for s in range(1, chans - 1):
        for k in range(2):
            up, down = onward(shares, parts_of[k], *moving[k], s, after)
            after = [up]
            moving[k] = permuted(up, down, s)
        if s == 1:
            out = direct_final(0, normed, pieces, up)
            after = [in_hbm(out)]
    for k in range(2):
        out = final(lead, shares, parts_of[k], *moving[k], out)
    return out


def solution(mesh):
    return jax.shard_map(
        local,
        mesh=mesh,
        in_specs=(
            P("seq", "chan"),
            P("seq", None, "chan", None),
            P("seq", "chan"),
            P("seq", "chan"),
            P("chan"),
            P("chan"),
            P("chan"),
            P(None, "chan"),
            P(None, None, "chan", None),
            P("chan"),
            P("chan", None),
        ),
        out_specs=P("seq", "chan"),
        check_vma=False,
    )
```

```python
import functools
import math

import jax
import jax.numpy as jnp
import numpy as np
from jax import lax
from jax.experimental import pallas as pl
from jax.experimental.pallas import tpu as pltpu
from jax.sharding import PartitionSpec as P

HEAD_DIM = 64
STATE = 128
BLK = 128
LANES = 128
HALO = 8
ROWS = 16
WIDE = 512

step_limit = 0.5
epsilon = 1e-05
LOG2E = 1.4426950408889634
F32 = jnp.float32
BF16 = jnp.bfloat16
VMEM_LIMIT = 40 * 1024 * 1024
SMALL_LIMIT = 10 * 1024 * 1024


def silu(v):
    return v * pl.reciprocal(1.0 + jnp.exp2(v * -LOG2E), approx=True)


def high_low(v):
    high = v.astype(BF16).astype(F32)
    return high, v - high


def spread(heads, width):
    result = np.zeros((LANES, width), np.float32)
    for k in range(2 * heads):
        h = k % heads
        result[k, h * HEAD_DIM : (h + 1) * HEAD_DIM] = 1.0
    return jnp.asarray(result, BF16)


def dot(a, b):
    return jnp.dot(a, b, preferred_element_type=F32)


def dot_t(a, b):
    return lax.dot_general(a, b, (((1,), (1,)), ((), ())), preferred_element_type=F32)


def column(row):
    count = row.shape[1]
    eye = lax.broadcasted_iota(jnp.int32, (count, count), 0) == lax.broadcasted_iota(
        jnp.int32, (count, count), 1
    )
    return jnp.sum(jnp.where(eye, row, 0.0), axis=1, keepdims=True)


def padded(pieces):
    rows = jnp.concatenate(pieces, 0)
    if rows.shape[0] == LANES:
        return rows
    return jnp.concatenate([rows, jnp.zeros((LANES - rows.shape[0], rows.shape[1]), rows.dtype)], 0)


def conv(before, cur, taps):
    full = jnp.concatenate([before, cur], 0)
    late = pltpu.roll(full, 1, 0)
    early = taps[1] * full + taps[0] * late
    acc = taps[3] * cur + taps[2] * late[HALO:] + pltpu.roll(early, 2, 0)[HALO:]
    return silu(acc)


def states_kernel(
    xa_ref, xb_ref, xc_in_ref, xd_ref, maps_ref, step_ref, tail_ref, mtail_ref, bias_ref, rate_ref, ck_ref, mk_ref, e_ref,
    xc_ref, pay_ref, *rest,
):
    outs, (bc_ref, bt_ref, crow_ref, cols_ref, wrow_ref, g_ref) = rest[:6], rest[6:12]
    weighted, w_ref, scale, plain, early, sems = rest[12:]
    copies = [
        pltpu.make_async_copy(kept, out, sems.at[k])
        for k, (kept, out) in enumerate(zip(rest[6:12], outs))
    ]
    c = pl.program_id(0)
    heads, tokens = step_ref.shape
    parts = mk_ref.shape[0] // 4
    groups = parts // 2
    blocks = tokens // BLK

    @pl.when(c == 0)
    def _():
        bias, rate = column(bias_ref[...]), -jnp.exp(column(rate_ref[...]))
        v = step_ref[...] + bias
        step = jnp.minimum(jnp.maximum(v, 0.0) + jnp.log1p(jnp.exp(-jnp.abs(v))), step_limit)
        log_step = rate * step
        first, rest = high_low(log_step)
        second, third = high_low(rest)
        pieces = []
        for b in range(blocks):
            at = slice(b * BLK, (b + 1) * BLK)
            pieces += [first[:, at], second[:, at], third[:, at]]
        row = lax.broadcasted_iota(jnp.int32, (BLK, BLK), 0)
        col = lax.broadcasted_iota(jnp.int32, (BLK, BLK), 1)
        tri = jnp.where(row <= col, 1.0, 0.0).astype(BF16)
        sums = dot(jnp.concatenate(pieces, 0).astype(BF16), tri)
        cums, leads = [], [jnp.zeros((heads, 1), F32)]
        for b in range(blocks):
            at = 3 * b * heads
            cum = (
                sums[at : at + heads]
                + sums[at + heads : at + 2 * heads]
                + sums[at + 2 * heads : at + 3 * heads]
            )
            cums.append(cum)
            leads.append(leads[-1] + cum[:, BLK - 1 : BLK])
        last = None
        for b in range(blocks):
            at = slice(b * BLK, (b + 1) * BLK)
            cum, step_b = cums[b], step[:, at]
            total = cum[:, BLK - 1 : BLK]
            wrow_ref[:, at] = jnp.exp(total - cum) * step_b
            slab_weight = jnp.exp(leads[blocks] - (leads[b] + cum)) * step_b
            entered = jnp.exp(cum + leads[b])
            crow_ref[:, at] = (cum - jnp.log(step_b)) * LOG2E
            w_ref[at, :] = padded(high_low(slab_weight)).T.astype(BF16)
            last = padded(high_low(entered)).T
            g_ref[at, :] = last.astype(BF16)
            cols_ref[at, :] = padded((cum * LOG2E,)).T
        pay_ref[:, heads * HEAD_DIM :] = jnp.broadcast_to(last[BLK - 1 :], (STATE, LANES)).astype(BF16)

        few = BLK // 2
        row = lax.broadcasted_iota(jnp.int32, (few * parts, few * parts), 0)
        col = lax.broadcasted_iota(jnp.int32, (few * parts, few * parts), 1)
        source = (row & (few - 1)) * parts + row // few
        pick = jnp.where(col == source, 1.0, 0.0).astype(BF16)
        before = [mtail_ref[:, q * STATE : (q + 1) * STATE].astype(F32) for q in range(parts)]
        for b in range(blocks):
            at = 2 * b * few * parts
            mixed = [maps_ref[at + k * few * parts : at + (k + 1) * few * parts] for k in range(2)]
            ordered = dot(pick, jnp.concatenate(mixed, 1))
            for q in range(parts):
                own = ordered[q * few : (q + 1) * few]
                cur = jnp.concatenate([own[:, :STATE], own[:, STATE:]], 0)
                taps = [mk_ref[k * parts + q : k * parts + q + 1] for k in range(4)]
                result = conv(before[q], cur, taps).astype(BF16)
                before[q] = cur[BLK - HALO :]
                bc_ref[b * BLK : (b + 1) * BLK, q * STATE : (q + 1) * STATE] = result
                if q < groups:
                    bt_ref[q, :, b * BLK : (b + 1) * BLK] = result.astype(F32).T.astype(BF16)

        for copy in copies:
            copy.start()

    scale[...] = dot(w_ref[...], e_ref[...])
    for lane in range(0, xa_ref.shape[1], LANES):
        at_lanes = slice(lane, lane + LANES)
        taps = [ck_ref[k : k + 1, at_lanes] for k in range(4)]
        tail = tail_ref[:, at_lanes].astype(F32)
        plain[:HALO] = tail
        early[:HALO] = taps[1] * tail + taps[0] * pltpu.roll(tail, 1, 0)
        quarter = tokens // 4
        for k, x_ref in enumerate((xa_ref, xb_ref, xc_in_ref, xd_ref)):
            first = HALO + k * quarter
            plain[first : first + quarter] = x_ref[:, at_lanes].astype(F32)
        for b in range(blocks):
            at = b * BLK
            late = plain[at + HALO - 1 : at + HALO - 1 + BLK]
            early[at + HALO : at + HALO + BLK] = (
                taps[1] * plain[at + HALO : at + HALO + BLK] + taps[0] * late
            )
            acc = (
                taps[3] * plain[at + HALO : at + HALO + BLK]
                + taps[2] * late
                + early[at + HALO - 2 : at + HALO - 2 + BLK]
            )
            result = silu(acc)
            xc_ref[at : at + BLK, at_lanes] = result.astype(BF16)
            scaled = result * scale[at : at + BLK, at_lanes]
            weighted[at : at + BLK, at_lanes] = scaled.astype(BF16)
    step_width = xa_ref.shape[1]
    group = c * step_width * groups // (heads * HEAD_DIM)
    at = pl.ds(pl.multiple_of(c * step_width, step_width), step_width)
    pay_ref[:, at] = dot(bt_ref[group], weighted[...]).astype(BF16)

    @pl.when(c == pl.num_programs(0) - 1)
    def _():
        for copy in copies:
            copy.wait()


def local_kernel(xc_ref, bc_ref, bt_ref, crow_ref, cols_ref, wrow_ref, skip_ref, *rest):
    y_ref, state = rest[-2:]
    width = xc_ref.shape[1]
    groups = bt_ref.shape[0]
    gw = width // groups

    @pl.when(pl.program_id(0) == 0)
    def _():
        state[...] = rest[0][...] if len(rest) > 3 else jnp.zeros_like(state)

    left = lax.broadcasted_iota(jnp.int32, (BLK, LANES), 1) < HEAD_DIM
    row = lax.broadcasted_iota(jnp.int32, (BLK, BLK), 0)
    causal = row >= lax.broadcasted_iota(jnp.int32, (BLK, BLK), 1)
    for g in range(groups):
        b_g = bc_ref[:, g * STATE : (g + 1) * STATE]
        c_g = bc_ref[:, (groups + g) * STATE : (groups + g + 1) * STATE]
        scores = jnp.where(causal, dot_t(c_g, b_g), 0.0)
        b_t = bt_ref[g].astype(F32)
        for wide in range(g * gw, (g + 1) * gw, 2 * LANES):
            before = state[:, wide : wide + 2 * LANES]
            carry = dot(c_g, before.astype(BF16))
            for k in range(2):
                at = slice(wide + k * LANES, wide + (k + 1) * LANES)
                part = slice(k * LANES, (k + 1) * LANES)
                first = at.start // HEAD_DIM
                mixing, weighted, cums = [], [], []
                for h in (first, first + 1):
                    cum = jnp.broadcast_to(cols_ref[:, h : h + 1], (BLK, BLK))
                    gap = jnp.minimum(cum - crow_ref[h : h + 1], 0.0)
                    mixing.append((jnp.exp2(gap) * scores).astype(BF16))
                    weighted.append((b_t * wrow_ref[h : h + 1]).astype(BF16))
                    cums.append(cum)
                x = xc_ref[:, at]
                nil = jnp.zeros_like(x)
                stacked = jnp.concatenate([jnp.where(left, x, nil), jnp.where(left, nil, x)], 0)
                both = jnp.concatenate(
                    [jnp.concatenate(mixing, 1), jnp.concatenate(weighted, 1)], 0
                )
                result = dot(both, stacked)
                grown = jnp.exp2(jnp.where(left, cums[0], cums[1]))
                skip = jnp.where(left, skip_ref[0, first], skip_ref[0, first + 1])
                y = result[:BLK] + grown * carry[:, part] + skip * x.astype(F32)
                y_ref[:, at] = y.astype(BF16)
                state[:, at] = grown[BLK - 1 :] * before[:, part] + result[BLK:]


def prefix_kernel(pay_ref, e_ref, after_ref, out_ref):
    width = out_ref.shape[2]
    decays = dot(pay_ref[:, 0, width:], e_ref[...])
    running = jnp.zeros(out_ref.shape[1:], F32)
    for slab in range(out_ref.shape[0]):
        out_ref[slab] = running.astype(BF16)
        running = decays[slab : slab + 1] * running + pay_ref[slab, :, :width].astype(F32)


def norm_tile(
    y_ref, bc_ref, g_ref, enter_ref, gate_ref, gain_ref, e_ref, normed_ref, carry, grown, i
):
    width = y_ref.shape[1]
    groups = bc_ref.shape[1] // (2 * STATE)
    gw = width // groups
    grown[...] = dot(g_ref[...], e_ref[...])
    for g in range(groups):
        at = slice(g * gw, (g + 1) * gw)
        carry[:, at] = dot(bc_ref[:, (groups + g) * STATE : (groups + g + 1) * STATE], enter_ref[:, at])
    size = y_ref.shape[0]
    for r in range(0, size, ROWS):
        rows = slice(r, r + ROWS)
        out_rows = pl.ds(pl.multiple_of(i * size + r, ROWS), ROWS)
        for g in range(groups):
            at = slice(g * gw, (g + 1) * gw)
            y = y_ref[rows, at].astype(F32) + grown[rows, at] * carry[rows, at]
            gated = y * silu(gate_ref[rows, at].astype(F32))
            square_mean = jnp.mean(gated * gated, axis=-1, keepdims=True)
            scaled = gated * lax.rsqrt(square_mean + epsilon) * gain_ref[:, at]
            normed_ref[out_rows, at] = scaled.astype(BF16)


def direct_kernel(
    where_ref, y_ref, bc_ref, g_ref, enter_ref, gate_ref, gain_ref, e_ref, w_ref, after_ref,
    *rest, tiles, slots, chans,
):
    out_refs, (normed_ref, carry, grown, kept, sems) = rest[:-5], rest[-5:]
    i = pl.program_id(0)
    part = kept.shape[2]

    def fetch(k):
        dest = lax.rem(where_ref[0] + slots[k], chans)
        columns = pl.ds(pl.multiple_of(dest * part, part), part)
        return pltpu.make_async_copy(w_ref.at[:, columns], kept.at[k], sems.at[k])

    @pl.when(i == 0)
    def _():
        for k in range(len(slots)):
            fetch(k).start()

    @pl.when(i < tiles)
    def _():
        norm_tile(
            y_ref, bc_ref, g_ref, enter_ref, gate_ref, gain_ref, e_ref, normed_ref, carry, grown, i
        )

    for k, out_ref in enumerate(out_refs):
        @pl.when(i == tiles + k)
        def _(k=k, out_ref=out_ref):
            fetch(k).wait()
            out_ref[...] = dot(normed_ref[...], kept[k]).astype(BF16)


def ends_kernel(
    y_ref, bc_ref, g_ref, enter_ref, gate_ref, gain_ref, e_ref, w_ref, after_ref,
    shares_ref, up_ref, down_ref, normed_ref, carry, grown, *, tiles,
):
    i = pl.program_id(0)

    @pl.when(i < tiles)
    def _():
        norm_tile(
            y_ref, bc_ref, g_ref, enter_ref, gate_ref, gain_ref, e_ref, normed_ref, carry, grown, i
        )

    @pl.when(i >= tiles)
    def _():
        shares_ref[0] = dot(normed_ref[...], w_ref[...]).astype(BF16)

    @pl.when(i == tiles)
    def _():
        down_ref[...] = shares_ref[0]

    @pl.when(i == tiles + 1)
    def _():
        up_ref[...] = shares_ref[0]


def middle_kernel(normed_ref, w_ref, ends_ref, shares_ref):
    shares_ref[0] = dot(normed_ref[...], w_ref[...]).astype(BF16)


def onward_kernel(where_ref, up_own_ref, down_own_ref, up_ref, down_ref, *rest):
    up_out, down_out = rest[-2:]
    up_out[...] = (up_own_ref[0].astype(F32) + up_ref[...].astype(F32)).astype(BF16)
    down_out[...] = (down_own_ref[0].astype(F32) + down_ref[...].astype(F32)).astype(BF16)


def final_kernel(where_ref, own_ref, up_ref, down_ref, *rest):
    out_ref = rest[-1]
    total = own_ref[0].astype(F32) + up_ref[...].astype(F32) + down_ref[...].astype(F32)
    out_ref[...] = total.astype(BF16)


def arrived_kernel(*refs):
    refs[-1][...] = jnp.zeros_like(refs[-1])


def direct_final_kernel(where_ref, normed_ref, w_ref, *refs, count):
    out_ref = refs[-1]
    total = dot(normed_ref[...], w_ref[...])
    for ref in refs[:count]:
        total = total + ref[...].astype(F32)
    out_ref[...] = total.astype(BF16)


def in_hbm(x):
    return pltpu.with_memory_space_constraint(x, pltpu.HBM)


def brief():
    return pl.CostEstimate(flops=1, transcendentals=0, bytes_accessed=1)


def params(limit=VMEM_LIMIT):
    return pltpu.CompilerParams(dimension_semantics=("arbitrary",), vmem_limit_bytes=limit)


def whole(shape):
    return pl.BlockSpec(shape, lambda *b: (0,) * len(shape))


def unread():
    return pl.BlockSpec(memory_space=pl.ANY)


def shaped(shape, dtype=BF16):
    return pltpu.HBM(shape, dtype)


def local(
    inner_input, state_maps, gate_input, step_input, log_decay_rate, step_bias,
    skip_gain, conv_kernel, map_kernel, norm_gain, out_weight,
):
    tokens, width = inner_input.shape
    groups = state_maps.shape[2]
    parts = 2 * groups
    heads = step_input.shape[1]
    blocks = tokens // BLK
    slabs = lax.axis_size("seq")
    chans = lax.axis_size("chan")
    features = out_weight.shape[1]
    map_width = parts * STATE
    low = spread(heads, width)

    tail = jnp.concatenate(
        [inner_input[tokens - HALO :], state_maps[tokens - HALO :].reshape(HALO, map_width)], 1
    )
    tail = lax.ppermute(tail, "seq", [(i, i + 1) for i in range(slabs - 1)])

    def lanes_at(count):
        return pl.BlockSpec((count, WIDE), lambda c: (0, c))

    kept = [
        ((tokens, map_width), BF16),
        ((groups, STATE, tokens), BF16),
        ((heads, tokens), F32),
        ((tokens, LANES), F32),
        ((heads, tokens), F32),
        ((tokens, LANES), BF16),
    ]
    xc, pay, bc, bt, crow, cols, wrow, g_hl = pl.pallas_call(
        states_kernel,
        grid=(width // WIDE,),
        in_specs=[pl.BlockSpec((tokens // 4, WIDE), lambda c, k=k: (k, c)) for k in range(4)]
        + [
            whole((tokens * parts, STATE)),
            whole((heads, tokens)),
            lanes_at(HALO),
            pl.BlockSpec((HALO, map_width), lambda c: (0, width // map_width)),
            whole((1, heads)),
            whole((1, heads)),
            lanes_at(4),
            whole((4 * parts, STATE)),
            lanes_at(LANES),
        ],
        out_specs=[lanes_at(tokens), whole((STATE, width + LANES))] + [unread()] * 6,
        out_shape=[shaped((tokens, width)), shaped((STATE, width + LANES))]
        + [shaped(*k) for k in kept],
        scratch_shapes=[pltpu.VMEM(*k) for k in kept]
        + [
            pltpu.VMEM((tokens, WIDE), BF16),
            pltpu.VMEM((tokens, LANES), BF16),
            pltpu.VMEM((tokens, WIDE), F32),
            pltpu.VMEM((HALO + tokens, LANES), F32),
            pltpu.VMEM((HALO + tokens, LANES), F32),
            pltpu.SemaphoreType.DMA((6,)),
        ],
        compiler_params=params(),
        name="states",
    )(
        *[in_hbm(inner_input)] * 4, in_hbm(state_maps.reshape(tokens * parts, STATE)),
        in_hbm(step_input.T), tail, tail,
        in_hbm(step_bias.reshape(1, heads)), in_hbm(log_decay_rate.reshape(1, heads)),
        in_hbm(conv_kernel), in_hbm(map_kernel.reshape(4 * parts, STATE)), in_hbm(low),
    )

    part = STATE // slabs
    arrived = lax.all_to_all(
        pay.reshape(slabs, part, width + LANES), "seq", split_axis=0, concat_axis=0, tiled=True
    )

    def local_part(start, count, before, after):
        def tile(width):
            return pl.BlockSpec((BLK, width), lambda b: (start + b, 0))

        operands = [in_hbm(k) for k in (xc, bc, bt, crow, cols, wrow)]
        operands.append(skip_gain.reshape(1, heads))
        specs = [
            tile(width),
            tile(map_width),
            pl.BlockSpec((groups, STATE, BLK), lambda b: (0, 0, start + b)),
            pl.BlockSpec((heads, BLK), lambda b: (0, start + b)),
            tile(LANES),
            pl.BlockSpec((heads, BLK), lambda b: (0, start + b)),
            pl.BlockSpec(memory_space=pltpu.SMEM),
        ]
        aliases = {}
        if before is not None:
            y, state = before
            aliases = {len(operands) + 1: 0}
            operands += [in_hbm(state), in_hbm(y)]
            specs += [whole((STATE, width)), unread()]
        operands.append(in_hbm(after))
        specs.append(unread())
        return pl.pallas_call(
            local_kernel,
            grid=(count,),
            in_specs=specs,
            out_specs=[tile(width), whole((STATE, width))],
            out_shape=[shaped((tokens, width)), shaped((STATE, width), F32)],
            input_output_aliases=aliases,
            compiler_params=params(),
            cost_estimate=brief(),
            name="local_part",
        )(*operands)

    some = blocks * 3 // 8
    y_first = local_part(0, some, None, pay)
    entering = pl.pallas_call(
        prefix_kernel,
        out_shape=shaped((slabs, part, width)),
        in_specs=[
            pl.BlockSpec(memory_space=pltpu.VMEM),
            pl.BlockSpec(memory_space=pltpu.VMEM),
            unread(),
        ],
        out_specs=pl.BlockSpec(memory_space=pltpu.VMEM),
        compiler_params=pltpu.CompilerParams(vmem_limit_bytes=SMALL_LIMIT),
        name="prefix",
    )(arrived, low, in_hbm(y_first[0]))
    y_second = local_part(some, some, y_first, entering)
    entering = lax.all_to_all(entering, "seq", split_axis=0, concat_axis=0, tiled=True)
    entering = entering.reshape(STATE, width)

    part_out = features // chans
    norm_row = norm_gain.reshape(1, width)
    mine = lax.axis_index("chan").astype(jnp.int32)
    where = mine.reshape(1)

    def norm_operands(start, count, tokens_each, y):
        def tile(width):
            return pl.BlockSpec((tokens_each, width), lambda i, *_: (start + jnp.minimum(i, count - 1), 0))

        operands = [in_hbm(k) for k in (y, bc, g_hl)] + [entering]
        operands += [in_hbm(k) for k in (gate_input, norm_row, low)]
        specs = [
            tile(width),
            tile(map_width),
            tile(LANES),
            whole((STATE, width)),
            tile(width),
            whole((1, width)),
            whole((LANES, width)),
        ]
        return operands, specs

    def project_direct(start, count, tokens_each, y, after, slots):
        operands, specs = norm_operands(start, count, tokens_each, y)
        size = count * tokens_each

        return pl.pallas_call(
            functools.partial(direct_kernel, tiles=count, slots=slots, chans=chans),
            grid_spec=pltpu.PrefetchScalarGridSpec(
                num_scalar_prefetch=1,
                grid=(count + len(slots),),
                in_specs=specs + [unread(), unread()],
                out_specs=[whole((size, part_out))] * len(slots) + [whole((size, width))],
                scratch_shapes=[pltpu.VMEM((tokens_each, width), F32)] * 2
                + [
                    pltpu.VMEM((len(slots), width, part_out), BF16),
                    pltpu.SemaphoreType.DMA((len(slots),)),
                ],
            ),
            out_shape=[shaped((size, part_out))] * len(slots) + [shaped((size, width))],
            compiler_params=params(),
            name="project_direct",
        )(where, *operands, in_hbm(out_weight), in_hbm(after))

    def direct_final(start, normed, pieces, after):
        def tile(width, start=0):
            return pl.BlockSpec((BLK, width), lambda i, where: (start + i, 0))

        return pl.pallas_call(
            functools.partial(direct_final_kernel, count=len(pieces)),
            grid_spec=pltpu.PrefetchScalarGridSpec(
                num_scalar_prefetch=1,
                grid=(normed.shape[0] // BLK,),
                in_specs=[
                    tile(width),
                    pl.BlockSpec((width, part_out), lambda i, where: (0, where[0])),
                ]
                + [tile(part_out)] * len(pieces)
                + [unread()],
                out_specs=tile(part_out, start),
            ),
            out_shape=shaped((tokens, part_out)),
            compiler_params=params(SMALL_LIMIT),
            name="direct_final",
        )(where, in_hbm(normed), in_hbm(out_weight), *pieces, after)

    def project_ends(start, count, tokens_each, y, after):
        operands, specs = norm_operands(start, count, tokens_each, y)
        size = count * tokens_each

        def dest(i):
            return jnp.where(i <= count, 0, chans - 1)

        return pl.pallas_call(
            functools.partial(ends_kernel, tiles=count),
            grid=(count + 2,),
            in_specs=specs
            + [pl.BlockSpec((width, part_out), lambda i: (0, dest(i))), unread()],
            out_specs=[
                pl.BlockSpec((1, size, part_out), lambda i: (dest(i), 0, 0)),
                whole((size, part_out)),
                whole((size, part_out)),
                whole((size, width)),
            ],
            out_shape=[
                shaped((chans, size, part_out)),
                shaped((size, part_out)),
                shaped((size, part_out)),
                shaped((size, width)),
            ],
            scratch_shapes=[pltpu.VMEM((tokens_each, width), F32)] * 2,
            compiler_params=params(),
            cost_estimate=brief(),
            name="project_ends",
        )(*operands, in_hbm(out_weight), in_hbm(after))

    def project_middle(shares, normed):
        size = normed.shape[0]
        return pl.pallas_call(
            middle_kernel,
            grid=(chans - 2,),
            in_specs=[
                whole((size, width)),
                pl.BlockSpec((width, part_out), lambda i: (0, i + 1)),
                unread(),
            ],
            out_specs=pl.BlockSpec((1, size, part_out), lambda i: (i + 1, 0, 0)),
            out_shape=shaped((chans, size, part_out)),
            input_output_aliases={2: 0},
            compiler_params=params(),
            cost_estimate=brief(),
            name="project_middle",
        )(in_hbm(normed), in_hbm(out_weight), in_hbm(shares))

    def permuted(up, down, s):
        up = lax.ppermute(up, "chan", [(a, a + 1) for a in range(s + 1)])
        down = lax.ppermute(down, "chan", [(a, a - 1) for a in range(chans - 1 - s, chans)])
        return up, down

    def onward(shares, part, up, down, s, after):
        first, count = part
        tile = math.gcd(first, count) if first else count
        skipped = first // tile
        held = skipped if s == 1 else 0

        def plain(i, where):
            return (i, 0)

        def arrived(i, where):
            return (held + i, 0)

        def own(index):
            return pl.BlockSpec(
                (1, tile, part_out), lambda i, where: (index(where[0]), skipped + i, 0)
            )

        return pl.pallas_call(
            onward_kernel,
            grid_spec=pltpu.PrefetchScalarGridSpec(
                num_scalar_prefetch=1,
                grid=(count // tile,),
                in_specs=[
                    own(lambda me: jnp.minimum(chans - 1 - s + me, chans - 1)),
                    own(lambda me: jnp.maximum(me - (chans - 1) + s, 0)),
                    pl.BlockSpec((tile, part_out), arrived),
                    pl.BlockSpec((tile, part_out), arrived),
                ]
                + [unread()] * len(after),
                out_specs=[pl.BlockSpec((tile, part_out), plain)] * 2,
            ),
            out_shape=[jax.ShapeDtypeStruct((count, part_out), BF16)] * 2,
            compiler_params=params(SMALL_LIMIT),
            name="onward",
        )(where, in_hbm(shares), in_hbm(shares), up, down, *after)

    def final(start, shares, part, up, down, out):
        count, skipped = part[1] // BLK, part[0] // BLK

        def plain(i, where):
            return (i, 0)

        operands = [where, in_hbm(shares), up, down]
        in_specs = [
            pl.BlockSpec((1, BLK, part_out), lambda i, where: (where[0], skipped + i, 0)),
            pl.BlockSpec((BLK, part_out), plain),
            pl.BlockSpec((BLK, part_out), plain),
        ]
        aliases = {}
        if out is not None:
            aliases = {len(operands): 0}
            operands.append(in_hbm(out))
            in_specs.append(unread())
        return pl.pallas_call(
            final_kernel,
            grid_spec=pltpu.PrefetchScalarGridSpec(
                num_scalar_prefetch=1,
                grid=(count,),
                in_specs=in_specs,
                out_specs=pl.BlockSpec((BLK, part_out), lambda i, where: (start + skipped + i, 0)),
            ),
            out_shape=shaped((tokens, part_out)),
            input_output_aliases=aliases,
            compiler_params=params(SMALL_LIMIT),
            name="final",
        )(*operands)

    lead = blocks * 3 // 8
    order = sorted(range(1, chans), key=lambda k: (min(k, chans - k), k))
    *slots, normed = project_direct(0, 2, lead * BLK // 2, y_second[0], y_second[1], order)
    pieces = []
    for k, slot in zip(order, slots):
        turn = [(a, (a + k) % chans) for a in range(chans)]
        pieces.append(lax.ppermute(slot, "chan", turn))

    y_third = local_part(2 * some, blocks - 2 * some, y_second, normed)
    rest = blocks - lead
    some = (rest + 1) // 2 * BLK
    parts_of = [(0, some), (some, rest * BLK - some)]
    shares, up, down, line_normed = project_ends(lead, rest, BLK, y_third[0], normed)
    moving = [permuted(up, down, 0)] * 2
    shares = project_middle(shares, line_normed)
    mark = pl.pallas_call(
        arrived_kernel,
        in_specs=[unread()] * (len(pieces) + 1),
        out_specs=pl.BlockSpec(memory_space=pltpu.VMEM),
        out_shape=jax.ShapeDtypeStruct((HALO, LANES), F32),
        compiler_params=pltpu.CompilerParams(vmem_limit_bytes=SMALL_LIMIT),
        cost_estimate=pl.CostEstimate(flops=20000000000, transcendentals=0, bytes_accessed=1),
        name="arrived",
    )(*pieces, in_hbm(shares))
    after = [mark]
    for s in range(1, chans - 1):
        for k in range(2):
            up, down = onward(shares, parts_of[k], *moving[k], s, after)
            after = [up]
            moving[k] = permuted(up, down, s)
        if s == 1:
            out = direct_final(0, normed, pieces, up)
            after = [in_hbm(out)]
    for k in range(2):
        out = final(lead, shares, parts_of[k], *moving[k], out)
    return out


def solution(mesh):
    return jax.shard_map(
        local,
        mesh=mesh,
        in_specs=(
            P("seq", "chan"),
            P("seq", None, "chan", None),
            P("seq", "chan"),
            P("seq", "chan"),
            P("chan"),
            P("chan"),
            P("chan"),
            P(None, "chan"),
            P(None, None, "chan", None),
            P("chan"),
            P("chan", None),
        ),
        out_specs=P("seq", "chan"),
        check_vma=False,
    )
```
